32 devices in a mesh: groups: 1, expert: 16 (over z, y, core), tensor: 2 (over x).
Axes of the slice: x: 2, y: 2, z: 4, core: 2. Of those that a mesh axis runs over, the one named last changes fastest.
Arguments:
- tokens: bfloat16 [2048, 4096], P(('groups', 'expert')), may hold values from -6 to 6
- expert_ids: int32 [2048, 8], P(('groups', 'expert')), may hold values from 0 to 15, all different within a row; in each aligned block of 128 rows (0 to 127, 128 to 255, ...) at most 96 rows name the same one
- route_weights: float32 [2048, 8], P(('groups', 'expert')), may hold values from 0.1 to 1
- gate_w: bfloat16 [16, 4096, 1536], P('expert', None, 'tensor'), may hold values from -0.09375 to 0.09375
- up_w: bfloat16 [16, 4096, 1536], P('expert', None, 'tensor'), may hold values from -0.09375 to 0.09375
- down_w: bfloat16 [16, 1536, 4096], P('expert', 'tensor'), may hold values from -0.15625 to 0.15625
Outputs:
- moe_out: bfloat16 [2048, 4096], P(('groups', 'expert'), 'tensor')
The draws below stay inside these ranges and needn't reach their ends.
Inputs may be any that keep to these rules, and one draw needn't show every extreme that they name: `expert_ids`: each row names 8 different experts. Among the rows of one device (aligned blocks of 128 rows) no expert is named more than 96 times, a bound that some block reaches.
All inputs are finite; a program needn't handle non-finite values.
Results may differ from the reference program's by a relative error of at most 0.014.
Values may be sent and summed in bfloat16 or wider, within the bound.
No kernel may reach another device: no remote copies, remote signals or barrier semaphores. Data moves between devices by JAX's collectives and lax.ppermute only.
A program may use at most 128 MiB of HBM per device.

```python
import math
import jax
import jax.numpy as jnp
import numpy as np
from jax import lax

D = 4096
FF = 1536
TOK_DEV = 128
EXPERTS = 16
TOP = 8
CAP = 96
TOKENS = 2048


def block_levels(rng, extent, pieces, least, high):
    loudness, own = 1.0, jax.random.fold_in(rng, 6)
    for dim, shards_of in pieces:
        steps = jnp.exp(jax.random.uniform(jax.random.fold_in(own, dim), (shards_of,), jnp.float32, least / len(pieces), high / len(pieces)))
        loudness = loudness * jnp.repeat(steps, extent[dim] // shards_of).reshape([-1 if axis == dim else 1 for axis in range(len(extent))])
    return loudness


def routed_block(stream_key, own, number, rows, number_of, top, reach, slope):
    order = jax.random.permutation(stream_key, number_of)
    crowded, common = portions_of(number_of, rows * top, reach, slope, True), portions_of(number_of, rows * top, reach, slope, False)
    places = jnp.arange(number_of)

    def named(tallies, turn):
        used = int((tallies > 0).sum())
        fixed = max(1, used // 4)
        passed = fixed + (places - fixed + turn * (used - fixed)) % max(1, number_of - fixed)
        return jnp.zeros((number_of,), jnp.int32).at[order[jnp.where(places < fixed, places, passed)]].set(jnp.asarray(tallies, jnp.int32))

    tallies = jnp.where(number % 4 == 0, named(crowded, number // 4), named(common, number - number // 4 - 1))
    mixed = jax.random.permutation(jax.random.fold_in(own, 3), number_of)
    donor, sink = mixed[0:number_of // 2 * 2:2], mixed[1:number_of // 2 * 2:2]
    margin = jnp.minimum(tallies[donor] - 1, reach - tallies[sink]) // 2
    margin = jnp.where((donor == order[0]) | (sink == order[0]) | (tallies[sink] == 0), 0, jnp.maximum(margin, 0))
    passed = jax.random.randint(jax.random.fold_in(own, 4), (number_of // 2,), 0, 1 << 20) % (margin + 1)
    tallies = tallies.at[donor].add(-passed).at[sink].add(passed)
    members = jnp.searchsorted(jnp.cumsum(tallies), jnp.arange(rows * top), side="right").astype(jnp.int32)
    listing = members.reshape(top, rows).T
    listing = listing[jax.random.permutation(jax.random.fold_in(own, 1), rows)]
    turn = jax.random.randint(jax.random.fold_in(own, 2), (rows, 1), 0, top)
    return jnp.take_along_axis(listing, (jnp.arange(top)[None, :] + turn) % top, axis=1)


def portions_of(number_of, total, bound, slope, full):
    weights = [(1 << 20) // math.isqrt(grade ** slope) + 1 for grade in range(1, number_of + 1)]
    largest = bound if full else min(bound, max(-(-total // number_of), total * weights[0] // sum(weights)))
    least = 1 if total - largest >= number_of - 1 else 0
    holding, rest = [largest] + [least] * (number_of - 1), total - largest - least * (number_of - 1)
    while rest > 0:
        movable = [i for i in range(1, number_of) if holding[i] < largest] or [i for i in range(1, number_of) if holding[i] < bound]
        pool, remaining = sum([weights[i] for i in movable]), rest
        for i in movable:
            more = min(bound - holding[i], max(1, remaining * weights[i] // pool), rest)
            holding[i] = holding[i] + more
            rest = rest - more
    return np.array(holding)


def normal_values(stream_key, shape, spread, most, shards=(), kind=jnp.bfloat16):
    values = spread * jax.random.normal(stream_key, shape, jnp.float32)
    if shards:
        values = values * block_levels(stream_key, shape, shards, -0.22, 0.18)
    return jnp.clip(values, -most, most).astype(kind)


def setup_inputs(seed: int = 0, part: int = 0) -> dict:
    splits = jax.random.split(jax.random.key(seed), 7)
    own_keys = jax.random.split(jax.random.fold_in(splits[6], part), 7)
    tokens = normal_values(own_keys[0], (TOKENS, D), 1.0, 6.0, ((0, 16),))
    expert_ids_keys = jax.random.split(jax.random.fold_in(own_keys[1], 1), TOKENS // TOK_DEV)
    expert_ids_turns = jax.random.permutation(jax.random.fold_in(own_keys[1], 3), TOKENS // TOK_DEV)
    expert_ids = jax.vmap(lambda own, number: routed_block(jax.random.fold_in(own_keys[1], 2), own, number, TOK_DEV, EXPERTS, TOP, CAP, 2))(expert_ids_keys, expert_ids_turns).reshape((TOKENS, TOP))
    route_weights = jnp.clip(0.1 + 0.9 * jax.random.uniform(own_keys[2], (TOKENS, TOP), jnp.float32) ** block_levels(own_keys[2], (TOKENS, TOP), ((0, 16),), -0.2, 0.2), 0.1, 1.0)
    gate_w = normal_values(splits[3], (EXPERTS, D, FF), D ** -0.5, 0.09375, ((0, 16), (2, 2)))
    up_w = normal_values(splits[4], (EXPERTS, D, FF), D ** -0.5, 0.09375, ((0, 16), (2, 2)))
    down_w = normal_values(splits[5], (EXPERTS, FF, D), FF ** -0.5, 0.15625, ((0, 16), (1, 2)))
    return dict(tokens=tokens, expert_ids=expert_ids, route_weights=route_weights, gate_w=gate_w, up_w=up_w, down_w=down_w)


def reference(tokens, expert_ids, route_weights, gate_w, up_w, down_w):
    total_rows = tokens.shape[0]
    blocks = total_rows // TOK_DEV
    grouped = expert_ids.reshape(blocks, TOK_DEV * TOP)
    onehot = (grouped[:, :, None] == jnp.arange(EXPERTS, dtype=jnp.int32)[None, None, :]).astype(jnp.int32)
    before = jnp.cumsum(onehot, axis=1) - onehot
    slot = jnp.sum(before * onehot, axis=2)
    block_index = jnp.arange(blocks, dtype=jnp.int32)[:, None]
    position = (block_index * CAP + slot).reshape(-1).astype(jnp.int32)
    flat_ids = expert_ids.reshape(-1)
    flat_weights = route_weights.reshape(-1)
    token_index = (jnp.arange(total_rows * TOP, dtype=jnp.int32) // TOP).astype(jnp.int32)
    quarter = FF // 4
    outside = blocks * CAP

    def step(accum, expert):
        chosen = flat_ids == expert
        target = jnp.where(chosen, position, outside).astype(jnp.int32)
        source = jnp.zeros((outside,), jnp.int32).at[target].set(token_index, mode="drop")
        filled = jnp.zeros((outside,), jnp.bool_).at[target].set(True, mode="drop")
        rows = jnp.where(filled[:, None], tokens[source], jnp.zeros((), tokens.dtype))
        gate = jnp.dot(rows, gate_w[expert], preferred_element_type=jnp.float32)
        up_part = jnp.dot(rows, up_w[expert], preferred_element_type=jnp.float32)
        hidden = (jax.nn.silu(gate) * up_part).astype(jnp.bfloat16)
        summed = jnp.zeros((outside, D), jnp.float32)
        for block in range(4):
            piece = jnp.dot(hidden[:, block * quarter:(block + 1) * quarter],
                            down_w[expert][block * quarter:(block + 1) * quarter],
                            preferred_element_type=jnp.float32).astype(jnp.bfloat16)
            piece = lax.optimization_barrier(piece)
            summed = summed + piece.astype(jnp.float32)
        expert_out = summed.astype(jnp.bfloat16)
        weight_pick = jnp.where(chosen, flat_weights, jnp.zeros((), flat_weights.dtype)).reshape(total_rows, TOP)
        where_rows = jnp.where(chosen, position, 0).astype(jnp.int32).reshape(total_rows, TOP)
        for choice_index in range(TOP):
            fetched = expert_out[where_rows[:, choice_index]].astype(jnp.float32)
            accum = accum + weight_pick[:, choice_index][:, None].astype(jnp.float32) * fetched
        return accum, None

    start = jnp.zeros((total_rows, D), jnp.float32)
    result, unused = lax.scan(step, start, jnp.arange(EXPERTS, dtype=jnp.int32))
    return result.astype(jnp.bfloat16)
```

```python
import jax
import jax.numpy as jnp
from jax import lax
from jax.sharding import PartitionSpec as P


def shards(tokens, expert_ids, route_weights, gate_w, up_w, down_w):
    local_experts = gate_w.shape[0]
    experts_all = local_experts * lax.axis_size("expert")
    chosen = expert_ids[:, :, None] == jnp.arange(experts_all, dtype=jnp.int32)
    table = jnp.sum(jnp.where(chosen, route_weights[:, :, None], 0.0), axis=1)
    table_all = lax.all_gather(table, "expert", axis=0, tiled=True)
    tokens_all = lax.all_gather(tokens, "expert", axis=0, tiled=True)
    first = lax.axis_index("expert") * local_experts
    total = None
    for e in range(local_experts):
        mine = lax.dynamic_slice_in_dim(table_all, first + e, 1, axis=1)
        gate = jnp.dot(tokens_all, gate_w[e], preferred_element_type=jnp.float32)
        up_part = jnp.dot(tokens_all, up_w[e], preferred_element_type=jnp.float32)
        hidden = (jax.nn.silu(gate) * up_part * mine).astype(jnp.bfloat16)
        part = jnp.dot(hidden, down_w[e], preferred_element_type=jnp.float32)
        total = part if total is None else total + part
    total = total.astype(jnp.bfloat16)
    total = lax.psum_scatter(total, "expert", scatter_dimension=0, tiled=True)
    return lax.psum_scatter(total, "tensor", scatter_dimension=1, tiled=True)


def solution(mesh):
    in_specs = (
        P(("groups", "expert"), None),
        P(("groups", "expert"), None),
        P(("groups", "expert"), None),
        P("expert", None, "tensor"),
        P("expert", None, "tensor"),
        P("expert", "tensor", None),
    )
    out_specs = P(("groups", "expert"), "tensor")
    return jax.shard_map(shards, mesh=mesh, in_specs=in_specs, out_specs=out_specs, check_vma=False)
```

```python
import jax
import jax.numpy as jnp
from jax import lax
from jax.sharding import PartitionSpec as P

CHUNKS = 4


def add(a, b):
    return (a.astype(jnp.float32) + b.astype(jnp.float32)).astype(jnp.bfloat16)


def line_reduce(slots, move):
    n = len(slots)
    slots = list(slots)
    if n == 1:
        return slots[0]
    if n == 2:
        return add(slots[0], move(slots[1], [(0, 1), (1, 0)]))
    for s in range(n - 1):
        right = move(slots[s + 1], [(i, i + 1) for i in range(s + 1)])
        left = move(slots[n - 1 - s], [(i, i - 1) for i in range(n - 1 - s, n)])
        slots[(s + 2) % n] = add(slots[(s + 2) % n], right)
        slots[n - 2 - s] = add(slots[n - 2 - s], left)
    return slots[0]


def make(mesh):
    experts, nx = mesh.shape["expert"], mesh.shape["tensor"]
    nc = 2 if experts % 2 == 0 else 1
    ny = 2 if experts // nc == 8 else 1
    nz = experts // (nc * ny)

    def index(z, y, c):
        return (z * ny + y) * nc + c

    def move_z(a, pairs):
        return lax.ppermute(a, "expert", [
            (index(s, y, c), index(t, y, c)) for s, t in pairs for y in range(ny) for c in range(nc)])

    def move_y(a, pairs):
        return lax.ppermute(a, "expert", [
            (index(z, s, c), index(z, t, c)) for s, t in pairs for z in range(nz) for c in range(nc)])

    def move_c(a, pairs):
        return lax.ppermute(a, "expert", [
            (index(z, y, s), index(z, y, t)) for s, t in pairs for z in range(nz) for y in range(ny)])

    def move_x(a, pairs):
        return lax.ppermute(a, "tensor", pairs)

    def shards(tokens, expert_ids, route_weights, gate_w, up_w, down_w):
        rows, width = tokens.shape
        local_experts = gate_w.shape[0]
        experts_all = local_experts * experts
        me = lax.axis_index("expert")
        z, y, c = me // (ny * nc), (me // nc) % ny, me % nc
        x = lax.axis_index("tensor")
        chosen = expert_ids[:, :, None] == jnp.arange(experts_all, dtype=jnp.int32)
        table = jnp.sum(jnp.where(chosen, route_weights[:, :, None], 0.0), axis=1)
        table_all = lax.all_gather(table, "expert", axis=0, tiled=True)
        tokens_all = lax.all_gather(tokens, "expert", axis=0, tiled=True)
        hidden = []
        for e in range(local_experts):
            mine = lax.dynamic_slice_in_dim(table_all, me * local_experts + e, 1, axis=1)
            gate = jnp.dot(tokens_all, gate_w[e], preferred_element_type=jnp.float32)
            up_part = jnp.dot(tokens_all, up_w[e], preferred_element_type=jnp.float32)
            hidden.append((jax.nn.silu(gate) * up_part * mine).astype(jnp.bfloat16))
        hidden = jnp.concatenate(hidden, axis=1) if local_experts > 1 else hidden[0]
        down = down_w.reshape(-1, width)
        depth = down.shape[0]
        order = [index((z - jz) % nz, (y - jy) % ny, (c - jc) % nc)
                 for jc in range(nc) for jy in range(ny) for jz in range(nz)]
        blocks = hidden.reshape(experts, rows, depth)
        blocks = jnp.take(blocks, jnp.stack(order), axis=0)
        blocks = blocks.reshape(nc, ny, nz * rows, depth)
        share = width // nx
        downs = [lax.dynamic_slice_in_dim(down, ((x - jx) % nx) * share, share, axis=1) for jx in range(nx)]
        part = share // CHUNKS

        def product(jc, jy, jx, k):
            return jnp.dot(blocks[jc, jy], downs[jx][:, k * part:(k + 1) * part],
                           preferred_element_type=jnp.float32)

        out = []
        for k in range(CHUNKS):
            held = {}
            for jy in reversed(range(ny)):
                for jx in reversed(range(nx)):
                    value = product(0, jy, jx, k)
                    if nc == 2:
                        other = move_c(product(1, jy, jx, k).astype(jnp.bfloat16), [(0, 1), (1, 0)])
                        value = value + other.astype(jnp.float32)
                    held[jy, jx] = value.astype(jnp.bfloat16)
            if k % 2 == 0:
                ys = [line_reduce([held[jy, jx] for jx in range(nx)], move_x) for jy in reversed(range(ny))][::-1]
                mine = line_reduce(ys, move_y)
            else:
                xs = [line_reduce([held[jy, jx] for jy in range(ny)], move_y) for jx in reversed(range(nx))][::-1]
                mine = line_reduce(xs, move_x)
            mine = mine.reshape(nz, rows, part)
            out.append(line_reduce([mine[jz] for jz in range(nz)], move_z))
        return jnp.concatenate(out, axis=1)

    return shards


def solution(mesh):
    in_specs = (
        P(("groups", "expert"), None),
        P(("groups", "expert"), None),
        P(("groups", "expert"), None),
        P("expert", None, "tensor"),
        P("expert", None, "tensor"),
        P("expert", "tensor", None),
    )
    out_specs = P(("groups", "expert"), "tensor")
    return jax.shard_map(make(mesh), mesh=mesh, in_specs=in_specs, out_specs=out_specs, check_vma=False)
```

```python
import jax
import jax.numpy as jnp
from jax import lax
from jax.sharding import PartitionSpec as P

CHUNKS = 4


def add(a, b):
    return (a.astype(jnp.float32) + b.astype(jnp.float32)).astype(jnp.bfloat16)


def offsets(n):
    out, d = [0], n // 2
    while d:
        out, d = out + [o ^ d for o in out], d // 2
    return out


def make(mesh):
    experts, nx = mesh.shape["expert"], mesh.shape["tensor"]
    nc = 2
    ny = 2 if experts // nc == 8 else 1
    nz = experts // (nc * ny)

    def index(z, y, c):
        return (z * ny + y) * nc + c

    places = [(z, y, c) for z in range(nz) for y in range(ny) for c in range(nc)]

    def move_z(a, d):
        return lax.ppermute(a, "expert", [(index(z, y, c), index(z ^ d, y, c)) for z, y, c in places])

    def move_y(a, d):
        return lax.ppermute(a, "expert", [(index(z, y, c), index(z, y ^ d, c)) for z, y, c in places])

    def move_c(a, d):
        return lax.ppermute(a, "expert", [(index(z, y, c), index(z, y, c ^ d)) for z, y, c in places])

    def move_x(a, d):
        return lax.ppermute(a, "tensor", [(i, i ^ d) for i in range(nx)])

    def halve_rows(a, n, move):
        d = 1
        while d < n:
            half = a.shape[0] // 2
            a = add(a[:half], move(a[half:], d))
            d *= 2
        return a

    def halve_columns(a, n, move, d=1):
        while d < n:
            half = a.shape[1] // 2
            a = add(a[:, :half], move(a[:, half:], d))
            d *= 2
        return a

    def shards(tokens, expert_ids, route_weights, gate_w, up_w, down_w):
        rows, width = tokens.shape
        local_experts = gate_w.shape[0]
        experts_all = local_experts * experts
        me = lax.axis_index("expert")
        x = lax.axis_index("tensor")
        chosen = expert_ids[None, :, :] == jnp.arange(experts_all, dtype=jnp.int32)[:, None, None]
        table = jnp.sum(jnp.where(chosen, route_weights[None], 0.0), axis=2)
        table_all = lax.all_gather(table, "expert", axis=0, tiled=True)
        table_all = table_all.reshape(experts, experts_all, rows)

        held = {(0, 0, 0): tokens}
        z_order = offsets(nz)
        d = nz // 2
        while d:
            for jz in [key[2] for key in list(held)]:
                held[0, 0, jz ^ d] = move_z(held[0, 0, jz], d)
            d //= 2
        if ny == 2:
            for jz in z_order:
                held[0, 1, jz] = move_y(held[0, 0, jz], 1)
        for jy in range(ny):
            for jz in z_order:
                held[1, jy, jz] = move_c(held[0, jy, jz], 1)

        blocks = {}
        for jz in z_order:
            for jy in range(ny):
                pair = jnp.concatenate([held[0, jy, jz], held[1, jy, jz]], axis=0)
                values = []
                for e in range(local_experts):
                    scale = []
                    for jc in range(nc):
                        place = me ^ index(jz, jy, jc)
                        scale.append(lax.dynamic_slice(
                            table_all, (place, me * local_experts + e, 0), (1, 1, rows)).reshape(rows))
                    scale = jnp.concatenate(scale)[:, None]
                    gate = jnp.dot(pair, gate_w[e], preferred_element_type=jnp.float32)
                    up_part = jnp.dot(pair, up_w[e], preferred_element_type=jnp.float32)
                    values.append((jax.nn.silu(gate) * up_part * scale).astype(jnp.bfloat16))
                value = jnp.concatenate(values, axis=1) if local_experts > 1 else values[0]
                blocks[0, jy, jz] = value[:rows]
                blocks[1, jy, jz] = value[rows:]
        hidden = {jc: jnp.concatenate([blocks[jc, jy, jz] for jy in range(ny) for jz in z_order], axis=0)
                  for jc in range(nc)}

        down = down_w.reshape(-1, width)
        share = width // nx
        part = share // CHUNKS
        downs = [lax.dynamic_slice_in_dim(down, (x ^ jx) * share, share, axis=1) for jx in offsets(nx)]

        def product(h, w):
            return jnp.dot(h, w, preferred_element_type=jnp.float32)

        def first_sums(k):
            w = jnp.concatenate([v[:, k * part:(k + 1) * part] for v in downs], axis=1)
            sums = []
            for far in (1, 0):
                if k % 2 == 0 or ny == 1:
                    half = w.shape[1] // 2
                    mine, other = [product(hidden[jc], w[:, far * half:(far + 1) * half]) for jc in (0, 1)]
                else:
                    half = hidden[0].shape[0] // 2
                    mine, other = [product(hidden[jc][far * half:(far + 1) * half], w) for jc in (0, 1)]
                got = move_c(other.astype(jnp.bfloat16), 1)
                sums.append((mine + got.astype(jnp.float32)).astype(jnp.bfloat16))
            return sums[1], sums[0]

        out = []
        for k in range(CHUNKS):
            near, far = first_sums(k)
            if k % 2 == 1 and k + 1 < CHUNKS:
                hidden[0], hidden[1], far = lax.optimization_barrier((hidden[0], hidden[1], far))
            if k % 2 == 0 or ny == 1:
                value = add(near, move_x(far, 1))
                value = halve_columns(value, nx, move_x, 2)
                value = halve_rows(value, ny, move_y)
            else:
                value = add(near, move_y(far, 1))
                value = halve_columns(value, nx, move_x)
            out.append(halve_rows(value, nz, move_z))
        return jnp.concatenate(out, axis=1)

    return shards


def solution(mesh):
    in_specs = (
        P(("groups", "expert"), None),
        P(("groups", "expert"), None),
        P(("groups", "expert"), None),
        P("expert", None, "tensor"),
        P("expert", None, "tensor"),
        P("expert", "tensor", None),
    )
    out_specs = P(("groups", "expert"), "tensor")
    return jax.shard_map(make(mesh), mesh=mesh, in_specs=in_specs, out_specs=out_specs, check_vma=False)
```

```python
import jax
import jax.numpy as jnp
from jax import lax
from jax.sharding import PartitionSpec as P

WIDTHS = (256, 256, 512, 512, 256, 256)
ALONE = 40


def add(a, b):
    return (a.astype(jnp.float32) + b.astype(jnp.float32)).astype(jnp.bfloat16)


def after(*values):
    return lax.optimization_barrier(values)


def offsets(n):
    out, d = [0], n // 2
    while d:
        out, d = out + [o ^ d for o in out], d // 2
    return out


def make(mesh):
    experts, nx = mesh.shape["expert"], mesh.shape["tensor"]
    nc = 2
    ny = 2 if experts // nc == 8 else 1
    nz = experts // (nc * ny)

    def index(z, y, c):
        return (z * ny + y) * nc + c

    places = [(z, y, c) for z in range(nz) for y in range(ny) for c in range(nc)]

    def move_z(a, d):
        return lax.ppermute(a, "expert", [(index(z, y, c), index(z ^ d, y, c)) for z, y, c in places])

    def move_y(a, d):
        return lax.ppermute(a, "expert", [(index(z, y, c), index(z, y ^ d, c)) for z, y, c in places])

    def move_c(a, d):
        return lax.ppermute(a, "expert", [(index(z, y, c), index(z, y, c ^ d)) for z, y, c in places])

    def move_x(a, d):
        return lax.ppermute(a, "tensor", [(i, i ^ d) for i in range(nx)])

    def halve_rows(a, n, move):
        d = 1
        while d < n:
            half = a.shape[0] // 2
            a = add(a[:half], move(a[half:], d))
            d *= 2
        return a

    def halve_columns(a, n, move, d=1):
        while d < n:
            half = a.shape[1] // 2
            a = add(a[:, :half], move(a[:, half:], d))
            d *= 2
        return a

    def shards(tokens, expert_ids, route_weights, gate_w, up_w, down_w):
        rows, width = tokens.shape
        local_experts = gate_w.shape[0]
        experts_all = local_experts * experts
        me = lax.axis_index("expert")
        x = lax.axis_index("tensor")
        chosen = expert_ids[None, :, :] == jnp.arange(experts_all, dtype=jnp.int32)[:, None, None]
        table = jnp.sum(jnp.where(chosen, route_weights[None], 0.0), axis=2)[None]
        tables = {(0, 0, 0): table}
        tables[1, 0, 0] = move_c(table, 1)
        table = jnp.concatenate([table, tables[1, 0, 0]], axis=0)
        names = [(0, 0, 0), (1, 0, 0)]

        def widen(table, names, move, d, axis):
            got = move(table, d)
            new = []
            for i, name in enumerate(names):
                name = tuple(v ^ d if k == axis else v for k, v in enumerate(name))
                tables[name] = got[i:i + 1]
                new.append(name)
            return jnp.concatenate([table, got], axis=0), names + new

        if ny == 2:
            table, names = widen(table, names, move_y, 1, 1)
        d = 1
        while d < nz:
            table, names = widen(table, names, move_z, d, 2)
            d *= 2
        z_order = offsets(nz)

        def expert_rows(jy, jz, near, far):
            far, near_table, far_table = after(far, tables[0, jy, jz], tables[1, jy, jz])
            pair = jnp.concatenate([near, far], axis=0)
            values = []
            for e in range(local_experts):
                scale = [lax.dynamic_slice_in_dim(v, me * local_experts + e, 1, axis=1)
                         for v in (near_table, far_table)]
                scale = jnp.concatenate([v.reshape(rows) for v in scale])[:, None]
                gate = jnp.dot(pair, gate_w[e], preferred_element_type=jnp.float32)
                up_part = jnp.dot(pair, up_w[e], preferred_element_type=jnp.float32)
                values.append((jax.nn.silu(gate) * up_part * scale).astype(jnp.bfloat16))
            value = jnp.concatenate(values, axis=1) if local_experts > 1 else values[0]
            blocks[0, jy, jz], blocks[1, jy, jz] = value[:rows], value[rows:]
            return value

        blocks = {}
        if (nx, ny, nz) == (2, 2, 4):
            alone = ALONE * rows // 128
            low = jnp.equal(x, 0)

            def whole(piece, other):
                mine, both = piece[:alone], piece[alone:]
                return jnp.concatenate([jnp.where(low, mine, other), both, jnp.where(low, other, mine)], axis=0)

            own = jnp.concatenate(
                [jnp.where(low, tokens[:alone], tokens[rows - alone:]), tokens[alone:rows - alone]], axis=0)
            z1, z2, y0 = move_z(own, 1), move_z(own, 2), move_y(own, 1)
            done = expert_rows(0, 0, tokens, move_c(tokens, 1))
            z1, y0 = after(z1, done)[0], after(y0, done)[0]
            y1 = move_y(z1, 1)
            b01 = whole(z1, move_x(z1[:alone], 1))
            b10 = whole(y0, move_x(y0[:alone], 1))
            c01, c10 = move_c(b01, 1), move_c(b10, 1)
            z2, y1 = after(z2, b01, b10)[0], after(y1, b01, b10)[0]
            z3, y2 = move_z(z2, 1), move_y(z2, 1)
            b02 = whole(z2, move_x(z2[:alone], 1))
            b11 = whole(y1, move_x(y1[:alone], 1))
            done01 = expert_rows(0, 1, b01, c01)
            done10 = expert_rows(1, 0, b10, c10)
            c02, c11 = move_c(b02, 1), move_c(b11, 1)
            z3, y2 = after(z3, done01, done10, b02)[0], after(y2, done01, done10, b02)[0]
            y3e, y3b = move_y(z3[:alone], 1), move_y(z3[alone:], 1)
            b03 = whole(z3, move_x(z3[:alone], 1))
            b12 = whole(y2, move_x(y2[:alone], 1))
            done02 = expert_rows(0, 2, b02, c02)
            expert_rows(1, 1, b11, c11)
            y3e = after(y3e, done02, b11)[0]
            b13 = whole(jnp.concatenate([y3e, y3b], axis=0), move_x(y3e, 1))
            c03, c12 = move_c(b03, 1), move_c(b12, 1)
            expert_rows(0, 3, b03, c03)
            expert_rows(1, 2, b12, c12)
            expert_rows(1, 3, b13, move_c(b13, 1))
        else:
            held = {(0, 0): tokens}
            d = nz // 2
            while d:
                for jz in sorted((key[1] for key in held), reverse=True):
                    held[0, jz ^ d] = move_z(held[0, jz], d)
                d //= 2
            for jz in z_order:
                for jy in range(ny):
                    if jy:
                        held[1, jz] = move_y(held[0, jz], 1)
                    expert_rows(jy, jz, held[jy, jz], move_c(held[jy, jz], 1))
        hidden = {jc: jnp.concatenate([blocks[jc, jy, jz] for jy in range(ny) for jz in z_order], axis=0)
                  for jc in range(nc)}

        down = down_w.reshape(-1, width)
        share = width // nx
        starts = [0]
        for w in WIDTHS:
            starts.append(starts[-1] + w * share // sum(WIDTHS))
        downs = [lax.dynamic_slice_in_dim(down, (x ^ jx) * share, share, axis=1) for jx in offsets(nx)]

        def product(h, w):
            return jnp.dot(h, w, preferred_element_type=jnp.float32)

        def first_sums(k):
            w = jnp.concatenate([v[:, starts[k]:starts[k + 1]] for v in downs], axis=1)
            sums = []
            for far in (1, 0):
                if k % 2 == 0 or ny == 1:
                    half = w.shape[1] // 2
                    mine, other = [product(hidden[jc], w[:, far * half:(far + 1) * half]) for jc in (0, 1)]
                else:
                    half = hidden[0].shape[0] // 2
                    mine, other = [product(hidden[jc][far * half:(far + 1) * half], w) for jc in (0, 1)]
                got = move_c(other.astype(jnp.bfloat16), 1)
                sums.append((mine + got.astype(jnp.float32)).astype(jnp.bfloat16))
            return sums[1], sums[0]

        out = []
        for k in range(len(WIDTHS)):
            near, far = first_sums(k)
            if k % 2 == 1 and k + 1 < len(WIDTHS):
                hidden[0], hidden[1], far = after(hidden[0], hidden[1], far)
            if k % 2 == 0 or ny == 1:
                value = add(near, move_x(far, 1))
                value = halve_columns(value, nx, move_x, 2)
                value = halve_rows(value, ny, move_y)
            else:
                value = add(near, move_y(far, 1))
                value = halve_columns(value, nx, move_x)
            out.append(halve_rows(value, nz, move_z))
        return jnp.concatenate(out, axis=1)

    return shards


def solution(mesh):
    in_specs = (
        P(("groups", "expert"), None),
        P(("groups", "expert"), None),
        P(("groups", "expert"), None),
        P("expert", None, "tensor"),
        P("expert", None, "tensor"),
        P("expert", "tensor", None),
    )
    out_specs = P(("groups", "expert"), "tensor")
    return jax.shard_map(make(mesh), mesh=mesh, in_specs=in_specs, out_specs=out_specs, check_vma=False)
```

```python
import jax
import jax.numpy as jnp
from jax import lax
from jax.sharding import PartitionSpec as P

WIDTHS = (384, 512, 128)
WINDOW = 5
LANES = 128


def after(*values):
    return lax.optimization_barrier(values)


def add(a, b):
    return (a.astype(jnp.float32) + b.astype(jnp.float32)).astype(jnp.bfloat16)


def offsets(n):
    out, d = [0], n // 2
    while d:
        out, d = out + [o ^ d for o in out], d // 2
    return out


def steps_of(n):
    return [1 << i for i in range(n.bit_length() - 1)]


class Queue:
    def __init__(self):
        self.sent, self.marks = [], []

    def mark(self, *values):
        self.marks += values

    def send(self, value, move, d=1):
        deps = list(self.marks)
        if len(self.sent) >= WINDOW:
            deps.append(self.sent[-WINDOW])
        if deps:
            value = after(value, *deps)[0]
        self.marks = []
        self.sent.append(move(value, d))
        return self.sent[-1]


def half(value, axis, which):
    dim = 1 if axis == "x" else 0
    size = value[0].shape[dim] // 2
    parts = [lax.slice_in_dim(v, which * size, (which + 1) * size, axis=dim) for v in value]
    return add(*parts) if len(parts) > 1 else parts[0]


def make(mesh):
    experts, nx = mesh.shape["expert"], mesh.shape["tensor"]
    nc = 2
    ny = 2 if experts // nc == 8 else 1
    nz = experts // (nc * ny)

    def index(z, y, c):
        return (z * ny + y) * nc + c

    places = [(z, y, c) for z in range(nz) for y in range(ny) for c in range(nc)]

    def move_z(a, d):
        return lax.ppermute(a, "expert", [(index(z, y, c), index(z ^ d, y, c)) for z, y, c in places])

    def move_y(a, d):
        return lax.ppermute(a, "expert", [(index(z, y, c), index(z, y ^ d, c)) for z, y, c in places])

    def move_c(a, d):
        return lax.ppermute(a, "expert", [(index(z, y, c), index(z, y, c ^ d)) for z, y, c in places])

    def move_x(a, d):
        return lax.ppermute(a, "tensor", [(i, i ^ d) for i in range(nx)])

    moves = {"x": move_x, "y": move_y, "z": move_z}

    def shards(tokens, expert_ids, route_weights, gate_w, up_w, down_w):
        rows, width = tokens.shape
        local_experts = gate_w.shape[0]
        experts_all = local_experts * experts
        me = lax.axis_index("expert")
        x = lax.axis_index("tensor")
        z_order = offsets(nz)
        assert 3 * experts_all <= LANES
        chosen = expert_ids[:, :, None] == jnp.arange(experts_all, dtype=jnp.int32)
        table = jnp.sum(jnp.where(chosen, route_weights[:, :, None], 0.0), axis=1)
        parts = []
        for _ in range(3):
            parts.append(lax.reduce_precision(table, 8, 7))
            table = table - parts[-1]
        parts.append(jnp.zeros((rows, LANES - 3 * experts_all), jnp.float32))
        table = jnp.concatenate(parts, axis=1).astype(jnp.bfloat16)
        wide = jnp.concatenate([tokens, table], axis=1)

        queue = Queue()
        blocks = {}

        def expert_rows(jy, jz, near, far):
            pair = jnp.concatenate([near[:, :width], far[:, :width]], axis=0)
            table = jnp.concatenate([near[:, width:], far[:, width:]], axis=0).astype(jnp.float32)
            lane = lax.broadcasted_iota(jnp.int32, table.shape, 1)
            values = []
            for e in range(local_experts):
                mine = (lane % experts_all == me * local_experts + e) & (lane < 3 * experts_all)
                scale = jnp.sum(jnp.where(mine, table, 0.0), axis=1, keepdims=True)
                gate = jnp.dot(pair, gate_w[e], preferred_element_type=jnp.float32)
                up_part = jnp.dot(pair, up_w[e], preferred_element_type=jnp.float32)
                values.append((jax.nn.silu(gate) * up_part * scale).astype(jnp.bfloat16))
            value = jnp.concatenate(values, axis=1) if local_experts > 1 else values[0]
            blocks[0, jy, jz], blocks[1, jy, jz] = value[:rows], value[rows:]
            return value

        if (nx, ny, nz) == (2, 2, 4):
            low = jnp.equal(x, 0)
            first, second = wide[:rows // 2], wide[rows // 2:]
            mine, rest = jnp.where(low, first, second), jnp.where(low, second, first)

            def whole(a, b):
                return jnp.concatenate([jnp.where(low, a, b), jnp.where(low, b, a)], axis=0)

            send = queue.send
            c00 = send(wide, move_c)
            z2m = send(mine, move_z, 2)
            y0m = send(mine, move_y)
            z1m = send(mine, move_z, 1)
            y0r = send(rest, move_y)
            queue.mark(expert_rows(0, 0, wide, c00))
            z1r = send(rest, move_z, 1)
            y1m = send(z1m, move_y)
            z3m = send(z2m, move_z, 1)
            y2m = send(z2m, move_y)
            b10 = whole(y0m, y0r)
            c10 = send(b10, move_c)
            z2r = send(rest, move_z, 2)
            queue.mark(expert_rows(1, 0, b10, c10))
            y1r = send(y1m, move_x)
            b01 = whole(z1m, z1r)
            c01 = send(b01, move_c)
            y3m = send(z3m, move_y)
            y2r = send(y2m, move_x)
            b11 = whole(y1m, y1r)
            c11 = send(b11, move_c)
            queue.mark(expert_rows(0, 1, b01, c01))
            z3r = send(z2r, move_z, 1)
            b02 = whole(z2m, z2r)
            c02 = send(b02, move_c)
            y3r = send(y3m, move_x)
            b12 = whole(y2m, y2r)
            c12 = send(b12, move_c)
            queue.mark(expert_rows(1, 1, b11, c11))
            b03 = whole(z3m, z3r)
            c03 = send(b03, move_c)
            b13 = whole(y3m, y3r)
            c13 = send(b13, move_c)
            expert_rows(0, 2, b02, c02)
            expert_rows(1, 2, b12, c12)
            expert_rows(0, 3, b03, c03)
            expert_rows(1, 3, b13, c13)
        else:
            held = {(0, 0): wide}
            for d in reversed(steps_of(nz)):
                for jz in sorted((key[1] for key in held), reverse=True):
                    held[0, jz ^ d] = move_z(held[0, jz], d)
            for jz in z_order:
                for jy in range(ny):
                    if jy:
                        held[1, jz] = move_y(held[0, jz], 1)
                    expert_rows(jy, jz, held[jy, jz], move_c(held[jy, jz], 1))
        hidden = [jnp.concatenate([blocks[jc, jy, jz] for jy in range(ny) for jz in z_order], axis=0)
                  for jc in range(nc)]

        down = down_w.reshape(-1, width)
        share = width // nx
        downs = [lax.dynamic_slice_in_dim(down, (x ^ jx) * share, share, axis=1) for jx in offsets(nx)]

        def product(h, w):
            return jnp.dot(h, w, preferred_element_type=jnp.float32)

        orders = [[("x", d) for d in steps_of(nx)] + [("y", d) for d in steps_of(ny)],
                  [("y", d) for d in steps_of(ny)] + [("x", d) for d in steps_of(nx)]]
        pairs = []
        start = 0
        for w in WIDTHS:
            w = w * share // (2 * sum(WIDTHS))
            pairs.append((start, start + w, start + 2 * w))
            start += 2 * w

        def core_sums(i, which):
            w = jnp.concatenate([v[:, pairs[i][which]:pairs[i][which + 1]] for v in downs], axis=1)
            columns = orders[which][0][0] == "x"
            cut = w.shape[1] // 2 if columns else hidden[0].shape[0] // 2

            def operands(jc, far):
                if columns:
                    return hidden[jc], w[:, far * cut:(far + 1) * cut]
                return hidden[jc][far * cut:(far + 1) * cut], w

            if i == 0:
                got = {far: queue.send(product(*operands(1, far)).astype(jnp.bfloat16), move_c) for far in (1, 0)}
            else:
                got = queue.send(product(hidden[1], w).astype(jnp.bfloat16), move_c)
                got = {far: half((got,), "x" if columns else "y", far) for far in (1, 0)}
            return [(product(*operands(0, far)) + got[far].astype(jnp.float32)).astype(jnp.bfloat16) for far in (0, 1)]

        state = {}

        def run(i, step):
            if step == 0:
                sums = [core_sums(i, which) for which in (0, 1)]
                for which in (0, 1):
                    state[i, which] = sums[which]
                return
            for which in (0, 1):
                if step - 1 < len(orders[which]):
                    axis, d = orders[which][step - 1]
                    if step == 1:
                        near, far = state[i, which]
                    else:
                        far = half(state[i, which], axis, 1)
                        near = half(state[i, which], axis, 0)
                    state[i, which] = (near, queue.send(far, moves[axis], d))
            k = step - 1 - len(orders[0])
            if k >= 0:
                if k == 0:
                    both = [(half(state[i, 0], "z", r), half(state[i, 1], "z", r)) for r in (0, 1)]
                    near, far = [jnp.concatenate(v, axis=1) for v in both]
                else:
                    near, far = [half(state[i], "z", r) for r in (0, 1)]
                state[i] = (near, queue.send(far, move_z, steps_of(nz)[k]))

        last = len(orders[0]) + len(steps_of(nz))
        if last == 4 and len(WIDTHS) == 3:
            plan = [(0, 0), (0, 1), (1, 0), (1, 1), (0, 2), (2, 0), (0, 3), (2, 1), (1, 2), (0, 4), (1, 3), (2, 2),
                    (1, 4), (2, 3), (2, 4)]
        else:
            plan = [(i, step) for i in range(len(WIDTHS)) for step in range(last + 1)]
        for i, step in plan:
            run(i, step)
            if (i, step) == (0, 0):
                hidden[0], hidden[1], _, _ = after(hidden[0], hidden[1], state[0, 0][1], state[0, 1][1])
        return jnp.concatenate([add(*state[i]) for i in range(len(WIDTHS))], axis=1)

    return shards


def solution(mesh):
    in_specs = (
        P(("groups", "expert"), None),
        P(("groups", "expert"), None),
        P(("groups", "expert"), None),
        P("expert", None, "tensor"),
        P("expert", None, "tensor"),
        P("expert", "tensor", None),
    )
    out_specs = P(("groups", "expert"), "tensor")
    return jax.shard_map(make(mesh), mesh=mesh, in_specs=in_specs, out_specs=out_specs, check_vma=False)
```

```python
import jax
import jax.numpy as jnp
from jax import lax
from jax.sharding import PartitionSpec as P

CHUNKS = 4
LANES = 128


def after(*values):
    return lax.optimization_barrier(values)


def add(a, b):
    return (a.astype(jnp.float32) + b.astype(jnp.float32)).astype(jnp.bfloat16)


def offsets(n):
    out, d = [0], n // 2
    while d:
        out, d = out + [o ^ d for o in out], d // 2
    return out


def steps_of(n):
    return [1 << i for i in range(n.bit_length() - 1)]


def make(mesh):
    experts, nx = mesh.shape["expert"], mesh.shape["tensor"]
    nc = 2
    ny = 2 if experts // nc == 8 else 1
    nz = experts // (nc * ny)

    def index(z, y, c):
        return (z * ny + y) * nc + c

    places = [(z, y, c) for z in range(nz) for y in range(ny) for c in range(nc)]

    def move_z(a, d):
        return lax.ppermute(a, "expert", [(index(z, y, c), index(z ^ d, y, c)) for z, y, c in places])

    def move_y(a, d):
        return lax.ppermute(a, "expert", [(index(z, y, c), index(z, y ^ d, c)) for z, y, c in places])

    def move_c(a, d):
        return lax.ppermute(a, "expert", [(index(z, y, c), index(z, y, c ^ d)) for z, y, c in places])

    def move_x(a, d):
        return lax.ppermute(a, "tensor", [(i, i ^ d) for i in range(nx)])

    def halve_rows(a, n, move):
        d = 1
        while d < n:
            half = a.shape[0] // 2
            a = add(a[:half], move(a[half:], d))
            d *= 2
        return a

    def halve_columns(a, n, move, d=1):
        while d < n:
            half = a.shape[1] // 2
            a = add(a[:, :half], move(a[:, half:], d))
            d *= 2
        return a

    def shards(tokens, expert_ids, route_weights, gate_w, up_w, down_w):
        rows, width = tokens.shape
        local_experts = gate_w.shape[0]
        experts_all = local_experts * experts
        me = lax.axis_index("expert")
        x = lax.axis_index("tensor")
        z_order = offsets(nz)
        assert 3 * experts_all <= LANES
        chosen = expert_ids[:, :, None] == jnp.arange(experts_all, dtype=jnp.int32)
        table = jnp.sum(jnp.where(chosen, route_weights[:, :, None], 0.0), axis=1)
        parts = []
        for _ in range(3):
            parts.append(lax.reduce_precision(table, 8, 7))
            table = table - parts[-1]
        parts.append(jnp.zeros((rows, LANES - 3 * experts_all), jnp.float32))
        table = jnp.concatenate(parts, axis=1).astype(jnp.bfloat16)
        wide = jnp.concatenate([tokens, table], axis=1)

        blocks = {}

        def expert_rows(jy, jz, near, far):
            pair = jnp.concatenate([near[:, :width], far[:, :width]], axis=0)
            table = jnp.concatenate([near[:, width:], far[:, width:]], axis=0).astype(jnp.float32)
            lane = lax.broadcasted_iota(jnp.int32, table.shape, 1)
            values = []
            for e in range(local_experts):
                mine = (lane % experts_all == me * local_experts + e) & (lane < 3 * experts_all)
                scale = jnp.sum(jnp.where(mine, table, 0.0), axis=1, keepdims=True)
                gate = jnp.dot(pair, gate_w[e], preferred_element_type=jnp.float32)
                up_part = jnp.dot(pair, up_w[e], preferred_element_type=jnp.float32)
                values.append((jax.nn.silu(gate) * up_part * scale).astype(jnp.bfloat16))
            value = jnp.concatenate(values, axis=1) if local_experts > 1 else values[0]
            blocks[0, jy, jz], blocks[1, jy, jz] = value[:rows], value[rows:]
            return value

        held = {(0, 0): wide}
        for d in reversed(steps_of(nz)):
            for jz in sorted((key[1] for key in held), reverse=True):
                held[0, jz ^ d] = move_z(held[0, jz], d)
        for jz in z_order:
            for jy in range(ny):
                if jy:
                    held[1, jz] = move_y(held[0, jz], 1)
                expert_rows(jy, jz, held[jy, jz], move_c(held[jy, jz], 1))
        hidden = [jnp.concatenate([blocks[jc, jy, jz] for jy in range(ny) for jz in z_order], axis=0)
                  for jc in range(nc)]

        down = down_w.reshape(-1, width)
        share = width // nx
        part = share // CHUNKS
        downs = [lax.dynamic_slice_in_dim(down, (x ^ jx) * share, share, axis=1) for jx in offsets(nx)]

        def product(h, w):
            return jnp.dot(h, w, preferred_element_type=jnp.float32)

        def first_sums(k):
            w = jnp.concatenate([v[:, k * part:(k + 1) * part] for v in downs], axis=1)
            sums = []
            for far in (1, 0):
                if k % 2 == 0 or ny == 1:
                    half = w.shape[1] // 2
                    mine, other = [product(hidden[jc], w[:, far * half:(far + 1) * half]) for jc in (0, 1)]
                else:
                    half = hidden[0].shape[0] // 2
                    mine, other = [product(hidden[jc][far * half:(far + 1) * half], w) for jc in (0, 1)]
                got = move_c(other.astype(jnp.bfloat16), 1)
                sums.append((mine + got.astype(jnp.float32)).astype(jnp.bfloat16))
            return sums[1], sums[0]

        out = []
        for k in range(CHUNKS):
            near, far = first_sums(k)
            if k % 2 == 1 and k + 1 < CHUNKS:
                hidden[0], hidden[1], far = lax.optimization_barrier((hidden[0], hidden[1], far))
            if k % 2 == 0 or ny == 1:
                value = add(near, move_x(far, 1))
                value = halve_columns(value, nx, move_x, 2)
                value = halve_rows(value, ny, move_y)
            else:
                value = add(near, move_y(far, 1))
                value = halve_columns(value, nx, move_x)
            out.append(halve_rows(value, nz, move_z))
        return jnp.concatenate(out, axis=1)

    return shards


def solution(mesh):
    in_specs = (
        P(("groups", "expert"), None),
        P(("groups", "expert"), None),
        P(("groups", "expert"), None),
        P("expert", None, "tensor"),
        P("expert", None, "tensor"),
        P("expert", "tensor", None),
    )
    out_specs = P(("groups", "expert"), "tensor")
    return jax.shard_map(make(mesh), mesh=mesh, in_specs=in_specs, out_specs=out_specs, check_vma=False)
```

```python
import functools

import jax
import jax.numpy as jnp
from jax import lax
from jax.experimental import pallas as pl
from jax.experimental.pallas import tpu as pltpu
from jax.sharding import PartitionSpec as P

WIDTHS = (512, 256, 256)
LANES = 128
VMEM = 40 * 1024 * 1024


def after(*values):
    return lax.optimization_barrier(values)


def add(a, b):
    return (a.astype(jnp.float32) + b.astype(jnp.float32)).astype(jnp.bfloat16)


def offsets(n):
    out, d = [0], n // 2
    while d:
        out, d = out + [o ^ d for o in out], d // 2
    return out


def steps_of(n):
    return [1 << i for i in range(n.bit_length() - 1)]


def half(value, axis, which, dep=None):
    dim = 1 if axis == "x" else 0
    size = value[0].shape[dim] // 2
    a, b = [lax.slice_in_dim(v, which * size, (which + 1) * size, axis=dim).astype(jnp.float32) for v in value]
    a = a + b
    if dep is not None:
        a = a + dep[:1, :1].astype(jnp.float32) * 0.0
    return a.astype(jnp.bfloat16)


def hidden_kernel(counts, all_experts, width, info, *refs):
    pieces, (gate_ref, up_ref, near_ref, far_ref, rows_ref, sems) = refs[:sum(counts)], refs[-6:]
    block = near_ref.shape[0]

    @pl.when(pl.program_id(0) == 0)
    def _():
        copies, at = [], 0
        for b, count in enumerate(counts):
            for i in range(count):
                size = block // count
                first = b * block + (i * size if count == 1 else pl.multiple_of((info[0] ^ i) * size, size))
                copies.append(pltpu.make_async_copy(
                    pieces[at], rows_ref.at[pl.ds(first, size)], sems.at[at]))
                at += 1
        for copy in copies:
            copy.start()
        for copy in copies:
            copy.wait()

    rows = rows_ref[:, :width]
    table = rows_ref[:, width:].astype(jnp.float32)
    lane = lax.broadcasted_iota(jnp.int32, table.shape, 1)
    mine = (lane == info[1]) | (lane == info[1] + all_experts) | (lane == info[1] + 2 * all_experts)
    scale = jnp.sum(jnp.where(mine, table, 0.0), axis=1, keepdims=True)
    gate = jnp.dot(rows, gate_ref[...], preferred_element_type=jnp.float32)
    up_part = jnp.dot(rows, up_ref[...], preferred_element_type=jnp.float32)
    value = (gate / (1.0 + jnp.exp(-gate)) * up_part * scale).astype(jnp.bfloat16)
    near_ref[...] = value[:block]
    far_ref[...] = value[block:]


def hidden_rows(near, far, gate_w, up_w, local, info, all_experts, deps):
    _, width, depth = gate_w.shape
    tile = 256 if depth % 256 == 0 else 128
    block = sum(v.shape[0] for v in near)
    counts = (len(near), len(far))
    weights = pl.BlockSpec((None, width, tile), lambda j, _: (local, 0, j))
    out = pl.BlockSpec((block, tile), lambda j, _: (0, j))
    return pl.pallas_call(
        functools.partial(hidden_kernel, counts, all_experts, width),
        grid_spec=pltpu.PrefetchScalarGridSpec(
            num_scalar_prefetch=1,
            grid=(depth // tile,),
            in_specs=[pl.BlockSpec(memory_space=pl.ANY)] * (sum(counts) + len(deps)) + [weights, weights],
            out_specs=[out, out],
            scratch_shapes=[
                pltpu.VMEM((2 * block, width + LANES), jnp.bfloat16),
                pltpu.SemaphoreType.DMA((sum(counts),)),
            ],
        ),
        out_shape=[jax.ShapeDtypeStruct((block, depth), jnp.bfloat16)] * 2,
        compiler_params=pltpu.CompilerParams(vmem_limit_bytes=VMEM),
        cost_estimate=pl.CostEstimate(
            flops=8 * block * width * depth, bytes_accessed=4 * width * depth, transcendentals=2 * block * depth),
        name="hidden_rows",
    )(info, *near, *far, *deps, gate_w, up_w)


def down_kernel(more, columns, rows_ref, down_ref, *refs):
    value = jnp.dot(rows_ref[...], down_ref[...], preferred_element_type=jnp.float32)
    if more:
        value = value + refs[0][...].astype(jnp.float32)
    refs[-1][...] = value.astype(jnp.bfloat16)


def down_rows(rows, part, parts, down, columns, tile, other, deps):
    size, depth = rows.shape[0] // parts, rows.shape[1]
    count = columns.shape[0]
    out = pl.BlockSpec((size, tile), lambda j, _: (0, j))
    args = [rows, down] + ([] if other is None else [other])
    return pl.pallas_call(
        functools.partial(down_kernel, other is not None),
        grid_spec=pltpu.PrefetchScalarGridSpec(
            num_scalar_prefetch=1,
            grid=(count,),
            in_specs=[
                pl.BlockSpec((size, depth), lambda j, _: (part, 0)),
                pl.BlockSpec((depth, tile), lambda j, columns: (0, columns[j])),
            ] + [out] * (len(args) - 2) + [pl.BlockSpec(memory_space=pl.ANY)] * len(deps),
            out_specs=out,
        ),
        out_shape=jax.ShapeDtypeStruct((size, count * tile), jnp.bfloat16),
        compiler_params=pltpu.CompilerParams(vmem_limit_bytes=VMEM),
        cost_estimate=pl.CostEstimate(
            flops=2 * size * depth * count * tile, bytes_accessed=2 * count * tile * (2 * size + depth), transcendentals=0),
        name="down_rows",
    )(columns, *args, *deps)


def make(mesh):
    experts, nx = mesh.shape["expert"], mesh.shape["tensor"]
    nc = 2
    ny = 2 if experts // nc == 8 else 1
    nz = experts // (nc * ny)

    def index(z, y, c):
        return (z * ny + y) * nc + c

    places = [(z, y, c) for z in range(nz) for y in range(ny) for c in range(nc)]

    def move_z(a, d):
        return lax.ppermute(a, "expert", [(index(z, y, c), index(z ^ d, y, c)) for z, y, c in places])

    def move_y(a, d):
        return lax.ppermute(a, "expert", [(index(z, y, c), index(z, y ^ d, c)) for z, y, c in places])

    def move_c(a, d):
        return lax.ppermute(a, "expert", [(index(z, y, c), index(z, y, c ^ d)) for z, y, c in places])

    def move_x(a, d):
        return lax.ppermute(a, "tensor", [(i, i ^ d) for i in range(nx)])

    moves = {"x": move_x, "y": move_y, "z": move_z}

    def shards(tokens, expert_ids, route_weights, gate_w, up_w, down_w):
        rows, width = tokens.shape
        local_experts = gate_w.shape[0]
        experts_all = local_experts * experts
        me = lax.axis_index("expert")
        x = lax.axis_index("tensor")
        z_order = offsets(nz)
        assert 3 * experts_all <= LANES
        chosen = expert_ids[:, :, None] == jnp.arange(experts_all, dtype=jnp.int32)
        table = jnp.sum(jnp.where(chosen, route_weights[:, :, None], 0.0), axis=1)
        parts = []
        for _ in range(3):
            parts.append(lax.reduce_precision(table, 8, 7))
            table = table - parts[-1]
        parts.append(jnp.zeros((rows, LANES - 3 * experts_all), jnp.float32))
        table = jnp.concatenate(parts, axis=1).astype(jnp.bfloat16)
        wide = jnp.concatenate([tokens, table], axis=1)

        blocks, ran = {}, []

        def expert_rows(jy, jz, near, far):
            for e in range(local_experts):
                info = jnp.stack([x, me * local_experts + e]).astype(jnp.int32)
                values = hidden_rows(near, far, gate_w, up_w, e, info, experts_all, ran[-1:])
                ran.append(values[0])
                for jc in range(nc):
                    blocks.setdefault((jc, jy, jz), []).append(values[jc])

        if (nx, ny, nz) == (2, 2, 4):
            low = jnp.equal(x, 0)
            first, second = wide[:rows // 2], wide[rows // 2:]
            m, r = jnp.where(low, first, second), jnp.where(low, second, first)
            z1m, z2m, y0, c00 = move_z(m, 1), move_z(m, 2), move_y(wide, 1), move_c(wide, 1)
            z1m, y0 = after(z1m, y0)
            y1m = move_y(z1m, 1)
            r, z1m = after(r, z1m)
            z1r = move_z(r, 1)
            z3m = move_z(z2m, 1)
            z2m, y1m = after(z2m, y1m)
            y2m, x1r = move_y(z2m, 1), move_x(y1m, 1)
            r, z3m = after(r, z3m)
            z2r = move_z(r, 2)
            z3r = move_z(z2r, 1)
            z3m, y2m = after(z3m, y2m)
            y3m = move_y(z3m, 1)
            y2m, x1r = after(y2m, x1r)
            x2r = move_x(y2m, 1)
            y3m, x2r = after(y3m, x2r)
            x3r = move_x(y3m, 1)
            expert_rows(0, 0, [wide], [c00])
            for jy, jz, near in ((1, 0, [y0]), (0, 1, [z1m, z1r]), (1, 1, [y1m, x1r]), (0, 2, [z2m, z2r]),
                                 (1, 2, [y2m, x2r]), (0, 3, [z3m, z3r]), (1, 3, [y3m, x3r])):
                expert_rows(jy, jz, near, [move_c(v, 1) for v in near])
        else:
            held = {(0, 0): wide}
            for d in reversed(steps_of(nz)):
                for jz in sorted((key[1] for key in held), reverse=True):
                    held[0, jz ^ d] = move_z(held[0, jz], d)
            for jz in z_order:
                for jy in range(ny):
                    if jy:
                        held[1, jz] = move_y(held[0, jz], 1)
                    expert_rows(jy, jz, [held[jy, jz]], [move_c(held[jy, jz], 1)])
        blocks = {key: jnp.concatenate(v, axis=1) if len(v) > 1 else v[0] for key, v in blocks.items()}
        hidden = [jnp.concatenate([blocks[jc, jy, jz] for jy in range(ny) for jz in z_order], axis=0)
                  for jc in range(nc)]

        down = down_w.reshape(-1, width)
        share = width // nx
        tile = share // 8
        x_order = offsets(nx)
        orders = [[("x", d) for d in steps_of(nx)] + [("y", d) for d in steps_of(ny)],
                  [("y", d) for d in steps_of(ny)] + [("x", d) for d in steps_of(nx)]]
        z_steps = steps_of(nz)
        bounds = [0]
        for w in WIDTHS:
            for _ in range(2):
                bounds.append(bounds[-1] + w * 8 // (2 * sum(WIDTHS)))
        state = {}

        def product(i, which, jc, far, other=None, deps=()):
            tiles = range(bounds[2 * i + which], bounds[2 * i + which + 1])
            by_columns = orders[which][0][0] == "x"
            slots = x_order
            if by_columns:
                slots = x_order[nx // 2:] if far else x_order[:nx // 2]
            columns = jnp.stack([(x ^ jx) * 8 + t for jx in slots for t in tiles]).astype(jnp.int32)
            part, parts = (0, 1) if by_columns else (far, 2)
            return down_rows(hidden[jc], part, parts, down, columns, tile, other, deps)

        def begin(i, deps):
            got = {(which, far): move_c(product(i, which, 1, far, deps=deps[which]), 1)
                   for far in (1, 0) for which in (0, 1)}
            for far in (1, 0):
                for which in (0, 1):
                    value = product(i, which, 0, far, got[which, far], deps[which])
                    state[i, which, far] = value
                    if far:
                        axis, d = orders[which][0]
                        state[i, which] = moves[axis](value, d)

        def turn(i, step, deps):
            for which in (0, 1):
                if step < len(orders[which]):
                    axis, d = orders[which][step]
                    value = (state[i, which, 0], state[i, which])
                    state[i, which] = moves[axis](half(value, axis, 1, deps[which]), d)
                    state[i, which, 0] = half(value, axis, 0)

        def turn_z(i, k, dep=None):
            if k == 0:
                values = [(state[i, which, 0], state[i, which]) for which in (0, 1)]
                near, far = [jnp.concatenate([half(v, "z", h, dep if h else None) for v in values], axis=1)
                             for h in (0, 1)]
            else:
                value = (state[i, "near"], state[i, "z"])
                if k == len(z_steps):
                    return add(*value)
                near, far = [half(value, "z", h, dep if h else None) for h in (0, 1)]
            state[i, "near"], state[i, "z"] = near, move_z(far, z_steps[k])
            return state[i, "z"]

        if (nx, ny, nz) == (2, 2, 4):
            begin(0, [(), ()])
            p0 = [state[0, 0], state[0, 1]]
            begin(1, [(state[0, 0, 1], state[0, 1, 1])] * 2)
            p1 = [state[1, 0], state[1, 1]]
            turn(0, 1, p0[::-1])
            q0 = [state[0, 0], state[0, 1]]
            begin(2, [(p1[0],), (p1[1],)])
            p2 = [state[2, 0], state[2, 1]]
            turn(1, 1, q0)
            turn(2, 1, p2[::-1])
            z0a = turn_z(0, 0)
            z0b = turn_z(0, 1)
            z1a = turn_z(1, 0, z0b)
            turn_z(1, 1)
            turn_z(2, 0, z1a)
            turn_z(2, 1)
        else:
            for i in range(len(WIDTHS)):
                begin(i, [(), ()])
                for step in range(1, len(orders[0])):
                    turn(i, step, [None, None])
                for k in range(len(z_steps)):
                    turn_z(i, k)
        out = [turn_z(i, len(z_steps)) for i in range(len(WIDTHS))]
        return jnp.concatenate(out, axis=1)

    return shards


def solution(mesh):
    in_specs = (
        P(("groups", "expert"), None),
        P(("groups", "expert"), None),
        P(("groups", "expert"), None),
        P("expert", None, "tensor"),
        P("expert", None, "tensor"),
        P("expert", "tensor", None),
    )
    out_specs = P(("groups", "expert"), "tensor")
    return jax.shard_map(make(mesh), mesh=mesh, in_specs=in_specs, out_specs=out_specs, check_vma=False)
```

```python
import functools

import jax
import jax.numpy as jnp
from jax import lax
from jax.experimental import pallas as pl
from jax.experimental.pallas import tpu as pltpu
from jax.sharding import PartitionSpec as P

WIDTHS = (512, 256, 256)
LANES = 128
VMEM = 56 * 1024 * 1024


def after(*values):
    return lax.optimization_barrier(values)


def add(a, b):
    return (a.astype(jnp.float32) + b.astype(jnp.float32)).astype(jnp.bfloat16)


def offsets(n):
    out, d = [0], n // 2
    while d:
        out, d = out + [o ^ d for o in out], d // 2
    return out


def steps_of(n):
    return [1 << i for i in range(n.bit_length() - 1)]


def half(value, axis, which):
    dim = 1 if axis == "x" else 0
    size = value[0].shape[dim] // 2
    return add(*[lax.slice_in_dim(v, which * size, (which + 1) * size, axis=dim) for v in value])


def hidden_kernel(counts, tile, all_experts, local, info, *refs):
    pieces = refs[:sum(counts)]
    gate_hbm, up_hbm = refs[sum(counts):sum(counts) + 2]
    rows_ref, gate_ref, up_ref, row_sems, weight_sems = refs[-5:]
    outs = refs[-5 - len(counts):-5]
    block, depth = outs[0].shape
    width = gate_ref.shape[0]
    copies, at = [], 0
    for b, count in enumerate(counts):
        for i in range(count):
            size = block // count
            first = b * block + (0 if count == 1 else pl.multiple_of((info[0] ^ i) * size, size))
            copies.append(pltpu.make_async_copy(pieces[at], rows_ref.at[pl.ds(first, size)], row_sems.at[at]))
            at += 1
    for copy in copies:
        copy.start()
    weights = []
    for t in range(depth // tile):
        part = pl.ds(t * tile, tile)
        weights.append([
            pltpu.make_async_copy(hbm.at[local, :, part], ref.at[:, part], weight_sems.at[k, t])
            for k, (hbm, ref) in enumerate(((gate_hbm, gate_ref), (up_hbm, up_ref)))])
        for copy in weights[-1]:
            copy.start()
    for copy in copies:
        copy.wait()
    table = rows_ref[:, width:].astype(jnp.float32)
    lane = lax.broadcasted_iota(jnp.int32, table.shape, 1)
    mine = (lane == info[1]) | (lane == info[1] + all_experts) | (lane == info[1] + 2 * all_experts)
    scale = jnp.sum(jnp.where(mine, table, 0.0), axis=1, keepdims=True)
    for t in range(depth // tile):
        part = pl.ds(t * tile, tile)
        weights[t][0].wait()
        gate = jnp.dot(rows_ref[:, :width], gate_ref[:, part], preferred_element_type=jnp.float32)
        weights[t][1].wait()
        up_part = jnp.dot(rows_ref[:, :width], up_ref[:, part], preferred_element_type=jnp.float32)
        value = (gate / (1.0 + jnp.exp(-gate)) * up_part * scale).astype(jnp.bfloat16)
        for b, out in enumerate(outs):
            out[:, part] = value[b * block:(b + 1) * block]


def hidden_rows(blocks, gate_w, up_w, local, info, all_experts, deps):
    _, width, depth = gate_w.shape
    tile = 256 if depth % 256 == 0 else 128
    block = sum(v.shape[0] for v in blocks[0])
    counts = tuple(len(v) for v in blocks)
    size = len(blocks) * block
    return pl.pallas_call(
        functools.partial(hidden_kernel, counts, tile, all_experts, local),
        in_specs=[pl.BlockSpec(memory_space=pltpu.SMEM)] + [pl.BlockSpec(memory_space=pl.ANY)] * (sum(counts) + 2 + len(deps)),
        out_specs=[pl.BlockSpec(memory_space=pltpu.VMEM)] * len(blocks),
        scratch_shapes=[
            pltpu.VMEM((size, width + LANES), jnp.bfloat16),
            pltpu.VMEM((width, depth), jnp.bfloat16),
            pltpu.VMEM((width, depth), jnp.bfloat16),
            pltpu.SemaphoreType.DMA((sum(counts),)),
            pltpu.SemaphoreType.DMA((2, depth // tile)),
        ],
        out_shape=[jax.ShapeDtypeStruct((block, depth), jnp.bfloat16)] * len(blocks),
        compiler_params=pltpu.CompilerParams(vmem_limit_bytes=VMEM),
        cost_estimate=pl.CostEstimate(
            flops=4 * size * width * depth, bytes_accessed=4 * width * depth, transcendentals=size * depth),
        name="hidden_rows",
    )(info, *[v for pieces in blocks for v in pieces], gate_w, up_w, *deps)


def make(mesh):
    experts, nx = mesh.shape["expert"], mesh.shape["tensor"]
    nc = 2
    ny = 2 if experts // nc == 8 else 1
    nz = experts // (nc * ny)

    def index(z, y, c):
        return (z * ny + y) * nc + c

    places = [(z, y, c) for z in range(nz) for y in range(ny) for c in range(nc)]

    def move_z(a, d):
        return lax.ppermute(a, "expert", [(index(z, y, c), index(z ^ d, y, c)) for z, y, c in places])

    def move_y(a, d):
        return lax.ppermute(a, "expert", [(index(z, y, c), index(z, y ^ d, c)) for z, y, c in places])

    def move_c(a, d):
        return lax.ppermute(a, "expert", [(index(z, y, c), index(z, y, c ^ d)) for z, y, c in places])

    def move_x(a, d):
        return lax.ppermute(a, "tensor", [(i, i ^ d) for i in range(nx)])

    moves = {"x": move_x, "y": move_y, "z": move_z}

    def shards(tokens, expert_ids, route_weights, gate_w, up_w, down_w):
        rows, width = tokens.shape
        local_experts = gate_w.shape[0]
        experts_all = local_experts * experts
        me = lax.axis_index("expert")
        x = lax.axis_index("tensor")
        z_order = offsets(nz)
        assert 3 * experts_all <= LANES
        chosen = expert_ids[:, :, None] == jnp.arange(experts_all, dtype=jnp.int32)
        table = jnp.sum(jnp.where(chosen, route_weights[:, :, None], 0.0), axis=1)
        parts = []
        for _ in range(3):
            parts.append(lax.reduce_precision(table, 8, 7))
            table = table - parts[-1]
        parts.append(jnp.zeros((rows, LANES - 3 * experts_all), jnp.float32))
        table = jnp.concatenate(parts, axis=1).astype(jnp.bfloat16)
        wide = jnp.concatenate([tokens, table], axis=1)

        blocks, ran = {}, []

        def expert_rows(*places):
            pieces = [v for place in places for v in place[2:]]
            for e in range(local_experts):
                info = jnp.stack([x, me * local_experts + e]).astype(jnp.int32)
                values = hidden_rows(pieces, gate_w, up_w, e, info, experts_all, ran[-1:])
                ran.append(values[0])
                for k, (jy, jz, _, _) in enumerate(places):
                    for jc in range(nc):
                        blocks.setdefault((jc, jy, jz), []).append(values[nc * k + jc])

        def paired(jy, jz, near):
            return jy, jz, near, [move_c(v, 1) for v in near]

        if (nx, ny, nz) == (2, 2, 4):
            low = jnp.equal(x, 0)
            first, second = wide[:rows // 2], wide[rows // 2:]
            m, r = jnp.where(low, first, second), jnp.where(low, second, first)
            z1m, z2m, y0 = move_z(m, 1), move_z(m, 2), move_y(wide, 1)
            own = paired(0, 0, [wide])
            z1m, y0 = after(z1m, y0)
            y1m = move_y(z1m, 1)
            z3m = move_z(z2m, 1)
            r, z1m = after(r, z1m)
            z1r = move_z(r, 1)
            z2m, r = after(z2m, r)
            z2r = move_z(r, 2)
            expert_rows(own, paired(1, 0, [y0]))
            z2m, y1m = after(z2m, y1m)
            y2m, x1r = move_y(z2m, 1), move_x(y1m, 1)
            z3r = move_z(z2r, 1)
            z3m, y2m = after(z3m, y2m)
            y3m = move_y(z3m, 1)
            y2m, x1r = after(y2m, x1r)
            x2r = move_x(y2m, 1)
            y3m, x2r = after(y3m, x2r)
            x3r = move_x(y3m, 1)
            expert_rows(paired(0, 1, [z1m, z1r]), paired(1, 1, [y1m, x1r]))
            expert_rows(paired(0, 2, [z2m, z2r]), paired(1, 2, [y2m, x2r]))
            expert_rows(paired(0, 3, [z3m, z3r]), paired(1, 3, [y3m, x3r]))
        else:
            held = {(0, 0): wide}
            for d in reversed(steps_of(nz)):
                for jz in sorted((key[1] for key in held), reverse=True):
                    held[0, jz ^ d] = move_z(held[0, jz], d)
            for jz in z_order:
                for jy in range(ny):
                    if jy:
                        held[1, jz] = move_y(held[0, jz], 1)
                    expert_rows(paired(jy, jz, [held[jy, jz]]))
        blocks = {key: jnp.concatenate(v, axis=1) if len(v) > 1 else v[0] for key, v in blocks.items()}
        hidden = [jnp.concatenate([blocks[jc, jy, jz] for jy in range(ny) for jz in z_order], axis=0)
                  for jc in range(nc)]

        down = down_w.reshape(-1, width)
        share = width // nx
        downs = [lax.dynamic_slice_in_dim(down, (x ^ jx) * share, share, axis=1) for jx in offsets(nx)]
        orders = [[("x", d) for d in steps_of(nx)] + [("y", d) for d in steps_of(ny)],
                  [("y", d) for d in steps_of(ny)] + [("x", d) for d in steps_of(nx)]]
        z_steps = steps_of(nz)
        bounds = [0]
        for w in WIDTHS:
            for _ in range(2):
                bounds.append(bounds[-1] + w * share // (2 * sum(WIDTHS)))
        state = {}

        def product(i, which, jc, far):
            w = jnp.concatenate([v[:, bounds[2 * i + which]:bounds[2 * i + which + 1]] for v in downs], axis=1)
            h = hidden[jc]
            if orders[which][0][0] == "x":
                cut = w.shape[1] // 2
                w = w[:, far * cut:(far + 1) * cut]
            else:
                cut = h.shape[0] // 2
                h = h[far * cut:(far + 1) * cut]
            return jnp.dot(h, w, preferred_element_type=jnp.float32)

        def tied(value, key):
            if key is not None:
                value, state[key] = after(value, state[key])
            return value

        def begin(i, keys=(None, None)):
            got = {(which, far): move_c(product(i, which, 1, far).astype(jnp.bfloat16), 1)
                   for far in (1, 0) for which in (0, 1)}
            for far in (1, 0):
                for which in (0, 1):
                    value = product(i, which, 0, far) + got[which, far].astype(jnp.float32)
                    state[i, which, far] = value.astype(jnp.bfloat16)
            if i + 1 < len(WIDTHS):
                hidden[0], hidden[1], state[i, 0, 1], state[i, 1, 1] = after(
                    hidden[0], hidden[1], state[i, 0, 1], state[i, 1, 1])
            for which in (0, 1):
                axis, d = orders[which][0]
                state[i, which] = moves[axis](tied(state[i, which, 1], keys[which]), d)

        def turn(i, step, keys=(None, None)):
            for which in (0, 1):
                if step < len(orders[which]):
                    axis, d = orders[which][step]
                    value = (state[i, which, 0], state[i, which])
                    far, state[i, which, 0] = half(value, axis, 1), half(value, axis, 0)
                    state[i, which] = moves[axis](tied(far, keys[which]), d)

        def turn_z(i, k, key=None):
            if k == 0:
                values = [(state[i, which, 0], state[i, which]) for which in (0, 1)]
                near, far = [jnp.concatenate([half(v, "z", h) for v in values], axis=1) for h in (0, 1)]
            else:
                value = (state[i, "near"], state[i, "z"])
                if k == len(z_steps):
                    return add(*value)
                near, far = [half(value, "z", h) for h in (0, 1)]
            state[i, "near"], state[i, "z"] = near, move_z(tied(far, key), z_steps[k])

        if (nx, ny, nz) == (2, 2, 4):
            begin(0)
            begin(1, ((0, 0), (0, 1)))
            turn(0, 1, ((1, 1), (1, 0)))
            begin(2, ((0, 1), (0, 0)))
            turn(1, 1, ((2, 1), (2, 0)))
            turn(2, 1, ((1, 0), (1, 1)))
            turn_z(0, 0)
            turn_z(0, 1)
            turn_z(1, 0, (0, "z"))
            turn_z(2, 0, (1, "z"))
            turn_z(1, 1)
            turn_z(2, 1)
        else:
            for i in range(len(WIDTHS)):
                begin(i)
                for step in range(1, len(orders[0])):
                    turn(i, step)
                for k in range(len(z_steps)):
                    turn_z(i, k)
        out = [turn_z(i, len(z_steps)) for i in range(len(WIDTHS))]
        return jnp.concatenate(out, axis=1)

    return shards


def solution(mesh):
    in_specs = (
        P(("groups", "expert"), None),
        P(("groups", "expert"), None),
        P(("groups", "expert"), None),
        P("expert", None, "tensor"),
        P("expert", None, "tensor"),
        P("expert", "tensor", None),
    )
    out_specs = P(("groups", "expert"), "tensor")
    return jax.shard_map(make(mesh), mesh=mesh, in_specs=in_specs, out_specs=out_specs, check_vma=False)
```

```python
import functools

import jax
import jax.numpy as jnp
from jax import lax
from jax.experimental import pallas as pl
from jax.experimental.pallas import tpu as pltpu
from jax.sharding import PartitionSpec as P

WIDTHS = (512, 384, 128)
LANES = 128
VMEM = 16 * 1024 * 1024


def after(*values):
    return lax.optimization_barrier(values)


def add(a, b):
    return (a.astype(jnp.float32) + b.astype(jnp.float32)).astype(jnp.bfloat16)


def offsets(n):
    out, d = [0], n // 2
    while d:
        out, d = out + [o ^ d for o in out], d // 2
    return out


def steps_of(n):
    return [1 << i for i in range(n.bit_length() - 1)]


def half(value, axis, which):
    dim = 1 if axis == "x" else 0
    size = value[0].shape[dim] // 2
    return add(*[lax.slice_in_dim(v, which * size, (which + 1) * size, axis=dim) for v in value])


def rows_kernel(counts, all_experts, width, info, *refs):
    pieces = refs[:sum(counts)]
    rows_ref, scale_ref, table_ref, sems = refs[-4:]
    block = rows_ref.shape[0] // len(counts)
    copies, at = [], 0
    for b, count in enumerate(counts):
        for i in range(count):
            size = block // count
            first = b * block + (0 if count == 1 else pl.multiple_of((info[0] ^ i) * size, size))
            copies.append(pltpu.make_async_copy(
                pieces[at].at[:, pl.ds(width, LANES)], table_ref.at[pl.ds(first, size)], sems.at[0, at]))
            copies.append(pltpu.make_async_copy(
                pieces[at].at[:, pl.ds(0, width)], rows_ref.at[pl.ds(first, size)], sems.at[1, at]))
            at += 1
    for copy in copies:
        copy.start()
    for copy in copies[::2]:
        copy.wait()
    table = table_ref[...].astype(jnp.float32)
    lane = lax.broadcasted_iota(jnp.int32, table.shape, 1)
    mine = (lane == info[1]) | (lane == info[1] + all_experts) | (lane == info[1] + 2 * all_experts)
    scale_ref[...] = jnp.sum(jnp.where(mine, table, 0.0), axis=1, keepdims=True)
    for copy in copies[1::2]:
        copy.wait()


def gather_rows(blocks, info, all_experts, deps):
    block = sum(v.shape[0] for v in blocks[0])
    width = blocks[0][0].shape[1] - LANES
    counts = tuple(len(v) for v in blocks)
    size = len(blocks) * block
    return pl.pallas_call(
        functools.partial(rows_kernel, counts, all_experts, width),
        in_specs=[pl.BlockSpec(memory_space=pltpu.SMEM)] + [pl.BlockSpec(memory_space=pl.ANY)] * (sum(counts) + len(deps)),
        out_specs=[pl.BlockSpec(memory_space=pl.ANY), pl.BlockSpec(memory_space=pltpu.VMEM)],
        scratch_shapes=[
            pltpu.VMEM((size, LANES), jnp.bfloat16),
            pltpu.SemaphoreType.DMA((2, sum(counts))),
        ],
        out_shape=[jax.ShapeDtypeStruct((size, width), jnp.bfloat16), jax.ShapeDtypeStruct((size, 1), jnp.float32)],
        compiler_params=pltpu.CompilerParams(vmem_limit_bytes=VMEM),
        cost_estimate=pl.CostEstimate(flops=0, bytes_accessed=4 * size * width, transcendentals=0),
        name="gather_rows",
    )(info, *[v for pieces in blocks for v in pieces], *deps)


def make(mesh):
    experts, nx = mesh.shape["expert"], mesh.shape["tensor"]
    nc = 2
    ny = 2 if experts // nc == 8 else 1
    nz = experts // (nc * ny)

    def index(z, y, c):
        return (z * ny + y) * nc + c

    places = [(z, y, c) for z in range(nz) for y in range(ny) for c in range(nc)]

    def move_z(a, d):
        return lax.ppermute(a, "expert", [(index(z, y, c), index(z ^ d, y, c)) for z, y, c in places])

    def move_y(a, d):
        return lax.ppermute(a, "expert", [(index(z, y, c), index(z, y ^ d, c)) for z, y, c in places])

    def move_c(a, d):
        return lax.ppermute(a, "expert", [(index(z, y, c), index(z, y, c ^ d)) for z, y, c in places])

    def move_x(a, d):
        return lax.ppermute(a, "tensor", [(i, i ^ d) for i in range(nx)])

    moves = {"x": move_x, "y": move_y, "z": move_z}

    def shards(tokens, expert_ids, route_weights, gate_w, up_w, down_w):
        rows, width = tokens.shape
        local_experts = gate_w.shape[0]
        experts_all = local_experts * experts
        me = lax.axis_index("expert")
        x = lax.axis_index("tensor")
        z_order = offsets(nz)
        assert 3 * experts_all <= LANES
        chosen = expert_ids[:, :, None] == jnp.arange(experts_all, dtype=jnp.int32)
        table = jnp.sum(jnp.where(chosen, route_weights[:, :, None], 0.0), axis=1)
        parts = []
        for _ in range(3):
            parts.append(lax.reduce_precision(table, 8, 7))
            table = table - parts[-1]
        parts.append(jnp.zeros((rows, LANES - 3 * experts_all), jnp.float32))
        table = jnp.concatenate(parts, axis=1).astype(jnp.bfloat16)
        wide = jnp.concatenate([tokens, table], axis=1)

        blocks, ran = {}, []

        def expert_rows(jy, jz, *pieces):
            values = []
            for e in range(local_experts):
                info = jnp.stack([x, me * local_experts + e]).astype(jnp.int32)
                pair, scale = gather_rows(pieces, info, experts_all, ran[-1:])
                gate = jnp.dot(pair, gate_w[e], preferred_element_type=jnp.float32)
                up_part = jnp.dot(pair, up_w[e], preferred_element_type=jnp.float32)
                values.append((jax.nn.silu(gate) * up_part * scale).astype(jnp.bfloat16))
                ran.append(values[-1])
            value = jnp.concatenate(values, axis=1) if local_experts > 1 else values[0]
            blocks[jy, jz] = value

        def ordered(value, got, *done):
            out = after(value, got, *[blocks[place] for place in done])
            for place, new in zip(done, out[2:]):
                blocks[place] = new
            return out[0], out[1]

        def paired(jy, jz, near):
            return jy, jz, near, [move_c(v, 1) for v in near]

        if (nx, ny, nz) == (2, 2, 4):
            low = jnp.equal(x, 0)
            first, second = wide[:rows // 2], wide[rows // 2:]
            m, r = jnp.where(low, first, second), jnp.where(low, second, first)
            z1m, z2m, y0 = move_z(m, 1), move_z(m, 2), move_y(wide, 1)
            own = paired(0, 0, [wide])
            expert_rows(*own)
            z1m, y0 = ordered(z1m, y0, (0, 0))
            y1m = move_y(z1m, 1)
            z3m = move_z(z2m, 1)
            r, z1m = after(r, z1m)
            z1r = move_z(r, 1)
            z2m, r = after(z2m, r)
            z2r = move_z(r, 2)
            expert_rows(*paired(1, 0, [y0]))
            z2m, y1m = after(z2m, y1m)
            y2m, x1r = move_y(z2m, 1), move_x(y1m, 1)
            z3r = move_z(z2r, 1)
            z3m, y2m = ordered(z3m, y2m, (1, 0))
            y3m = move_y(z3m, 1)
            y2m, x1r = after(y2m, x1r)
            x2r = move_x(y2m, 1)
            expert_rows(*paired(0, 1, [z1m, z1r]))
            y3m, x2r = ordered(y3m, x2r, (0, 1))
            x3r = move_x(y3m, 1)
            expert_rows(*paired(1, 1, [y1m, x1r]))
            expert_rows(*paired(0, 2, [z2m, z2r]))
            expert_rows(*paired(1, 2, [y2m, x2r]))
            expert_rows(*paired(0, 3, [z3m, z3r]))
            expert_rows(*paired(1, 3, [y3m, x3r]))
        else:
            held = {(0, 0): wide}
            for d in reversed(steps_of(nz)):
                for jz in sorted((key[1] for key in held), reverse=True):
                    held[0, jz ^ d] = move_z(held[0, jz], d)
            for jz in z_order:
                for jy in range(ny):
                    if jy:
                        held[1, jz] = move_y(held[0, jz], 1)
                    expert_rows(*paired(jy, jz, [held[jy, jz]]))
        hidden = [jnp.concatenate([blocks[jy, jz][jc * rows:(jc + 1) * rows] for jy in range(ny) for jz in z_order], axis=0)
                  for jc in range(nc)]

        down = down_w.reshape(-1, width)
        share = width // nx
        downs = [lax.dynamic_slice_in_dim(down, (x ^ jx) * share, share, axis=1) for jx in offsets(nx)]
        orders = [[("x", d) for d in steps_of(nx)] + [("y", d) for d in steps_of(ny)],
                  [("y", d) for d in steps_of(ny)] + [("x", d) for d in steps_of(nx)]]
        z_steps = steps_of(nz)
        bounds = [0]
        for w in WIDTHS:
            for _ in range(2):
                bounds.append(bounds[-1] + w * share // (2 * sum(WIDTHS)))
        state = {}

        def product(i, which, jc, far):
            w = jnp.concatenate([v[:, bounds[2 * i + which]:bounds[2 * i + which + 1]] for v in downs], axis=1)
            h = hidden[jc]
            if orders[which][0][0] == "x":
                cut = w.shape[1] // 2
                w = w[:, far * cut:(far + 1) * cut]
            else:
                cut = h.shape[0] // 2
                h = h[far * cut:(far + 1) * cut]
            return jnp.dot(h, w, preferred_element_type=jnp.float32)

        def tied(value, key):
            if key is not None:
                value, state[key] = after(value, state[key])
            return value

        def begin(i, keys=(None, None)):
            got = {(which, far): move_c(product(i, which, 1, far).astype(jnp.bfloat16), 1)
                   for far in (1, 0) for which in (0, 1)}
            for far in (1, 0):
                for which in (0, 1):
                    value = product(i, which, 0, far) + got[which, far].astype(jnp.float32)
                    state[i, which, far] = value.astype(jnp.bfloat16)
            if i + 1 < len(WIDTHS):
                hidden[0], hidden[1], state[i, 0, 1], state[i, 1, 1] = after(
                    hidden[0], hidden[1], state[i, 0, 1], state[i, 1, 1])
            for which in (0, 1):
                axis, d = orders[which][0]
                state[i, which] = moves[axis](tied(state[i, which, 1], keys[which]), d)

        def turn(i, step, keys=(None, None)):
            for which in (0, 1):
                if step < len(orders[which]):
                    axis, d = orders[which][step]
                    value = (state[i, which, 0], state[i, which])
                    far, state[i, which, 0] = half(value, axis, 1), half(value, axis, 0)
                    state[i, which] = moves[axis](tied(far, keys[which]), d)

        def turn_z(i, k, key=None):
            if k == 0:
                values = [(state[i, which, 0], state[i, which]) for which in (0, 1)]
                near, far = [jnp.concatenate([half(v, "z", h) for v in values], axis=1) for h in (0, 1)]
            else:
                value = (state[i, "near"], state[i, "z"])
                if k == len(z_steps):
                    return add(*value)
                near, far = [half(value, "z", h) for h in (0, 1)]
            state[i, "near"], state[i, "z"] = near, move_z(tied(far, key), z_steps[k])

        if (nx, ny, nz) == (2, 2, 4):
            begin(0)
            begin(1, ((0, 0), (0, 1)))
            turn(0, 1, ((1, 1), (1, 0)))
            turn(1, 1, ((0, 0), (0, 1)))
            begin(2, ((1, 1), (1, 0)))
            turn(2, 1, ((2, 1), (2, 0, 0)))
            turn_z(0, 0)
            turn_z(0, 1)
            turn_z(1, 0, (0, "z"))
            turn_z(2, 0, (1, "z"))
            turn_z(1, 1)
            turn_z(2, 1)
        else:
            for i in range(len(WIDTHS)):
                begin(i)
                for step in range(1, len(orders[0])):
                    turn(i, step)
                for k in range(len(z_steps)):
                    turn_z(i, k)
        out = [turn_z(i, len(z_steps)) for i in range(len(WIDTHS))]
        return jnp.concatenate(out, axis=1)

    return shards


def solution(mesh):
    in_specs = (
        P(("groups", "expert"), None),
        P(("groups", "expert"), None),
        P(("groups", "expert"), None),
        P("expert", None, "tensor"),
        P("expert", None, "tensor"),
        P("expert", "tensor", None),
    )
    out_specs = P(("groups", "expert"), "tensor")
    return jax.shard_map(make(mesh), mesh=mesh, in_specs=in_specs, out_specs=out_specs, check_vma=False)
```

```python
import functools

import jax
import jax.numpy as jnp
from jax import lax
from jax.experimental import pallas as pl
from jax.experimental.pallas import tpu as pltpu
from jax.sharding import PartitionSpec as P

WIDTHS = (512, 384, 128)
LANES = 128
VMEM = 2 * 1024 * 1024


def after(*values):
    return lax.optimization_barrier(values)


def add(a, b):
    return (a.astype(jnp.float32) + b.astype(jnp.float32)).astype(jnp.bfloat16)


def offsets(n):
    out, d = [0], n // 2
    while d:
        out, d = out + [o ^ d for o in out], d // 2
    return out


def steps_of(n):
    return [1 << i for i in range(n.bit_length() - 1)]


def pick(value, axis, which):
    dim = 1 if axis == "x" else 0
    size = value.shape[dim] // 2
    return lax.slice_in_dim(value, which * size, (which + 1) * size, axis=dim)


def half(value, axis, which):
    return add(*[pick(v, axis, which) for v in value])


def rows_kernel(counts, all_experts, width, info, *refs):
    pieces = refs[:sum(counts)]
    rows_ref, scale_ref, table_ref, sems = refs[-4:]
    block = rows_ref.shape[0] // len(counts)
    copies, at = [], 0
    for b, count in enumerate(counts):
        for i in range(count):
            size = block // count
            first = b * block + (0 if count == 1 else pl.multiple_of((info[0] ^ i) * size, size))
            copies.append(pltpu.make_async_copy(
                pieces[at].at[:, pl.ds(width, LANES)], table_ref.at[pl.ds(first, size)], sems.at[0, at]))
            copies.append(pltpu.make_async_copy(
                pieces[at].at[:, pl.ds(0, width)], rows_ref.at[pl.ds(first, size)], sems.at[1, at]))
            at += 1
    for copy in copies:
        copy.start()
    for copy in copies[::2]:
        copy.wait()
    table = table_ref[...].astype(jnp.float32)
    lane = lax.broadcasted_iota(jnp.int32, table.shape, 1)
    mine = (lane == info[1]) | (lane == info[1] + all_experts) | (lane == info[1] + 2 * all_experts)
    scale_ref[...] = jnp.sum(jnp.where(mine, table, 0.0), axis=1, keepdims=True)
    for copy in copies[1::2]:
        copy.wait()


def gather_rows(blocks, info, all_experts, deps):
    block = sum(v.shape[0] for v in blocks[0])
    width = blocks[0][0].shape[1] - LANES
    counts = tuple(len(v) for v in blocks)
    size = len(blocks) * block
    return pl.pallas_call(
        functools.partial(rows_kernel, counts, all_experts, width),
        in_specs=[pl.BlockSpec(memory_space=pltpu.SMEM)] + [pl.BlockSpec(memory_space=pl.ANY)] * (sum(counts) + len(deps)),
        out_specs=[pl.BlockSpec(memory_space=pl.ANY), pl.BlockSpec(memory_space=pltpu.VMEM)],
        scratch_shapes=[
            pltpu.VMEM((size, LANES), jnp.bfloat16),
            pltpu.SemaphoreType.DMA((2, sum(counts))),
        ],
        out_shape=[jax.ShapeDtypeStruct((size, width), jnp.bfloat16), jax.ShapeDtypeStruct((size, 1), jnp.float32)],
        compiler_params=pltpu.CompilerParams(vmem_limit_bytes=VMEM),
        cost_estimate=pl.CostEstimate(flops=4 * size * width * 1024, bytes_accessed=4 * size * width, transcendentals=0),
        name="gather_rows",
    )(info, *[v for pieces in blocks for v in pieces], *deps)


def make(mesh):
    experts, nx = mesh.shape["expert"], mesh.shape["tensor"]
    nc = 2
    ny = 2 if experts // nc == 8 else 1
    nz = experts // (nc * ny)

    def index(z, y, c):
        return (z * ny + y) * nc + c

    places = [(z, y, c) for z in range(nz) for y in range(ny) for c in range(nc)]

    def move_z(a, d):
        return lax.ppermute(a, "expert", [(index(z, y, c), index(z ^ d, y, c)) for z, y, c in places])

    def move_y(a, d):
        return lax.ppermute(a, "expert", [(index(z, y, c), index(z, y ^ d, c)) for z, y, c in places])

    def move_c(a, d):
        return lax.ppermute(a, "expert", [(index(z, y, c), index(z, y, c ^ d)) for z, y, c in places])

    def move_x(a, d):
        return lax.ppermute(a, "tensor", [(i, i ^ d) for i in range(nx)])

    moves = {"x": move_x, "y": move_y, "z": move_z}

    def shards(tokens, expert_ids, route_weights, gate_w, up_w, down_w):
        rows, width = tokens.shape
        local_experts = gate_w.shape[0]
        experts_all = local_experts * experts
        me = lax.axis_index("expert")
        x = lax.axis_index("tensor")
        z_order = offsets(nz)
        assert 3 * experts_all <= LANES
        chosen = expert_ids[:, :, None] == jnp.arange(experts_all, dtype=jnp.int32)
        table = jnp.sum(jnp.where(chosen, route_weights[:, :, None], 0.0), axis=1)
        parts = []
        for _ in range(3):
            parts.append(lax.reduce_precision(table, 8, 7))
            table = table - parts[-1]
        parts.append(jnp.zeros((rows, LANES - 3 * experts_all), jnp.float32))
        table = jnp.concatenate(parts, axis=1).astype(jnp.bfloat16)
        wide = jnp.concatenate([tokens, table], axis=1)

        blocks, ran = {}, []

        def expert_rows(jy, jz, *pieces):
            values = []
            for e in range(local_experts):
                info = jnp.stack([x, me * local_experts + e]).astype(jnp.int32)
                pair, scale = gather_rows(pieces, info, experts_all, ran[-1:])
                gate = jnp.dot(pair, gate_w[e], preferred_element_type=jnp.float32)
                up_part = jnp.dot(pair, up_w[e], preferred_element_type=jnp.float32)
                values.append((jax.nn.silu(gate) * up_part * scale).astype(jnp.bfloat16))
                ran.append(values[-1])
            value = jnp.concatenate(values, axis=1) if local_experts > 1 else values[0]
            blocks[jy, jz] = value

        def paired(jy, jz, near):
            return jy, jz, near, [move_c(v, 1) for v in near]

        if (nx, ny, nz) == (2, 2, 4):
            low = jnp.equal(x, 0)
            first, second = wide[:rows // 2], wide[rows // 2:]
            m, r = jnp.where(low, first, second), jnp.where(low, second, first)
            z1m, z2m, y0 = move_z(m, 1), move_z(m, 2), move_y(wide, 1)
            own = paired(0, 0, [wide])
            expert_rows(*own)
            z1m, y0, z2m = after(z1m, y0, z2m)
            y1m = move_y(z1m, 1)
            z3m = move_z(z2m, 1)
            r, z1m = after(r, z1m)
            z1r = move_z(r, 1)
            z2m, r = after(z2m, r)
            z2r = move_z(r, 2)
            expert_rows(*paired(1, 0, [y0]))
            z2m, y1m = after(z2m, y1m)
            y2m, x1r = move_y(z2m, 1), move_x(y1m, 1)
            z3r = move_z(z2r, 1)
            z3m, y2m = after(z3m, y2m)
            y3m = move_y(z3m, 1)
            y2m, x1r = after(y2m, x1r)
            x2r = move_x(y2m, 1)
            expert_rows(*paired(0, 1, [z1m, z1r]))
            y3m, x2r = after(y3m, x2r)
            x3r = move_x(y3m, 1)
            expert_rows(*paired(1, 1, [y1m, x1r]))
            expert_rows(*paired(0, 2, [z2m, z2r]))
            expert_rows(*paired(1, 2, [y2m, x2r]))
            expert_rows(*paired(0, 3, [z3m, z3r]))
            expert_rows(*paired(1, 3, [y3m, x3r]))
        else:
            held = {(0, 0): wide}
            for d in reversed(steps_of(nz)):
                for jz in sorted((key[1] for key in held), reverse=True):
                    held[0, jz ^ d] = move_z(held[0, jz], d)
            for jz in z_order:
                for jy in range(ny):
                    if jy:
                        held[1, jz] = move_y(held[0, jz], 1)
                    expert_rows(*paired(jy, jz, [held[jy, jz]]))
        hidden = [jnp.concatenate([blocks[jy, jz][jc * rows:(jc + 1) * rows] for jy in range(ny) for jz in z_order], axis=0)
                  for jc in range(nc)]

        down = down_w.reshape(-1, width)
        share = width // nx
        downs = [lax.dynamic_slice_in_dim(down, (x ^ jx) * share, share, axis=1) for jx in offsets(nx)]
        orders = [[("x", d) for d in steps_of(nx)] + [("y", d) for d in steps_of(ny)],
                  [("y", d) for d in steps_of(ny)] + [("x", d) for d in steps_of(nx)]]
        z_steps = steps_of(nz)
        bounds = [0]
        for w in WIDTHS:
            for _ in range(2):
                bounds.append(bounds[-1] + w * share // (2 * sum(WIDTHS)))
        state = {}

        def product(i, which, jc, far=None):
            w = jnp.concatenate([v[:, bounds[2 * i + which]:bounds[2 * i + which + 1]] for v in downs], axis=1)
            h = hidden[jc]
            if far is not None:
                w, h = (pick(w, "x", far), h) if orders[which][0][0] == "x" else (w, pick(h, "y", far))
            return jnp.dot(h, w, preferred_element_type=jnp.float32)

        def tied(value, key):
            if key is not None:
                value, state[key] = after(value, state[key])
            return value

        def begin(i, keys=(None, None)):
            if i == 0:
                got = {(which, far): move_c(product(i, which, 1, far).astype(jnp.bfloat16), 1)
                       for far in (1, 0) for which in (0, 1)}
            else:
                got = {}
                for which in (0, 1):
                    whole = move_c(product(i, which, 1).astype(jnp.bfloat16), 1)
                    for far in (1, 0):
                        got[which, far] = pick(whole, orders[which][0][0], far)
            for far in (1, 0):
                for which in (0, 1):
                    value = product(i, which, 0, far) + got[which, far].astype(jnp.float32)
                    state[i, which, far] = value.astype(jnp.bfloat16)
            if i + 1 < len(WIDTHS):
                hidden[0], hidden[1], state[i, 0, 1], state[i, 1, 1] = after(
                    hidden[0], hidden[1], state[i, 0, 1], state[i, 1, 1])
            for which in (0, 1):
                axis, d = orders[which][0]
                state[i, which] = moves[axis](tied(state[i, which, 1], keys[which]), d)

        def turn(i, step, keys=(None, None)):
            for which in (0, 1):
                if step < len(orders[which]):
                    axis, d = orders[which][step]
                    value = (state[i, which, 0], state[i, which])
                    far, state[i, which, 0] = half(value, axis, 1), half(value, axis, 0)
                    state[i, which] = moves[axis](tied(far, keys[which]), d)

        def turn_z(i, k, key=None):
            if k == 0:
                values = [(state[i, which, 0], state[i, which]) for which in (0, 1)]
                near, far = [jnp.concatenate([half(v, "z", h) for v in values], axis=1) for h in (0, 1)]
            else:
                value = (state[i, "near"], state[i, "z"])
                if k == len(z_steps):
                    return add(*value)
                near, far = [half(value, "z", h) for h in (0, 1)]
            state[i, "near"], state[i, "z"] = near, move_z(tied(far, key), z_steps[k])

        if (nx, ny, nz) == (2, 2, 4):
            begin(0)
            begin(1, ((0, 0), (0, 1)))
            turn(0, 1, ((1, 1), (1, 0)))
            turn(1, 1, ((0, 0), (0, 1)))
            begin(2, ((1, 1), (1, 0)))
            turn(2, 1, ((2, 1), (2, 0, 0)))
            turn_z(0, 0)
            turn_z(1, 0, (0, "z"))
            turn_z(0, 1)
            turn_z(2, 0, (1, "z"))
            turn_z(1, 1)
            turn_z(2, 1)
        else:
            for i in range(len(WIDTHS)):
                begin(i)
                for step in range(1, len(orders[0])):
                    turn(i, step)
                for k in range(len(z_steps)):
                    turn_z(i, k)
        out = [turn_z(i, len(z_steps)) for i in range(len(WIDTHS))]
        return jnp.concatenate(out, axis=1)

    return shards


def solution(mesh):
    in_specs = (
        P(("groups", "expert"), None),
        P(("groups", "expert"), None),
        P(("groups", "expert"), None),
        P("expert", None, "tensor"),
        P("expert", None, "tensor"),
        P("expert", "tensor", None),
    )
    out_specs = P(("groups", "expert"), "tensor")
    return jax.shard_map(make(mesh), mesh=mesh, in_specs=in_specs, out_specs=out_specs, check_vma=False)
```

```python
import functools

import jax
import jax.numpy as jnp
from jax import lax
from jax.experimental import pallas as pl
from jax.experimental.pallas import tpu as pltpu
from jax.sharding import PartitionSpec as P

WIDTHS = (512, 384, 128)
LANES = 128
VMEM = 4 * 1024 * 1024


def after(*values):
    return lax.optimization_barrier(values)


def add(a, b):
    return (a.astype(jnp.float32) + b.astype(jnp.float32)).astype(jnp.bfloat16)


def offsets(n):
    out, d = [0], n // 2
    while d:
        out, d = out + [o ^ d for o in out], d // 2
    return out


def steps_of(n):
    return [1 << i for i in range(n.bit_length() - 1)]


def pick(value, axis, which):
    dim = 1 if axis == "x" else 0
    size = value.shape[dim] // 2
    return lax.slice_in_dim(value, which * size, (which + 1) * size, axis=dim)


def half(value, axis, which):
    return add(*[pick(v, axis, which) for v in value])


def rows_kernel(halved, all_experts, width, info, *refs):
    pieces = refs[:len(halved)]
    rows_ref, scale_ref, table_ref, sems = refs[-4:]
    block = rows_ref.shape[0] // len(halved)
    copies = []
    for b, count in enumerate(halved):
        size = block // count
        for i in range(count):
            first = b * block + (0 if count == 1 else pl.multiple_of((info[0] ^ i) * size, size))
            source = pieces[b].at[pl.ds(i * size, size)]
            copies.append(pltpu.make_async_copy(
                source.at[:, pl.ds(width, LANES)], table_ref.at[pl.ds(first, size)], sems.at[0, 2 * b + i]))
            copies.append(pltpu.make_async_copy(
                source.at[:, pl.ds(0, width)], rows_ref.at[pl.ds(first, size)], sems.at[1, 2 * b + i]))
    for copy in copies:
        copy.start()
    for copy in copies[::2]:
        copy.wait()
    table = table_ref[...].astype(jnp.float32)
    lane = lax.broadcasted_iota(jnp.int32, table.shape, 1)
    mine = (lane == info[1]) | (lane == info[1] + all_experts) | (lane == info[1] + 2 * all_experts)
    scale_ref[...] = jnp.sum(jnp.where(mine, table, 0.0), axis=1, keepdims=True)
    for copy in copies[1::2]:
        copy.wait()


def gather_rows(blocks, halved, info, all_experts, deps):
    block, width = blocks[0].shape[0], blocks[0].shape[1] - LANES
    size = len(blocks) * block
    return pl.pallas_call(
        functools.partial(rows_kernel, tuple(halved), all_experts, width),
        in_specs=[pl.BlockSpec(memory_space=pltpu.SMEM)] + [pl.BlockSpec(memory_space=pl.ANY)] * (len(blocks) + len(deps)),
        out_specs=[pl.BlockSpec(memory_space=pl.ANY), pl.BlockSpec(memory_space=pltpu.VMEM)],
        scratch_shapes=[
            pltpu.VMEM((size, LANES), jnp.bfloat16),
            pltpu.SemaphoreType.DMA((2, 2 * len(blocks))),
        ],
        out_shape=[jax.ShapeDtypeStruct((size, width), jnp.bfloat16), jax.ShapeDtypeStruct((size, 1), jnp.float32)],
        compiler_params=pltpu.CompilerParams(vmem_limit_bytes=VMEM),
        cost_estimate=pl.CostEstimate(flops=0, bytes_accessed=4 * size * width, transcendentals=0),
        name="gather_rows",
    )(info, *blocks, *deps)


def make(mesh):
    experts, nx = mesh.shape["expert"], mesh.shape["tensor"]
    nc = 2
    ny = 2 if experts // nc == 8 else 1
    nz = experts // (nc * ny)

    def index(z, y, c):
        return (z * ny + y) * nc + c

    places = [(z, y, c) for z in range(nz) for y in range(ny) for c in range(nc)]

    def move_z(a, d):
        return lax.ppermute(a, "expert", [(index(z, y, c), index(z ^ d, y, c)) for z, y, c in places])

    def move_y(a, d):
        return lax.ppermute(a, "expert", [(index(z, y, c), index(z, y ^ d, c)) for z, y, c in places])

    def move_c(a, d):
        return lax.ppermute(a, "expert", [(index(z, y, c), index(z, y, c ^ d)) for z, y, c in places])

    def move_x(a, d):
        return lax.ppermute(a, "tensor", [(i, i ^ d) for i in range(nx)])

    moves = {"x": move_x, "y": move_y, "z": move_z}

    def shards(tokens, expert_ids, route_weights, gate_w, up_w, down_w):
        rows, width = tokens.shape
        local_experts = gate_w.shape[0]
        experts_all = local_experts * experts
        me = lax.axis_index("expert")
        x = lax.axis_index("tensor")
        z_order = offsets(nz)
        assert 3 * experts_all <= LANES
        chosen = expert_ids[:, :, None] == jnp.arange(experts_all, dtype=jnp.int32)
        table = jnp.sum(jnp.where(chosen, route_weights[:, :, None], 0.0), axis=1)
        parts = []
        for _ in range(3):
            parts.append(lax.reduce_precision(table, 8, 7))
            table = table - parts[-1]
        parts.append(jnp.zeros((rows, LANES - 3 * experts_all), jnp.float32))
        table = jnp.concatenate(parts, axis=1).astype(jnp.bfloat16)
        wide = jnp.concatenate([tokens, table], axis=1)

        blocks, ran = {}, []

        def expert_rows(*places):
            values = []
            pieces = [v for place in places for v in place[2:4]]
            halved = [place[4] for place in places for _ in range(nc)]
            for e in range(local_experts):
                info = jnp.stack([x, me * local_experts + e]).astype(jnp.int32)
                pair, scale = gather_rows(pieces, halved, info, experts_all, ran[-1:])
                gate = jnp.dot(pair, gate_w[e], preferred_element_type=jnp.float32)
                up_part = jnp.dot(pair, up_w[e], preferred_element_type=jnp.float32)
                values.append((jax.nn.silu(gate) * up_part * scale).astype(jnp.bfloat16))
                ran.append(values[-1])
            value = jnp.concatenate(values, axis=1) if local_experts > 1 else values[0]
            for k, place in enumerate(places):
                for jc in range(nc):
                    blocks[jc, place[0], place[1]] = value[(nc * k + jc) * rows:(nc * k + jc + 1) * rows]
            return value

        if (nx, ny, nz) == (2, 2, 4):
            low = jnp.equal(x, 0)
            first, second = wide[:rows // 2], wide[rows // 2:]
            m, r = jnp.where(low, first, second), jnp.where(low, second, first)

            def joined(a, b):
                return jnp.concatenate([a, b], axis=0)

            y0, z1m, z2m, c00 = move_y(wide, 1), move_z(m, 1), move_z(m, 2), move_c(wide, 1)
            y0, z1m, z2m, c00, r = after(y0, z1m, z2m, c00, r)
            y1m, x0r, z3m, z2r, c10 = move_y(z1m, 1), move_x(z1m, 1), move_z(z2m, 1), move_z(r, 2), move_c(y0, 1)
            h = expert_rows((0, 0, wide, c00, 1))
            y1m, x0r, z3m, c10, h, z1m, z2m = after(y1m, x0r, z3m, c10, h, z1m, z2m)
            b01 = joined(z1m, x0r)
            y2m, x1r, c01 = move_y(z2m, 1), move_x(y1m, 1), move_c(b01, 1)
            h = expert_rows((1, 0, y0, c10, 1))
            y2m, x1r, c01, z2r, h, y1m, z2m, z3m = after(y2m, x1r, c01, z2r, h, y1m, z2m, z3m)
            b11, b02 = joined(y1m, x1r), joined(z2m, z2r)
            y3m, x2r, z3r, c11, c02 = move_y(z3m, 1), move_x(y2m, 1), move_z(z2r, 1), move_c(b11, 1), move_c(b02, 1)
            h = expert_rows((0, 1, b01, c01, 2))
            y3m, x2r, z3r, c11, c02, h, y2m, z3m = after(y3m, x2r, z3r, c11, c02, h, y2m, z3m)
            b12, b03 = joined(y2m, x2r), joined(z3m, z3r)
            x3r, c12, c03 = move_x(y3m, 1), move_c(b12, 1), move_c(b03, 1)
            h = expert_rows((1, 1, b11, c11, 2))
            x3r, c12, c03, h, y3m = after(x3r, c12, c03, h, y3m)
            b13 = joined(y3m, x3r)
            c13 = move_c(b13, 1)
            expert_rows((0, 2, b02, c02, 2), (1, 2, b12, c12, 2), (0, 3, b03, c03, 2), (1, 3, b13, c13, 2))
        else:
            held = {(0, 0): wide}
            for d in reversed(steps_of(nz)):
                for jz in sorted((key[1] for key in held), reverse=True):
                    held[0, jz ^ d] = move_z(held[0, jz], d)
            for jz in z_order:
                for jy in range(ny):
                    if jy:
                        held[1, jz] = move_y(held[0, jz], 1)
                    expert_rows((jy, jz, held[jy, jz], move_c(held[jy, jz], 1), 1))
        hidden = [jnp.concatenate([blocks[jc, jy, jz] for jy in range(ny) for jz in z_order], axis=0)
                  for jc in range(nc)]

        down = down_w.reshape(-1, width)
        share = width // nx
        downs = [lax.dynamic_slice_in_dim(down, (x ^ jx) * share, share, axis=1) for jx in offsets(nx)]
        orders = [[("x", d) for d in steps_of(nx)] + [("y", d) for d in steps_of(ny)],
                  [("y", d) for d in steps_of(ny)] + [("x", d) for d in steps_of(nx)]]
        z_steps = steps_of(nz)
        bounds = [0]
        for w in WIDTHS:
            for _ in range(2):
                bounds.append(bounds[-1] + w * share // (2 * sum(WIDTHS)))
        state = {}

        def product(i, which, jc, far=None):
            w = jnp.concatenate([v[:, bounds[2 * i + which]:bounds[2 * i + which + 1]] for v in downs], axis=1)
            h = hidden[jc]
            if far is not None:
                w, h = (pick(w, "x", far), h) if orders[which][0][0] == "x" else (w, pick(h, "y", far))
            return jnp.dot(h, w, preferred_element_type=jnp.float32)

        def tied(value, key):
            if key is not None:
                value, state[key] = after(value, state[key])
            return value

        def begin(i, keys=(None, None)):
            if i == 0:
                got = {(which, far): move_c(product(i, which, 1, far).astype(jnp.bfloat16), 1)
                       for far in (1, 0) for which in (0, 1)}
            else:
                got = {}
                for which in (0, 1):
                    whole = move_c(product(i, which, 1).astype(jnp.bfloat16), 1)
                    for far in (1, 0):
                        got[which, far] = pick(whole, orders[which][0][0], far)
            for far in (1, 0):
                for which in (0, 1):
                    value = product(i, which, 0, far) + got[which, far].astype(jnp.float32)
                    state[i, which, far] = value.astype(jnp.bfloat16)
            if i + 1 < len(WIDTHS):
                hidden[0], hidden[1], state[i, 0, 1], state[i, 1, 1] = after(
                    hidden[0], hidden[1], state[i, 0, 1], state[i, 1, 1])
            for which in (0, 1):
                axis, d = orders[which][0]
                state[i, which] = moves[axis](tied(state[i, which, 1], keys[which]), d)

        def turn(i, step, keys=(None, None)):
            for which in (0, 1):
                if step < len(orders[which]):
                    axis, d = orders[which][step]
                    value = (state[i, which, 0], state[i, which])
                    far, state[i, which, 0] = half(value, axis, 1), half(value, axis, 0)
                    state[i, which] = moves[axis](tied(far, keys[which]), d)

        def turn_z(i, k, key=None):
            if k == 0:
                values = [(state[i, which, 0], state[i, which]) for which in (0, 1)]
                near, far = [jnp.concatenate([half(v, "z", h) for v in values], axis=1) for h in (0, 1)]
            else:
                value = (state[i, "near"], state[i, "z"])
                if k == len(z_steps):
                    return add(*value)
                near, far = [half(value, "z", h) for h in (0, 1)]
            state[i, "near"], state[i, "z"] = near, move_z(tied(far, key), z_steps[k])

        if (nx, ny, nz) == (2, 2, 4):
            begin(0)
            begin(1, ((0, 0), (0, 1)))
            turn(0, 1, ((1, 1), (1, 0)))
            turn(1, 1, ((0, 0), (0, 1)))
            begin(2, ((1, 1), (1, 0)))
            turn(2, 1, ((2, 1), (2, 0, 0)))
            turn_z(0, 0)
            turn_z(1, 0, (0, "z"))
            turn_z(0, 1)
            turn_z(2, 0, (1, "z"))
            turn_z(1, 1)
            turn_z(2, 1)
        else:
            for i in range(len(WIDTHS)):
                begin(i)
                for step in range(1, len(orders[0])):
                    turn(i, step)
                for k in range(len(z_steps)):
                    turn_z(i, k)
        out = [turn_z(i, len(z_steps)) for i in range(len(WIDTHS))]
        return jnp.concatenate(out, axis=1)

    return shards


def solution(mesh):
    in_specs = (
        P(("groups", "expert"), None),
        P(("groups", "expert"), None),
        P(("groups", "expert"), None),
        P("expert", None, "tensor"),
        P("expert", None, "tensor"),
        P("expert", "tensor", None),
    )
    out_specs = P(("groups", "expert"), "tensor")
    return jax.shard_map(make(mesh), mesh=mesh, in_specs=in_specs, out_specs=out_specs, check_vma=False)
```

```python
import jax
import jax.numpy as jnp
from jax import lax
from jax.sharding import PartitionSpec as P

WIDTHS = (512, 384, 128)


def after(*values):
    return lax.optimization_barrier(values)


def add(a, b):
    return (a.astype(jnp.float32) + b.astype(jnp.float32)).astype(jnp.bfloat16)


def offsets(n):
    out, d = [0], n // 2
    while d:
        out, d = out + [o ^ d for o in out], d // 2
    return out


def steps_of(n):
    return [1 << i for i in range(n.bit_length() - 1)]


def pick(value, axis, which):
    dim = 1 if axis == "x" else 0
    size = value.shape[dim] // 2
    return lax.slice_in_dim(value, which * size, (which + 1) * size, axis=dim)


def half(value, axis, which):
    return add(*[pick(v, axis, which) for v in value])


def make(mesh):
    experts, nx = mesh.shape["expert"], mesh.shape["tensor"]
    nc = 2
    ny = 2 if experts // nc == 8 else 1
    nz = experts // (nc * ny)

    def index(z, y, c):
        return (z * ny + y) * nc + c

    places = [(z, y, c) for z in range(nz) for y in range(ny) for c in range(nc)]

    def move_z(a, d):
        return lax.ppermute(a, "expert", [(index(z, y, c), index(z ^ d, y, c)) for z, y, c in places])

    def move_y(a, d):
        return lax.ppermute(a, "expert", [(index(z, y, c), index(z, y ^ d, c)) for z, y, c in places])

    def move_c(a, d):
        return lax.ppermute(a, "expert", [(index(z, y, c), index(z, y, c ^ d)) for z, y, c in places])

    def move_x(a, d):
        return lax.ppermute(a, "tensor", [(i, i ^ d) for i in range(nx)])

    moves = {"x": move_x, "y": move_y, "z": move_z}

    def shards(tokens, expert_ids, route_weights, gate_w, up_w, down_w):
        rows, width = tokens.shape
        local_experts = gate_w.shape[0]
        experts_all = local_experts * experts
        me = lax.axis_index("expert")
        x = lax.axis_index("tensor")
        z_order = offsets(nz)
        chosen = expert_ids[None, :, :] == jnp.arange(experts_all, dtype=jnp.int32)[:, None, None]
        table = jnp.sum(jnp.where(chosen, route_weights[None], 0.0), axis=2)
        table = lax.all_to_all(table, "expert", split_axis=0, concat_axis=0, tiled=True)
        tokens, table = after(tokens, table)
        table = table.reshape(experts, local_experts, rows)
        down = down_w.reshape(-1, width)
        share = width // nx
        downs = [lax.dynamic_slice_in_dim(down, (x ^ jx) * share, share, axis=1) for jx in offsets(nx)]
        blocks = {}

        def expert_rows(jy, jz, near, far):
            pair = jnp.concatenate(near + far, axis=0)
            values = []
            for e in range(local_experts):
                scale = []
                for jc in range(nc):
                    row = lax.dynamic_slice(table, (me ^ index(jz, jy, jc), e, 0), (1, 1, rows)).reshape(rows)
                    if len(near) == 2:
                        row = jnp.concatenate(in_order(row[:rows // 2], row[rows // 2:]))
                    scale.append(row)
                scale = jnp.concatenate(scale)[:, None]
                gate = jnp.dot(pair, gate_w[e], preferred_element_type=jnp.float32)
                up_part = jnp.dot(pair, up_w[e], preferred_element_type=jnp.float32)
                values.append((jax.nn.silu(gate) * up_part * scale).astype(jnp.bfloat16))
            value = jnp.concatenate(values, axis=1) if local_experts > 1 else values[0]
            blocks[jy, jz] = value, len(near)
            return value

        def in_order(a, b):
            return jnp.where(low, a, b), jnp.where(low, b, a)

        low = jnp.equal(x, 0)
        if (nx, ny, nz) == (2, 2, 4):
            m, r = in_order(tokens[:rows // 2], tokens[rows // 2:])
            y0, z1m, z2m, c00 = move_y(tokens, 1), move_z(m, 1), move_z(m, 2), move_c(tokens, 1)
            y0, z1m, z2m, c00, downs[0], downs[1] = after(y0, z1m, z2m, c00, downs[0], downs[1])
            y1m, x0r, z3m, c10, c01m = move_y(z1m, 1), move_x(z1m, 1), move_z(z2m, 1), move_c(y0, 1), move_c(z1m, 1)
            h00 = expert_rows(0, 0, [tokens], [c00])
            y1m, x0r, z3m, c10, c01m, h00, r, z2m = after(y1m, x0r, z3m, c10, c01m, h00, r, z2m)
            y2m, x1r, z2r, c01r, c02m = move_y(z2m, 1), move_x(y1m, 1), move_z(r, 2), move_c(x0r, 1), move_c(z2m, 1)
            h10 = expert_rows(1, 0, [y0], [c10])
            y2m, x1r, c01r, c02m, h10, z3m, y1m = after(y2m, x1r, c01r, c02m, h10, z3m, y1m)
            y3m, x2r, c11m, c11r = move_y(z3m, 1), move_x(y2m, 1), move_c(y1m, 1), move_c(x1r, 1)
            h01 = expert_rows(0, 1, [z1m, x0r], [c01m, c01r])
            y3m, x2r, z2r, c11m, c11r, h01, y2m = after(y3m, x2r, z2r, c11m, c11r, h01, y2m)
            x3r, z3r, c02r, c12m, c12r = move_x(y3m, 1), move_z(z2r, 1), move_c(z2r, 1), move_c(y2m, 1), move_c(x2r, 1)
            h11 = expert_rows(1, 1, [y1m, x1r], [c11m, c11r])
            x3r, z3r, c02r, c12m, c12r, h11, z3m, y3m = after(x3r, z3r, c02r, c12m, c12r, h11, z3m, y3m)
            c03m, c03r, c13m, c13r = move_c(z3m, 1), move_c(z3r, 1), move_c(y3m, 1), move_c(x3r, 1)
            expert_rows(0, 2, [z2m, z2r], [c02m, c02r])
            expert_rows(1, 2, [y2m, x2r], [c12m, c12r])
            expert_rows(0, 3, [z3m, z3r], [c03m, c03r])
            expert_rows(1, 3, [y3m, x3r], [c13m, c13r])
            for place, h in (((0, 0), h00), ((1, 0), h10), ((0, 1), h01), ((1, 1), h11)):
                blocks[place] = h, blocks[place][1]
        else:
            held = {(0, 0): tokens}
            for d in reversed(steps_of(nz)):
                for jz in sorted((key[1] for key in held), reverse=True):
                    held[0, jz ^ d] = move_z(held[0, jz], d)
            for jz in z_order:
                for jy in range(ny):
                    if jy:
                        held[1, jz] = move_y(held[0, jz], 1)
                    expert_rows(jy, jz, [held[jy, jz]], [move_c(held[jy, jz], 1)])
        hidden = []
        for jc in range(nc):
            parts = []
            for jy in range(ny):
                for jz in z_order:
                    value, count = blocks[jy, jz]
                    value = value[jc * rows:(jc + 1) * rows]
                    parts += in_order(value[:rows // 2], value[rows // 2:]) if count == 2 else [value]
            hidden.append(jnp.concatenate(parts, axis=0))

        orders = [[("x", d) for d in steps_of(nx)] + [("y", d) for d in steps_of(ny)],
                  [("y", d) for d in steps_of(ny)] + [("x", d) for d in steps_of(nx)]]
        z_steps = steps_of(nz)
        bounds = [0]
        for w in WIDTHS:
            for _ in range(2):
                bounds.append(bounds[-1] + w * share // (2 * sum(WIDTHS)))
        state = {}

        def product(i, which, jc, far=None):
            w = jnp.concatenate([v[:, bounds[2 * i + which]:bounds[2 * i + which + 1]] for v in downs], axis=1)
            h = hidden[jc]
            if far is not None:
                w, h = (pick(w, "x", far), h) if orders[which][0][0] == "x" else (w, pick(h, "y", far))
            return jnp.dot(h, w, preferred_element_type=jnp.float32)

        def tied(value, key):
            if key is not None:
                value, state[key] = after(value, state[key])
            return value

        def begin(i, keys=(None, None)):
            if i == 0:
                got = {(which, far): move_c(product(i, which, 1, far).astype(jnp.bfloat16), 1)
                       for far in (1, 0) for which in (0, 1)}
            else:
                got = {}
                for which in (0, 1):
                    whole = move_c(product(i, which, 1).astype(jnp.bfloat16), 1)
                    for far in (1, 0):
                        got[which, far] = pick(whole, orders[which][0][0], far)
            for far in (1, 0):
                for which in (0, 1):
                    value = product(i, which, 0, far) + got[which, far].astype(jnp.float32)
                    state[i, which, far] = value.astype(jnp.bfloat16)
            if i + 1 < len(WIDTHS):
                hidden[0], hidden[1], state[i, 0, 1], state[i, 1, 1] = after(
                    hidden[0], hidden[1], state[i, 0, 1], state[i, 1, 1])
            for which in (0, 1):
                axis, d = orders[which][0]
                state[i, which] = moves[axis](tied(state[i, which, 1], keys[which]), d)

        def turn(i, step, keys=(None, None)):
            for which in (0, 1):
                if step < len(orders[which]):
                    axis, d = orders[which][step]
                    value = (state[i, which, 0], state[i, which])
                    far, state[i, which, 0] = half(value, axis, 1), half(value, axis, 0)
                    state[i, which] = moves[axis](tied(far, keys[which]), d)

        def turn_z(i, k, key=None):
            if k == 0:
                values = [(state[i, which, 0], state[i, which]) for which in (0, 1)]
                near, far = [jnp.concatenate([half(v, "z", h) for v in values], axis=1) for h in (0, 1)]
            else:
                value = (state[i, "near"], state[i, "z"])
                if k == len(z_steps):
                    return add(*value)
                near, far = [half(value, "z", h) for h in (0, 1)]
            state[i, "near"], state[i, "z"] = near, move_z(tied(far, key), z_steps[k])

        if (nx, ny, nz) == (2, 2, 4):
            begin(0)
            begin(1, ((0, 0), (0, 1)))
            turn(0, 1, ((1, 1), (1, 0)))
            turn(1, 1, ((0, 0), (0, 1)))
            begin(2, ((1, 1), (1, 0)))
            turn(2, 1, ((2, 1), (2, 0, 0)))
            turn_z(0, 0)
            turn_z(1, 0, (0, "z"))
            turn_z(0, 1)
            turn_z(2, 0, (1, "z"))
            turn_z(1, 1)
            turn_z(2, 1)
        else:
            for i in range(len(WIDTHS)):
                begin(i)
                for step in range(1, len(orders[0])):
                    turn(i, step)
                for k in range(len(z_steps)):
                    turn_z(i, k)
        out = [turn_z(i, len(z_steps)) for i in range(len(WIDTHS))]
        return jnp.concatenate(out, axis=1)

    return shards


def solution(mesh):
    in_specs = (
        P(("groups", "expert"), None),
        P(("groups", "expert"), None),
        P(("groups", "expert"), None),
        P("expert", None, "tensor"),
        P("expert", None, "tensor"),
        P("expert", "tensor", None),
    )
    out_specs = P(("groups", "expert"), "tensor")
    return jax.shard_map(make(mesh), mesh=mesh, in_specs=in_specs, out_specs=out_specs, check_vma=False)
```

```python
import jax
import jax.numpy as jnp
from jax import lax
from jax.sharding import PartitionSpec as P

WIDTHS = (512, 384, 128)


def after(*values):
    return lax.optimization_barrier(values)


def add(a, b):
    return (a.astype(jnp.float32) + b.astype(jnp.float32)).astype(jnp.bfloat16)


def offsets(n):
    out, d = [0], n // 2
    while d:
        out, d = out + [o ^ d for o in out], d // 2
    return out


def steps_of(n):
    return [1 << i for i in range(n.bit_length() - 1)]


def pick(value, axis, which):
    dim = 1 if axis == "x" else 0
    size = value.shape[dim] // 2
    return lax.slice_in_dim(value, which * size, (which + 1) * size, axis=dim)


def half(value, axis, which):
    return add(*[pick(v, axis, which) for v in value])


def make(mesh):
    experts, nx = mesh.shape["expert"], mesh.shape["tensor"]
    nc = 2
    ny = 2 if experts // nc == 8 else 1
    nz = experts // (nc * ny)

    def index(z, y, c):
        return (z * ny + y) * nc + c

    places = [(z, y, c) for z in range(nz) for y in range(ny) for c in range(nc)]

    def move_z(a, d):
        return lax.ppermute(a, "expert", [(index(z, y, c), index(z ^ d, y, c)) for z, y, c in places])

    def move_y(a, d):
        return lax.ppermute(a, "expert", [(index(z, y, c), index(z, y ^ d, c)) for z, y, c in places])

    def move_c(a, d):
        return lax.ppermute(a, "expert", [(index(z, y, c), index(z, y, c ^ d)) for z, y, c in places])

    def move_x(a, d):
        return lax.ppermute(a, "tensor", [(i, i ^ d) for i in range(nx)])

    moves = {"x": move_x, "y": move_y, "z": move_z}

    def shards(tokens, expert_ids, route_weights, gate_w, up_w, down_w):
        rows, width = tokens.shape
        local_experts = gate_w.shape[0]
        experts_all = local_experts * experts
        me = lax.axis_index("expert")
        x = lax.axis_index("tensor")
        z_order = offsets(nz)
        chosen = expert_ids[None, :, :] == jnp.arange(experts_all, dtype=jnp.int32)[:, None, None]
        table = jnp.sum(jnp.where(chosen, route_weights[None], 0.0), axis=2)
        table = lax.all_to_all(table, "expert", split_axis=0, concat_axis=0, tiled=True)
        tokens, table = after(tokens, table)
        table = table.reshape(experts, local_experts, rows)
        down = down_w.reshape(-1, width)
        share = width // nx
        blocks = {}

        def expert_rows(jy, jz, near, far):
            pair = jnp.concatenate(near + far, axis=0)
            values = []
            for e in range(local_experts):
                scale = []
                for jc in range(nc):
                    row = lax.dynamic_slice(table, (me ^ index(jz, jy, jc), e, 0), (1, 1, rows)).reshape(rows)
                    if (jy, jz) in halved:
                        row = jnp.concatenate(in_order(row[:rows // 2], row[rows // 2:]))
                    scale.append(row)
                scale = jnp.concatenate(scale)[:, None]
                gate = jnp.dot(pair, gate_w[e], preferred_element_type=jnp.float32)
                up_part = jnp.dot(pair, up_w[e], preferred_element_type=jnp.float32)
                values.append((jax.nn.silu(gate) * up_part * scale).astype(jnp.bfloat16))
            value = jnp.concatenate(values, axis=1) if local_experts > 1 else values[0]
            blocks[jy, jz] = value
            return value

        def joined(a, b):
            return jnp.concatenate([a, b], axis=0)

        def in_order(a, b):
            return jnp.where(low, a, b), jnp.where(low, b, a)

        low = jnp.equal(x, 0)
        halved = [(0, 1), (1, 1), (0, 2), (1, 2), (0, 3), (1, 3)] if (nx, ny, nz) == (2, 2, 4) else []
        if (nx, ny, nz) == (2, 2, 4):
            m, r = in_order(tokens[:rows // 2], tokens[rows // 2:])
            y0, z1m, z2m, c00 = move_y(tokens, 1), move_z(m, 1), move_z(m, 2), move_c(tokens, 1)
            c00, down = after(c00, down)
            downs = [lax.dynamic_slice_in_dim(down, (x ^ jx) * share, share, axis=1) for jx in offsets(nx)]
            y0, z1m, z2m, c00, r, downs[0], downs[1] = after(y0, z1m, z2m, c00, r, downs[0], downs[1])
            y1m, x0r, z3m, z2r, c10 = move_y(z1m, 1), move_x(z1m, 1), move_z(z2m, 1), move_z(r, 2), move_c(y0, 1)
            h00 = expert_rows(0, 0, [tokens], [c00])
            y1m, x0r, c10, h00, z1m, z2m = after(y1m, x0r, c10, h00, z1m, z2m)
            b01 = joined(z1m, x0r)
            y2m, x1r, c01 = move_y(z2m, 1), move_x(y1m, 1), move_c(b01, 1)
            h10 = expert_rows(1, 0, [y0], [c10])
            y2m, x1r, c01, z3m, z2r, h10, y1m, z2m = after(y2m, x1r, c01, z3m, z2r, h10, y1m, z2m)
            b11, b02 = joined(y1m, x1r), joined(z2m, z2r)
            y3m, x2r, z3r, c11, c02 = move_y(z3m, 1), move_x(y2m, 1), move_z(z2r, 1), move_c(b11, 1), move_c(b02, 1)
            h01 = expert_rows(0, 1, [b01], [c01])
            y3m, x2r, z3r, c11, c02, h01, y2m, z3m = after(y3m, x2r, z3r, c11, c02, h01, y2m, z3m)
            b12, b03 = joined(y2m, x2r), joined(z3m, z3r)
            x3r, c12, c03, c13m = move_x(y3m, 1), move_c(b12, 1), move_c(b03, 1), move_c(y3m, 1)
            h11 = expert_rows(1, 1, [b11], [c11])
            x3r, c12, c03, c13m, h11 = after(x3r, c12, c03, c13m, h11)
            c13r = move_c(x3r, 1)
            expert_rows(0, 2, [b02], [c02])
            expert_rows(1, 2, [b12], [c12])
            expert_rows(0, 3, [b03], [c03])
            expert_rows(1, 3, [y3m, x3r], [c13m, c13r])
            for place, h in (((0, 0), h00), ((1, 0), h10), ((0, 1), h01), ((1, 1), h11)):
                blocks[place] = h
        else:
            downs = [lax.dynamic_slice_in_dim(down, (x ^ jx) * share, share, axis=1) for jx in offsets(nx)]
            held = {(0, 0): tokens}
            for d in reversed(steps_of(nz)):
                for jz in sorted((key[1] for key in held), reverse=True):
                    held[0, jz ^ d] = move_z(held[0, jz], d)
            for jz in z_order:
                for jy in range(ny):
                    if jy:
                        held[1, jz] = move_y(held[0, jz], 1)
                    expert_rows(jy, jz, [held[jy, jz]], [move_c(held[jy, jz], 1)])
        hidden = []
        for jc in range(nc):
            parts = []
            for jy in range(ny):
                for jz in z_order:
                    value = blocks[jy, jz][jc * rows:(jc + 1) * rows]
                    parts += in_order(value[:rows // 2], value[rows // 2:]) if (jy, jz) in halved else [value]
            hidden.append(jnp.concatenate(parts, axis=0))

        orders = [[("x", d) for d in steps_of(nx)] + [("y", d) for d in steps_of(ny)],
                  [("y", d) for d in steps_of(ny)] + [("x", d) for d in steps_of(nx)]]
        z_steps = steps_of(nz)
        bounds = [0]
        for w in WIDTHS:
            for _ in range(2):
                bounds.append(bounds[-1] + w * share // (2 * sum(WIDTHS)))
        state = {}

        def product(i, which, jc, far=None):
            w = jnp.concatenate([v[:, bounds[2 * i + which]:bounds[2 * i + which + 1]] for v in downs], axis=1)
            h = hidden[jc]
            if far is not None:
                w, h = (pick(w, "x", far), h) if orders[which][0][0] == "x" else (w, pick(h, "y", far))
            return jnp.dot(h, w, preferred_element_type=jnp.float32)

        def tied(value, key):
            if key is not None:
                value, state[key] = after(value, state[key])
            return value

        def begin(i, keys=(None, None)):
            if i == 0:
                got = {(which, far): move_c(product(i, which, 1, far).astype(jnp.bfloat16), 1)
                       for far in (1, 0) for which in (0, 1)}
            else:
                got = {}
                for which in (0, 1):
                    whole = move_c(product(i, which, 1).astype(jnp.bfloat16), 1)
                    for far in (1, 0):
                        got[which, far] = pick(whole, orders[which][0][0], far)
            for far in (1, 0):
                for which in (0, 1):
                    value = product(i, which, 0, far) + got[which, far].astype(jnp.float32)
                    state[i, which, far] = value.astype(jnp.bfloat16)
            if i + 1 < len(WIDTHS):
                hidden[0], hidden[1], state[i, 0, 1], state[i, 1, 1] = after(
                    hidden[0], hidden[1], state[i, 0, 1], state[i, 1, 1])
            for which in (0, 1):
                axis, d = orders[which][0]
                state[i, which] = moves[axis](tied(state[i, which, 1], keys[which]), d)

        def turn(i, step, keys=(None, None)):
            for which in (0, 1):
                if step < len(orders[which]):
                    axis, d = orders[which][step]
                    value = (state[i, which, 0], state[i, which])
                    far, state[i, which, 0] = half(value, axis, 1), half(value, axis, 0)
                    state[i, which] = moves[axis](tied(far, keys[which]), d)

        def turn_z(i, k, key=None):
            if k == 0:
                values = [(state[i, which, 0], state[i, which]) for which in (0, 1)]
                near, far = [jnp.concatenate([half(v, "z", h) for v in values], axis=1) for h in (0, 1)]
            else:
                value = (state[i, "near"], state[i, "z"])
                if k == len(z_steps):
                    return add(*value)
                near, far = [half(value, "z", h) for h in (0, 1)]
            state[i, "near"], state[i, "z"] = near, move_z(tied(far, key), z_steps[k])

        if (nx, ny, nz) == (2, 2, 4):
            begin(0)
            turn(0, 1, ((0, 1), (0, 0, 0)))
            begin(1, ((0, 1), (0, 0)))
            turn(1, 1, ((1, 1), (1, 0, 0)))
            begin(2, ((1, 1), (1, 0)))
            turn(2, 1, ((2, 1), (2, 0, 0)))
            turn_z(0, 0)
            turn_z(1, 0, (0, "z"))
            turn_z(0, 1)
            turn_z(2, 0, (1, "z"))
            turn_z(1, 1)
            turn_z(2, 1)
        else:
            for i in range(len(WIDTHS)):
                begin(i)
                for step in range(1, len(orders[0])):
                    turn(i, step)
                for k in range(len(z_steps)):
                    turn_z(i, k)
        out = [turn_z(i, len(z_steps)) for i in range(len(WIDTHS))]
        return jnp.concatenate(out, axis=1)

    return shards


def solution(mesh):
    in_specs = (
        P(("groups", "expert"), None),
        P(("groups", "expert"), None),
        P(("groups", "expert"), None),
        P("expert", None, "tensor"),
        P("expert", None, "tensor"),
        P("expert", "tensor", None),
    )
    out_specs = P(("groups", "expert"), "tensor")
    return jax.shard_map(make(mesh), mesh=mesh, in_specs=in_specs, out_specs=out_specs, check_vma=False)
```

```python
import jax
import jax.numpy as jnp
from jax import lax
from jax.sharding import PartitionSpec as P

WIDTHS = (512, 384, 128)


def after(*values):
    return lax.optimization_barrier(values)


def add(a, b):
    return (a.astype(jnp.float32) + b.astype(jnp.float32)).astype(jnp.bfloat16)


def offsets(n):
    out, d = [0], n // 2
    while d:
        out, d = out + [o ^ d for o in out], d // 2
    return out


def steps_of(n):
    return [1 << i for i in range(n.bit_length() - 1)]


def pick(value, axis, which):
    dim = 1 if axis == "x" else 0
    size = value.shape[dim] // 2
    return lax.slice_in_dim(value, which * size, (which + 1) * size, axis=dim)


def half(value, axis, which):
    return add(*[pick(v, axis, which) for v in value])


def make(mesh):
    experts, nx = mesh.shape["expert"], mesh.shape["tensor"]
    nc = 2
    ny = 2 if experts // nc == 8 else 1
    nz = experts // (nc * ny)

    def index(z, y, c):
        return (z * ny + y) * nc + c

    places = [(z, y, c) for z in range(nz) for y in range(ny) for c in range(nc)]

    def move_z(a, d):
        return lax.ppermute(a, "expert", [(index(z, y, c), index(z ^ d, y, c)) for z, y, c in places])

    def move_y(a, d):
        return lax.ppermute(a, "expert", [(index(z, y, c), index(z, y ^ d, c)) for z, y, c in places])

    def move_c(a, d):
        return lax.ppermute(a, "expert", [(index(z, y, c), index(z, y, c ^ d)) for z, y, c in places])

    def move_x(a, d):
        return lax.ppermute(a, "tensor", [(i, i ^ d) for i in range(nx)])

    moves = {"x": move_x, "y": move_y, "z": move_z}

    def shards(tokens, expert_ids, route_weights, gate_w, up_w, down_w):
        rows, width = tokens.shape
        local_experts = gate_w.shape[0]
        experts_all = local_experts * experts
        me = lax.axis_index("expert")
        x = lax.axis_index("tensor")
        z_order = offsets(nz)
        chosen = expert_ids[None, :, :] == jnp.arange(experts_all, dtype=jnp.int32)[:, None, None]
        table = jnp.sum(jnp.where(chosen, route_weights[None], 0.0), axis=2)
        table = lax.all_to_all(table, "expert", split_axis=0, concat_axis=0, tiled=True)
        down = down_w.reshape(-1, width)
        share = width // nx
        bounds = [0]
        for w in WIDTHS:
            for _ in range(2):
                bounds.append(bounds[-1] + w * share // (2 * sum(WIDTHS)))
        blocks, weights = {}, {}

        def chunk_weights(i, which):
            first, last = bounds[2 * i + which:2 * i + which + 2]
            return jnp.concatenate([
                lax.dynamic_slice_in_dim(down, (x ^ jx) * share + first, last - first, axis=1) for jx in offsets(nx)], axis=1)

        def expert_rows(jy, jz, near, far):
            pair = jnp.concatenate(near + far, axis=0)
            values = []
            for e in range(local_experts):
                scale = []
                for jc in range(nc):
                    row = lax.dynamic_slice(
                        table, ((me ^ index(jz, jy, jc)) * local_experts + e, 0), (1, rows)).reshape(rows)
                    if (jy, jz) in halved:
                        row = jnp.concatenate(in_order(row[:rows // 2], row[rows // 2:]))
                    scale.append(row)
                scale = jnp.concatenate(scale)[:, None]
                gate = jnp.dot(pair, gate_w[e], preferred_element_type=jnp.float32)
                up_part = jnp.dot(pair, up_w[e], preferred_element_type=jnp.float32)
                values.append((jax.nn.silu(gate) * up_part * scale).astype(jnp.bfloat16))
            value = jnp.concatenate(values, axis=1) if local_experts > 1 else values[0]
            blocks[jy, jz] = value
            return value

        def joined(a, b):
            return jnp.concatenate([a, b], axis=0)

        def in_order(a, b):
            return jnp.where(low, a, b), jnp.where(low, b, a)

        low = jnp.equal(x, 0)
        halved = [(0, 1), (1, 1), (0, 2), (1, 2), (0, 3), (1, 3)] if (nx, ny, nz) == (2, 2, 4) else []
        if (nx, ny, nz) == (2, 2, 4):
            m, r = in_order(tokens[:rows // 2], tokens[rows // 2:])
            y0, z1m, z2m, c00 = move_y(tokens, 1), move_z(m, 1), move_z(m, 2), move_c(tokens, 1)
            c00, down = after(c00, down)
            weights.update({(0, which): chunk_weights(0, which) for which in (0, 1)})
            y0, z1m, z2m, c00, r, table, weights[0, 0], weights[0, 1] = after(
                y0, z1m, z2m, c00, r, table, weights[0, 0], weights[0, 1])
            y1m, x0r, z3m, z2r, c10 = move_y(z1m, 1), move_x(z1m, 1), move_z(z2m, 1), move_z(r, 2), move_c(y0, 1)
            h00 = expert_rows(0, 0, [tokens], [c00])
            y1m, x0r, c10, h00, z1m, z2m = after(y1m, x0r, c10, h00, z1m, z2m)
            b01 = joined(z1m, x0r)
            y2m, x1r, c01 = move_y(z2m, 1), move_x(y1m, 1), move_c(b01, 1)
            h10 = expert_rows(1, 0, [y0], [c10])
            y2m, x1r, c01, z3m, z2r, h10, y1m, z2m = after(y2m, x1r, c01, z3m, z2r, h10, y1m, z2m)
            b11, b02 = joined(y1m, x1r), joined(z2m, z2r)
            y3m, x2r, z3r, c11, c02 = move_y(z3m, 1), move_x(y2m, 1), move_z(z2r, 1), move_c(b11, 1), move_c(b02, 1)
            h01 = expert_rows(0, 1, [b01], [c01])
            y3m, x2r, z3r, c11, c02, h01, y2m, z3m = after(y3m, x2r, z3r, c11, c02, h01, y2m, z3m)
            b12, b03 = joined(y2m, x2r), joined(z3m, z3r)
            x3r, c12, c03, c13m = move_x(y3m, 1), move_c(b12, 1), move_c(b03, 1), move_c(y3m, 1)
            h11 = expert_rows(1, 1, [b11], [c11])
            x3r, c12, c03, c13m, h11 = after(x3r, c12, c03, c13m, h11)
            c13r = move_c(x3r, 1)
            expert_rows(0, 2, [b02], [c02])
            expert_rows(1, 2, [b12], [c12])
            expert_rows(0, 3, [b03], [c03])
            expert_rows(1, 3, [y3m, x3r], [c13m, c13r])
            for place, h in (((0, 0), h00), ((1, 0), h10), ((0, 1), h01), ((1, 1), h11)):
                blocks[place] = h
        else:
            held = {(0, 0): tokens}
            for d in reversed(steps_of(nz)):
                for jz in sorted((key[1] for key in held), reverse=True):
                    held[0, jz ^ d] = move_z(held[0, jz], d)
            for jz in z_order:
                for jy in range(ny):
                    if jy:
                        held[1, jz] = move_y(held[0, jz], 1)
                    expert_rows(jy, jz, [held[jy, jz]], [move_c(held[jy, jz], 1)])
        hidden = []
        for jc in range(nc):
            parts = []
            for jy in range(ny):
                for jz in z_order:
                    value = blocks[jy, jz][jc * rows:(jc + 1) * rows]
                    parts += in_order(value[:rows // 2], value[rows // 2:]) if (jy, jz) in halved else [value]
            hidden.append(jnp.concatenate(parts, axis=0))

        orders = [[("x", d) for d in steps_of(nx)] + [("y", d) for d in steps_of(ny)],
                  [("y", d) for d in steps_of(ny)] + [("x", d) for d in steps_of(nx)]]
        z_steps = steps_of(nz)
        state = {}

        def product(i, which, jc, far=None):
            if (i, which) not in weights:
                weights[i, which] = chunk_weights(i, which)
            w, h = weights[i, which], hidden[jc]
            if far is not None:
                w, h = (pick(w, "x", far), h) if orders[which][0][0] == "x" else (w, pick(h, "y", far))
            return jnp.dot(h, w, preferred_element_type=jnp.float32)

        def tied(value, *keys):
            if keys:
                value, *got = after(value, *[state[key] for key in keys])
                state.update(zip(keys, got))
            return value

        def begin(i, keys=((), ())):
            if i == 0:
                got = {(which, far): move_c(product(i, which, 1, far).astype(jnp.bfloat16), 1)
                       for far in (1, 0) for which in (0, 1)}
            else:
                got = {}
                for which in (0, 1):
                    whole = move_c(product(i, which, 1).astype(jnp.bfloat16), 1)
                    for far in (1, 0):
                        got[which, far] = pick(whole, orders[which][0][0], far)
            for far in (1, 0):
                for which in (0, 1):
                    value = product(i, which, 0, far) + got[which, far].astype(jnp.float32)
                    state[i, which, far] = value.astype(jnp.bfloat16)
            if i + 1 < len(WIDTHS):
                hidden[0], hidden[1], state[i, 0, 1], state[i, 1, 1] = after(
                    hidden[0], hidden[1], state[i, 0, 1], state[i, 1, 1])
            for which in (0, 1):
                axis, d = orders[which][0]
                state[i, which] = moves[axis](tied(state[i, which, 1], *keys[which]), d)

        def turn(i, step, keys=((), ())):
            for which in (0, 1):
                if step < len(orders[which]):
                    axis, d = orders[which][step]
                    value = (state[i, which, 0], state[i, which])
                    far, state[i, which, 0] = half(value, axis, 1), half(value, axis, 0)
                    state[i, which] = moves[axis](tied(far, *keys[which]), d)

        def turn_z(i, k, *keys):
            if k == 0:
                values = [(state[i, which, 0], state[i, which]) for which in (0, 1)]
                near, far = [jnp.concatenate([half(v, "z", h) for v in values], axis=1) for h in (0, 1)]
            else:
                value = (state[i, "near"], state[i, "z"])
                if k == len(z_steps):
                    return add(*value)
                near, far = [half(value, "z", h) for h in (0, 1)]
            state[i, "near"], state[i, "z"] = near, move_z(tied(far, *keys), z_steps[k])

        if (nx, ny, nz) == (2, 2, 4):
            begin(0)
            turn(0, 1, (((0, 1),), ((0, 0, 0),)))
            begin(1, (((0, 1),), ((0, 0),)))
            turn_z(0, 0)
            turn(1, 1, (((1, 1), (0, "z")), ((1, 0, 0),)))
            turn_z(0, 1)
            begin(2, (((1, 1),), ((1, 0),)))
            turn_z(1, 0)
            turn(2, 1, (((2, 1), (0, "z")), ((2, 0, 0),)))
            turn_z(2, 0, (1, "z"))
            turn_z(1, 1)
            turn_z(2, 1)
        else:
            for i in range(len(WIDTHS)):
                begin(i)
                for step in range(1, len(orders[0])):
                    turn(i, step)
                for k in range(len(z_steps)):
                    turn_z(i, k)
        out = [turn_z(i, len(z_steps)) for i in range(len(WIDTHS))]
        return jnp.concatenate(out, axis=1)

    return shards


def solution(mesh):
    in_specs = (
        P(("groups", "expert"), None),
        P(("groups", "expert"), None),
        P(("groups", "expert"), None),
        P("expert", None, "tensor"),
        P("expert", None, "tensor"),
        P("expert", "tensor", None),
    )
    out_specs = P(("groups", "expert"), "tensor")
    return jax.shard_map(make(mesh), mesh=mesh, in_specs=in_specs, out_specs=out_specs, check_vma=False)
```

```python
import jax
import jax.numpy as jnp
from jax import lax
from jax.sharding import PartitionSpec as P

WIDTHS = (512, 384, 128)


def after(*values):
    return lax.optimization_barrier(values)


def add(a, b):
    return (a.astype(jnp.float32) + b.astype(jnp.float32)).astype(jnp.bfloat16)


def offsets(n):
    out, d = [0], n // 2
    while d:
        out, d = out + [o ^ d for o in out], d // 2
    return out


def steps_of(n):
    return [1 << i for i in range(n.bit_length() - 1)]


def pick(value, axis, which):
    dim = 1 if axis == "x" else 0
    size = value.shape[dim] // 2
    return lax.slice_in_dim(value, which * size, (which + 1) * size, axis=dim)


def half(value, axis, which):
    return add(*[pick(v, axis, which) for v in value])


def make(mesh):
    experts, nx = mesh.shape["expert"], mesh.shape["tensor"]
    nc = 2
    ny = 2 if experts // nc == 8 else 1
    nz = experts // (nc * ny)

    def index(z, y, c):
        return (z * ny + y) * nc + c

    places = [(z, y, c) for z in range(nz) for y in range(ny) for c in range(nc)]

    def move_z(a, d):
        return lax.ppermute(a, "expert", [(index(z, y, c), index(z ^ d, y, c)) for z, y, c in places])

    def move_y(a, d):
        return lax.ppermute(a, "expert", [(index(z, y, c), index(z, y ^ d, c)) for z, y, c in places])

    def move_c(a, d):
        return lax.ppermute(a, "expert", [(index(z, y, c), index(z, y, c ^ d)) for z, y, c in places])

    def move_x(a, d):
        return lax.ppermute(a, "tensor", [(i, i ^ d) for i in range(nx)])

    moves = {"x": move_x, "y": move_y, "z": move_z}

    def shards(tokens, expert_ids, route_weights, gate_w, up_w, down_w):
        rows, width = tokens.shape
        local_experts = gate_w.shape[0]
        experts_all = local_experts * experts
        me = lax.axis_index("expert")
        x = lax.axis_index("tensor")
        z_order = offsets(nz)
        chosen = expert_ids[None, :, :] == jnp.arange(experts_all, dtype=jnp.int32)[:, None, None]
        table = jnp.sum(jnp.where(chosen, route_weights[None], 0.0), axis=2)
        table = lax.all_to_all(table, "expert", split_axis=0, concat_axis=0, tiled=True)
        down = down_w.reshape(-1, width)
        share = width // nx
        bounds = [0]
        for w in WIDTHS:
            for _ in range(2):
                bounds.append(bounds[-1] + w * share // (2 * sum(WIDTHS)))
        blocks, weights = {}, {}

        def chunk_weights(i, which):
            first, last = bounds[2 * i + which:2 * i + which + 2]
            return jnp.concatenate([
                lax.dynamic_slice_in_dim(down, (x ^ jx) * share + first, last - first, axis=1) for jx in offsets(nx)], axis=1)

        def expert_values(near, far):
            pair = jnp.concatenate(near + far, axis=0)
            values = []
            for e in range(local_experts):
                gate = jnp.dot(pair, gate_w[e], preferred_element_type=jnp.float32)
                up_part = jnp.dot(pair, up_w[e], preferred_element_type=jnp.float32)
                values.append(jax.nn.silu(gate) * up_part)
            return values

        def weighted(jy, jz, values):
            for e in range(local_experts):
                scale = []
                for jc in range(nc):
                    row = lax.dynamic_slice(
                        table, ((me ^ index(jz, jy, jc)) * local_experts + e, 0), (1, rows)).reshape(rows)
                    if (jy, jz) in halved:
                        row = jnp.concatenate(in_order(row[:rows // 2], row[rows // 2:]))
                    scale.append(row)
                values[e] = (values[e] * jnp.concatenate(scale)[:, None]).astype(jnp.bfloat16)
            blocks[jy, jz] = jnp.concatenate(values, axis=1) if local_experts > 1 else values[0]
            return blocks[jy, jz]

        def expert_rows(jy, jz, near, far):
            return weighted(jy, jz, expert_values(near, far))

        def joined(a, b):
            return jnp.concatenate([a, b], axis=0)

        def in_order(a, b):
            return jnp.where(low, a, b), jnp.where(low, b, a)

        low = jnp.equal(x, 0)
        halved = [(0, 1), (1, 1), (0, 2), (1, 2), (0, 3), (1, 3)] if (nx, ny, nz) == (2, 2, 4) else []
        if (nx, ny, nz) == (2, 2, 4):
            m, r = [lax.dynamic_slice_in_dim(tokens, (x ^ i) * (rows // 2), rows // 2, axis=0) for i in (0, 1)]
            y0, z1m, z2m, c00 = move_y(tokens, 1), move_z(m, 1), move_z(m, 2), move_c(tokens, 1)
            c00, down = after(c00, down)
            weights.update({(0, which): chunk_weights(0, which) for which in (0, 1)})
            v00 = expert_values([tokens], [c00])
            y0, z1m, z2m, v00, r, table, weights[0, 0], weights[0, 1] = after(
                y0, z1m, z2m, v00, r, table, weights[0, 0], weights[0, 1])
            y1m, x0r, z3m, z2r, c10 = move_y(z1m, 1), move_x(z1m, 1), move_z(z2m, 1), move_z(r, 2), move_c(y0, 1)
            h00 = weighted(0, 0, v00)
            y1m, x0r, c10, h00, z1m, z2m = after(y1m, x0r, c10, h00, z1m, z2m)
            b01 = joined(z1m, x0r)
            y2m, x1r, c01 = move_y(z2m, 1), move_x(y1m, 1), move_c(b01, 1)
            h10 = expert_rows(1, 0, [y0], [c10])
            y2m, x1r, c01, z3m, z2r, h10, y1m, z2m = after(y2m, x1r, c01, z3m, z2r, h10, y1m, z2m)
            b11, b02 = joined(y1m, x1r), joined(z2m, z2r)
            y3m, x2r, z3r, c11, c02 = move_y(z3m, 1), move_x(y2m, 1), move_z(z2r, 1), move_c(b11, 1), move_c(b02, 1)
            h01 = expert_rows(0, 1, [b01], [c01])
            y3m, x2r, z3r, c11, c02, h01, y2m, z3m = after(y3m, x2r, z3r, c11, c02, h01, y2m, z3m)
            b12, b03 = joined(y2m, x2r), joined(z3m, z3r)
            x3r, c12, c03, c13m = move_x(y3m, 1), move_c(b12, 1), move_c(b03, 1), move_c(y3m, 1)
            h11 = expert_rows(1, 1, [b11], [c11])
            x3r, c12, c03, c13m, h11 = after(x3r, c12, c03, c13m, h11)
            c13r = move_c(x3r, 1)
            expert_rows(0, 2, [b02], [c02])
            expert_rows(1, 2, [b12], [c12])
            expert_rows(0, 3, [b03], [c03])
            expert_rows(1, 3, [y3m, x3r], [c13m, c13r])
            for place, h in (((0, 0), h00), ((1, 0), h10), ((0, 1), h01), ((1, 1), h11)):
                blocks[place] = h
        else:
            held = {(0, 0): tokens}
            for d in reversed(steps_of(nz)):
                for jz in sorted((key[1] for key in held), reverse=True):
                    held[0, jz ^ d] = move_z(held[0, jz], d)
            for jz in z_order:
                for jy in range(ny):
                    if jy:
                        held[1, jz] = move_y(held[0, jz], 1)
                    expert_rows(jy, jz, [held[jy, jz]], [move_c(held[jy, jz], 1)])
        hidden = []
        for jc in range(nc):
            parts = []
            for jy in range(ny):
                for jz in z_order:
                    value = blocks[jy, jz][jc * rows:(jc + 1) * rows]
                    parts += in_order(value[:rows // 2], value[rows // 2:]) if (jy, jz) in halved else [value]
            hidden.append(jnp.concatenate(parts, axis=0))

        orders = [[("x", d) for d in steps_of(nx)] + [("y", d) for d in steps_of(ny)],
                  [("y", d) for d in steps_of(ny)] + [("x", d) for d in steps_of(nx)]]
        z_steps = steps_of(nz)
        state = {}

        def product(i, which, jc, far=None):
            if (i, which) not in weights:
                weights[i, which] = chunk_weights(i, which)
            w, h = weights[i, which], hidden[jc]
            if far is not None:
                w, h = (pick(w, "x", far), h) if orders[which][0][0] == "x" else (w, pick(h, "y", far))
            return jnp.dot(h, w, preferred_element_type=jnp.float32)

        def tied(value, *keys):
            if keys:
                value, *got = after(value, *[state[key] for key in keys])
                state.update(zip(keys, got))
            return value

        def begin(i, keys=((), ())):
            if i == 0:
                got = {(which, far): move_c(product(i, which, 1, far).astype(jnp.bfloat16), 1)
                       for far in (1, 0) for which in (0, 1)}
            else:
                got = {}
                for which in (0, 1):
                    whole = move_c(product(i, which, 1).astype(jnp.bfloat16), 1)
                    for far in (1, 0):
                        got[which, far] = pick(whole, orders[which][0][0], far)
            for far in (1, 0):
                for which in (0, 1):
                    value = product(i, which, 0, far) + got[which, far].astype(jnp.float32)
                    state[i, which, far] = value.astype(jnp.bfloat16)
            if i + 1 < len(WIDTHS):
                hidden[0], hidden[1], state[i, 0, 1], state[i, 1, 1] = after(
                    hidden[0], hidden[1], state[i, 0, 1], state[i, 1, 1])
            for which in (0, 1):
                axis, d = orders[which][0]
                state[i, which] = moves[axis](tied(state[i, which, 1], *keys[which]), d)

        def turn(i, step, keys=((), ())):
            for which in (0, 1):
                if step < len(orders[which]):
                    axis, d = orders[which][step]
                    value = (state[i, which, 0], state[i, which])
                    far, state[i, which, 0] = half(value, axis, 1), half(value, axis, 0)
                    state[i, which] = moves[axis](tied(far, *keys[which]), d)

        def turn_z(i, k, *keys):
            if k == 0:
                values = [(state[i, which, 0], state[i, which]) for which in (0, 1)]
                near, far = [jnp.concatenate([half(v, "z", h) for v in values], axis=1) for h in (0, 1)]
            else:
                value = (state[i, "near"], state[i, "z"])
                if k == len(z_steps):
                    return add(*value)
                near, far = [half(value, "z", h) for h in (0, 1)]
            state[i, "near"], state[i, "z"] = near, move_z(tied(far, *keys), z_steps[k])

        if (nx, ny, nz) == (2, 2, 4):
            begin(0)
            turn(0, 1, (((0, 1),), ((0, 0, 0),)))
            begin(1, (((0, 1),), ((0, 0),)))
            turn_z(0, 0)
            turn(1, 1, (((1, 1), (0, "z")), ((1, 0, 0),)))
            turn_z(0, 1)
            begin(2, (((1, 1),), ((1, 0),)))
            turn_z(1, 0)
            turn(2, 1, (((2, 1), (0, "z")), ((2, 0, 0),)))
            turn_z(2, 0, (1, "z"))
            turn_z(1, 1)
            turn_z(2, 1)
        else:
            for i in range(len(WIDTHS)):
                begin(i)
                for step in range(1, len(orders[0])):
                    turn(i, step)
                for k in range(len(z_steps)):
                    turn_z(i, k)
        out = [turn_z(i, len(z_steps)) for i in range(len(WIDTHS))]
        return jnp.concatenate(out, axis=1)

    return shards


def solution(mesh):
    in_specs = (
        P(("groups", "expert"), None),
        P(("groups", "expert"), None),
        P(("groups", "expert"), None),
        P("expert", None, "tensor"),
        P("expert", None, "tensor"),
        P("expert", "tensor", None),
    )
    out_specs = P(("groups", "expert"), "tensor")
    return jax.shard_map(make(mesh), mesh=mesh, in_specs=in_specs, out_specs=out_specs, check_vma=False)
```

```python
import jax
import jax.numpy as jnp
from jax import lax
from jax.sharding import PartitionSpec as P

WIDTHS = (512, 384, 128)


def after(*values):
    return lax.optimization_barrier(values)


def add(a, b):
    return (a.astype(jnp.float32) + b.astype(jnp.float32)).astype(jnp.bfloat16)


def offsets(n):
    out, d = [0], n // 2
    while d:
        out, d = out + [o ^ d for o in out], d // 2
    return out


def steps_of(n):
    return [1 << i for i in range(n.bit_length() - 1)]


def pick(value, axis, which):
    dim = 1 if axis == "x" else 0
    size = value.shape[dim] // 2
    return lax.slice_in_dim(value, which * size, (which + 1) * size, axis=dim)


def half(value, axis, which):
    return add(*[pick(v, axis, which) for v in value])


def make(mesh):
    experts, nx = mesh.shape["expert"], mesh.shape["tensor"]
    nc = 2
    ny = 2 if experts // nc == 8 else 1
    nz = experts // (nc * ny)

    def index(z, y, c):
        return (z * ny + y) * nc + c

    places = [(z, y, c) for z in range(nz) for y in range(ny) for c in range(nc)]

    def move_z(a, d):
        return lax.ppermute(a, "expert", [(index(z, y, c), index(z ^ d, y, c)) for z, y, c in places])

    def move_y(a, d):
        return lax.ppermute(a, "expert", [(index(z, y, c), index(z, y ^ d, c)) for z, y, c in places])

    def move_c(a, d):
        return lax.ppermute(a, "expert", [(index(z, y, c), index(z, y, c ^ d)) for z, y, c in places])

    def move_x(a, d):
        return lax.ppermute(a, "tensor", [(i, i ^ d) for i in range(nx)])

    moves = {"x": move_x, "y": move_y, "z": move_z}

    def shards(tokens, expert_ids, route_weights, gate_w, up_w, down_w):
        rows, width = tokens.shape
        local_experts = gate_w.shape[0]
        experts_all = local_experts * experts
        me = lax.axis_index("expert")
        x = lax.axis_index("tensor")
        z_order = offsets(nz)
        chosen = expert_ids[None, :, :] == jnp.arange(experts_all, dtype=jnp.int32)[:, None, None]
        table = jnp.sum(jnp.where(chosen, route_weights[None], 0.0), axis=2)
        table = lax.all_to_all(table, "expert", split_axis=0, concat_axis=0, tiled=True)
        down = down_w.reshape(-1, width)
        share = width // nx
        bounds = [0]
        for w in WIDTHS:
            for _ in range(2):
                bounds.append(bounds[-1] + w * share // (2 * sum(WIDTHS)))
        blocks, weights = {}, {}

        def chunk_weights(i, which):
            first, last = bounds[2 * i + which:2 * i + which + 2]
            return jnp.concatenate([
                lax.dynamic_slice_in_dim(down, (x ^ jx) * share + first, last - first, axis=1) for jx in offsets(nx)], axis=1)

        def gate_values(near, far):
            pair = jnp.concatenate(near + far, axis=0)
            return pair, [jnp.dot(pair, w, preferred_element_type=jnp.float32) for w in gate_w]

        def expert_values(pair, gates):
            return [jax.nn.silu(gate) * jnp.dot(pair, w, preferred_element_type=jnp.float32)
                    for gate, w in zip(gates, up_w)]

        def weighted(jy, jz, values):
            for e in range(local_experts):
                scale = []
                for jc in range(nc):
                    row = lax.dynamic_slice(
                        table, ((me ^ index(jz, jy, jc)) * local_experts + e, 0), (1, rows)).reshape(rows)
                    if (jy, jz) in halved:
                        row = jnp.concatenate(in_order(row[:rows // 2], row[rows // 2:]))
                    scale.append(row)
                values[e] = (values[e] * jnp.concatenate(scale)[:, None]).astype(jnp.bfloat16)
            blocks[jy, jz] = jnp.concatenate(values, axis=1) if local_experts > 1 else values[0]
            return blocks[jy, jz]

        def expert_rows(jy, jz, near, far):
            return weighted(jy, jz, expert_values(*gate_values(near, far)))

        def joined(a, b):
            return jnp.concatenate([a, b], axis=0)

        def in_order(a, b):
            return jnp.where(low, a, b), jnp.where(low, b, a)

        low = jnp.equal(x, 0)
        halved = [(0, 1), (1, 1), (0, 2), (1, 2), (0, 3), (1, 3)] if (nx, ny, nz) == (2, 2, 4) else []
        if (nx, ny, nz) == (2, 2, 4):
            m, r = [lax.dynamic_slice_in_dim(tokens, (x ^ i) * (rows // 2), rows // 2, axis=0) for i in (0, 1)]
            y0, z1m, z2m, c00 = move_y(tokens, 1), move_z(m, 1), move_z(m, 2), move_c(tokens, 1)
            c00, down = after(c00, down)
            weights.update({(0, which): chunk_weights(0, which) for which in (0, 1)})
            v00 = expert_values(*gate_values([tokens], [c00]))
            y0, z1m, z2m, v00, r, table, weights[0, 0], weights[0, 1] = after(
                y0, z1m, z2m, v00, r, table, weights[0, 0], weights[0, 1])
            y1m, x0r, z3m, z2r, c10 = move_y(z1m, 1), move_x(z1m, 1), move_z(z2m, 1), move_z(r, 2), move_c(y0, 1)
            h00 = weighted(0, 0, v00)
            g10 = gate_values([y0], [c10])
            y1m, x0r, h00, g10, z1m, z2m = after(y1m, x0r, h00, g10, z1m, z2m)
            b01 = joined(z1m, x0r)
            y2m, x1r, c01 = move_y(z2m, 1), move_x(y1m, 1), move_c(b01, 1)
            h10 = weighted(1, 0, expert_values(*g10))
            g01 = gate_values([b01], [c01])
            y2m, x1r, z3m, z2r, h10, g01, y1m, z2m = after(y2m, x1r, z3m, z2r, h10, g01, y1m, z2m)
            b11, b02 = joined(y1m, x1r), joined(z2m, z2r)
            y3m, x2r, z3r, c11, c02 = move_y(z3m, 1), move_x(y2m, 1), move_z(z2r, 1), move_c(b11, 1), move_c(b02, 1)
            h01 = weighted(0, 1, expert_values(*g01))
            g11 = gate_values([b11], [c11])
            y3m, x2r, z3r, c02, h01, g11, y2m, z3m = after(y3m, x2r, z3r, c02, h01, g11, y2m, z3m)
            b12, b03 = joined(y2m, x2r), joined(z3m, z3r)
            x3r, c12, c03, c13m = move_x(y3m, 1), move_c(b12, 1), move_c(b03, 1), move_c(y3m, 1)
            h11 = weighted(1, 1, expert_values(*g11))
            x3r, c12, c03, c13m, h11 = after(x3r, c12, c03, c13m, h11)
            c13r = move_c(x3r, 1)
            expert_rows(0, 2, [b02], [c02])
            expert_rows(1, 2, [b12], [c12])
            expert_rows(0, 3, [b03], [c03])
            expert_rows(1, 3, [y3m, x3r], [c13m, c13r])
            for place, h in (((0, 0), h00), ((1, 0), h10), ((0, 1), h01), ((1, 1), h11)):
                blocks[place] = h
        else:
            held = {(0, 0): tokens}
            for d in reversed(steps_of(nz)):
                for jz in sorted((key[1] for key in held), reverse=True):
                    held[0, jz ^ d] = move_z(held[0, jz], d)
            for jz in z_order:
                for jy in range(ny):
                    if jy:
                        held[1, jz] = move_y(held[0, jz], 1)
                    expert_rows(jy, jz, [held[jy, jz]], [move_c(held[jy, jz], 1)])
        hidden = []
        for jc in range(nc):
            parts = []
            for jy in range(ny):
                for jz in z_order:
                    value = blocks[jy, jz][jc * rows:(jc + 1) * rows]
                    parts += in_order(value[:rows // 2], value[rows // 2:]) if (jy, jz) in halved else [value]
            hidden.append(jnp.concatenate(parts, axis=0))

        orders = [[("x", d) for d in steps_of(nx)] + [("y", d) for d in steps_of(ny)],
                  [("y", d) for d in steps_of(ny)] + [("x", d) for d in steps_of(nx)]]
        z_steps = steps_of(nz)
        state = {}

        def product(i, which, jc, far=None):
            if (i, which) not in weights:
                weights[i, which] = chunk_weights(i, which)
            w, h = weights[i, which], hidden[jc]
            if far is not None:
                w, h = (pick(w, "x", far), h) if orders[which][0][0] == "x" else (w, pick(h, "y", far))
            return jnp.dot(h, w, preferred_element_type=jnp.float32)

        def tied(value, *keys):
            if keys:
                value, *got = after(value, *[state[key] for key in keys])
                state.update(zip(keys, got))
            return value

        def begin(i, keys=((), ())):
            if i == 0:
                got = {(which, far): move_c(product(i, which, 1, far).astype(jnp.bfloat16), 1)
                       for far in (1, 0) for which in (0, 1)}
            else:
                got = {}
                for which in (0, 1):
                    whole = move_c(product(i, which, 1).astype(jnp.bfloat16), 1)
                    for far in (1, 0):
                        got[which, far] = pick(whole, orders[which][0][0], far)
            for far in (1, 0):
                for which in (0, 1):
                    value = product(i, which, 0, far) + got[which, far].astype(jnp.float32)
                    state[i, which, far] = value.astype(jnp.bfloat16)
            if i + 1 < len(WIDTHS):
                hidden[0], hidden[1], state[i, 0, 1], state[i, 1, 1] = after(
                    hidden[0], hidden[1], state[i, 0, 1], state[i, 1, 1])
            for which in (0, 1):
                axis, d = orders[which][0]
                state[i, which] = moves[axis](tied(state[i, which, 1], *keys[which]), d)

        def turn(i, step, keys=((), ())):
            for which in (0, 1):
                if step < len(orders[which]):
                    axis, d = orders[which][step]
                    value = (state[i, which, 0], state[i, which])
                    far, state[i, which, 0] = half(value, axis, 1), half(value, axis, 0)
                    state[i, which] = moves[axis](tied(far, *keys[which]), d)

        def turn_z(i, k, *keys):
            if k == 0:
                values = [(state[i, which, 0], state[i, which]) for which in (0, 1)]
                near, far = [jnp.concatenate([half(v, "z", h) for v in values], axis=1) for h in (0, 1)]
            else:
                value = (state[i, "near"], state[i, "z"])
                if k == len(z_steps):
                    return add(*value)
                near, far = [half(value, "z", h) for h in (0, 1)]
            state[i, "near"], state[i, "z"] = near, move_z(tied(far, *keys), z_steps[k])

        if (nx, ny, nz) == (2, 2, 4):
            begin(0)
            turn(0, 1, (((0, 1),), ((0, 0, 0),)))
            begin(1, (((0, 1),), ((0, 0),)))
            turn_z(0, 0)
            turn(1, 1, (((1, 1), (0, "z")), ((1, 0, 0),)))
            turn_z(0, 1)
            begin(2, (((1, 1),), ((1, 0),)))
            turn_z(1, 0)
            turn(2, 1, (((2, 1), (0, "z")), ((2, 0, 0),)))
            turn_z(2, 0, (1, "z"))
            turn_z(1, 1)
            turn_z(2, 1)
        else:
            for i in range(len(WIDTHS)):
                begin(i)
                for step in range(1, len(orders[0])):
                    turn(i, step)
                for k in range(len(z_steps)):
                    turn_z(i, k)
        out = [turn_z(i, len(z_steps)) for i in range(len(WIDTHS))]
        return jnp.concatenate(out, axis=1)

    return shards


def solution(mesh):
    in_specs = (
        P(("groups", "expert"), None),
        P(("groups", "expert"), None),
        P(("groups", "expert"), None),
        P("expert", None, "tensor"),
        P("expert", None, "tensor"),
        P("expert", "tensor", None),
    )
    out_specs = P(("groups", "expert"), "tensor")
    return jax.shard_map(make(mesh), mesh=mesh, in_specs=in_specs, out_specs=out_specs, check_vma=False)
```

```python
import jax
import jax.numpy as jnp
from jax import lax
from jax.sharding import PartitionSpec as P

WIDTHS = (512, 256, 128)


def after(*values):
    return lax.optimization_barrier(values)


def add(a, b):
    return (a.astype(jnp.float32) + b.astype(jnp.float32)).astype(jnp.bfloat16)


def offsets(n):
    out, d = [0], n // 2
    while d:
        out, d = out + [o ^ d for o in out], d // 2
    return out


def steps_of(n):
    return [1 << i for i in range(n.bit_length() - 1)]


def pick(value, axis, which):
    dim = 1 if axis == "x" else 0
    size = value.shape[dim] // 2
    return lax.slice_in_dim(value, which * size, (which + 1) * size, axis=dim)


def half(value, axis, which):
    return add(*[pick(v, axis, which) for v in value])


def make(mesh):
    experts, nx = mesh.shape["expert"], mesh.shape["tensor"]
    nc = 2
    ny = 2 if experts // nc == 8 else 1
    nz = experts // (nc * ny)

    def index(z, y, c):
        return (z * ny + y) * nc + c

    places = [(z, y, c) for z in range(nz) for y in range(ny) for c in range(nc)]

    def move_z(a, d):
        return lax.ppermute(a, "expert", [(index(z, y, c), index(z ^ d, y, c)) for z, y, c in places])

    def move_y(a, d):
        return lax.ppermute(a, "expert", [(index(z, y, c), index(z, y ^ d, c)) for z, y, c in places])

    def move_c(a, d):
        return lax.ppermute(a, "expert", [(index(z, y, c), index(z, y, c ^ d)) for z, y, c in places])

    def move_x(a, d):
        return lax.ppermute(a, "tensor", [(i, i ^ d) for i in range(nx)])

    moves = {"x": move_x, "y": move_y, "z": move_z}

    def shards(tokens, expert_ids, route_weights, gate_w, up_w, down_w):
        rows, width = tokens.shape
        local_experts = gate_w.shape[0]
        experts_all = local_experts * experts
        me = lax.axis_index("expert")
        x = lax.axis_index("tensor")
        z_order = offsets(nz)
        chosen = expert_ids[None, :, :] == jnp.arange(experts_all, dtype=jnp.int32)[:, None, None]
        table = jnp.sum(jnp.where(chosen, route_weights[None], 0.0), axis=2)
        table = lax.all_to_all(table, "expert", split_axis=0, concat_axis=0, tiled=True)
        down = down_w.reshape(-1, width)
        share = width // nx
        bounds = [0]
        for w in WIDTHS:
            for _ in range(2):
                bounds.append(bounds[-1] + w * share // 2048)
        bounds.append(share)
        blocks, weights = {}, {}

        def chunk_weights(i, which):
            first, last = bounds[2 * i + which:2 * i + which + 2]
            return jnp.concatenate([
                lax.dynamic_slice_in_dim(down, (x ^ jx) * share + first, last - first, axis=1) for jx in offsets(nx)], axis=1)

        def gate_values(near, far):
            pair = jnp.concatenate(near + far, axis=0)
            return pair, [jnp.dot(pair, w, preferred_element_type=jnp.float32) for w in gate_w]

        def expert_values(pair, gates):
            return [jax.nn.silu(gate) * jnp.dot(pair, w, preferred_element_type=jnp.float32)
                    for gate, w in zip(gates, up_w)]

        def weighted(jy, jz, values):
            for e in range(local_experts):
                scale = []
                for jc in range(nc):
                    row = lax.dynamic_slice(
                        table, ((me ^ index(jz, jy, jc)) * local_experts + e, 0), (1, rows)).reshape(rows)
                    if (jy, jz) in halved:
                        row = jnp.concatenate(in_order(row[:rows // 2], row[rows // 2:]))
                    scale.append(row)
                values[e] = (values[e] * jnp.concatenate(scale)[:, None]).astype(jnp.bfloat16)
            blocks[jy, jz] = jnp.concatenate(values, axis=1) if local_experts > 1 else values[0]
            return blocks[jy, jz]

        def expert_rows(jy, jz, near, far):
            return weighted(jy, jz, expert_values(*gate_values(near, far)))

        def joined(a, b):
            return jnp.concatenate([a, b], axis=0)

        def in_order(a, b):
            return jnp.where(low, a, b), jnp.where(low, b, a)

        low = jnp.equal(x, 0)
        halved = [(0, 1), (1, 1), (0, 2), (1, 2), (0, 3), (1, 3)] if (nx, ny, nz) == (2, 2, 4) else []
        if (nx, ny, nz) == (2, 2, 4):
            m = lax.dynamic_slice_in_dim(tokens, x * (rows // 2), rows // 2, axis=0)
            y0, z1m, z2m, c00 = move_y(tokens, 1), move_z(m, 1), move_z(m, 2), move_c(tokens, 1)
            c00, down, later = after(c00, down, tokens)
            r = lax.dynamic_slice_in_dim(later, (1 - x) * (rows // 2), rows // 2, axis=0)
            weights.update({(0, which): chunk_weights(0, which) for which in (0, 1)})
            v00 = expert_values(*gate_values([tokens], [c00]))
            y0, z1m, z2m, v00, r, table, weights[0, 0], weights[0, 1] = after(
                y0, z1m, z2m, v00, r, table, weights[0, 0], weights[0, 1])
            y1m, x0r, z3m, z2r, c10 = move_y(z1m, 1), move_x(z1m, 1), move_z(z2m, 1), move_z(r, 2), move_c(y0, 1)
            h00 = weighted(0, 0, v00)
            g10 = gate_values([y0], [c10])
            y1m, x0r, h00, g10, z1m, z2m = after(y1m, x0r, h00, g10, z1m, z2m)
            b01 = joined(z1m, x0r)
            y2m, x1r, c01 = move_y(z2m, 1), move_x(y1m, 1), move_c(b01, 1)
            h10 = weighted(1, 0, expert_values(*g10))
            g01 = gate_values([b01], [c01])
            y2m, x1r, z3m, z2r, h10, g01, y1m, z2m = after(y2m, x1r, z3m, z2r, h10, g01, y1m, z2m)
            b11, b02 = joined(y1m, x1r), joined(z2m, z2r)
            y3m, x2r, z3r, c11, c02 = move_y(z3m, 1), move_x(y2m, 1), move_z(z2r, 1), move_c(b11, 1), move_c(b02, 1)
            h01 = weighted(0, 1, expert_values(*g01))
            g11 = gate_values([b11], [c11])
            y3m, x2r, z3r, c02, h01, g11, y2m, z3m = after(y3m, x2r, z3r, c02, h01, g11, y2m, z3m)
            b12, b03 = joined(y2m, x2r), joined(z3m, z3r)
            x3r, c12, c03, c13m = move_x(y3m, 1), move_c(b12, 1), move_c(b03, 1), move_c(y3m, 1)
            h11 = weighted(1, 1, expert_values(*g11))
            x3r, c12, c03, c13m, h11 = after(x3r, c12, c03, c13m, h11)
            c13r = move_c(x3r, 1)
            expert_rows(0, 2, [b02], [c02])
            expert_rows(1, 2, [b12], [c12])
            expert_rows(0, 3, [b03], [c03])
            expert_rows(1, 3, [y3m, x3r], [c13m, c13r])
            for place, h in (((0, 0), h00), ((1, 0), h10), ((0, 1), h01), ((1, 1), h11)):
                blocks[place] = h
        else:
            held = {(0, 0): tokens}
            for d in reversed(steps_of(nz)):
                for jz in sorted((key[1] for key in held), reverse=True):
                    held[0, jz ^ d] = move_z(held[0, jz], d)
            for jz in z_order:
                for jy in range(ny):
                    if jy:
                        held[1, jz] = move_y(held[0, jz], 1)
                    expert_rows(jy, jz, [held[jy, jz]], [move_c(held[jy, jz], 1)])
        hidden = []
        for jc in range(nc):
            parts = []
            for jy in range(ny):
                for jz in z_order:
                    value = blocks[jy, jz][jc * rows:(jc + 1) * rows]
                    parts += in_order(value[:rows // 2], value[rows // 2:]) if (jy, jz) in halved else [value]
            hidden.append(jnp.concatenate(parts, axis=0))

        orders = [[("x", d) for d in steps_of(nx)] + [("y", d) for d in steps_of(ny)],
                  [("y", d) for d in steps_of(ny)] + [("x", d) for d in steps_of(nx)]]
        z_steps = steps_of(nz)
        state = {}

        def side_start():
            w = chunk_weights(len(WIDTHS), 0)
            got = move_c(jnp.dot(hidden[1], w, preferred_element_type=jnp.float32).astype(jnp.bfloat16), 1)
            value = jnp.dot(hidden[0], w, preferred_element_type=jnp.float32) + got.astype(jnp.float32)
            state["value"] = value.astype(jnp.bfloat16)

        def side(axis, d, *keys):
            value = state["value"]
            if axis == "z":
                value = value.reshape(ny, -1, value.shape[1])
                near, far = [v.reshape(-1, value.shape[2]) for v in jnp.split(value, 2, axis=1)]
            else:
                near, far = pick(value, axis, 0), pick(value, axis, 1)
            state["near"], state["side"] = near, moves[axis](tied(far, *keys), d)

        def side_sum():
            state["value"] = add(state["near"], state["side"])

        def product(i, which, jc, far=None):
            if (i, which) not in weights:
                weights[i, which] = chunk_weights(i, which)
            w, h = weights[i, which], hidden[jc]
            if far is not None:
                w, h = (pick(w, "x", far), h) if orders[which][0][0] == "x" else (w, pick(h, "y", far))
            return jnp.dot(h, w, preferred_element_type=jnp.float32)

        def tied(value, *keys):
            if keys:
                value, *got = after(value, *[state[key] for key in keys])
                state.update(zip(keys, got))
            return value

        def begin(i, keys=((), ())):
            if i == 0:
                got = {(which, far): move_c(product(i, which, 1, far).astype(jnp.bfloat16), 1)
                       for far in (1, 0) for which in (0, 1)}
            else:
                got = {}
                for which in (0, 1):
                    whole = move_c(product(i, which, 1).astype(jnp.bfloat16), 1)
                    for far in (1, 0):
                        got[which, far] = pick(whole, orders[which][0][0], far)
            for far in (1, 0):
                for which in (0, 1):
                    value = product(i, which, 0, far) + got[which, far].astype(jnp.float32)
                    state[i, which, far] = value.astype(jnp.bfloat16)
            if i + 1 < len(WIDTHS):
                hidden[0], hidden[1], state[i, 0, 1], state[i, 1, 1] = after(
                    hidden[0], hidden[1], state[i, 0, 1], state[i, 1, 1])
            for which in (0, 1):
                axis, d = orders[which][0]
                state[i, which] = moves[axis](tied(state[i, which, 1], *keys[which]), d)

        def turn(i, step, keys=((), ())):
            for which in (0, 1):
                if step < len(orders[which]):
                    axis, d = orders[which][step]
                    value = (state[i, which, 0], state[i, which])
                    far, state[i, which, 0] = half(value, axis, 1), half(value, axis, 0)
                    state[i, which] = moves[axis](tied(far, *keys[which]), d)

        def turn_z(i, k, *keys):
            if k == 0:
                values = [(state[i, which, 0], state[i, which]) for which in (0, 1)]
                near, far = [jnp.concatenate([half(v, "z", h) for v in values], axis=1) for h in (0, 1)]
            else:
                value = (state[i, "near"], state[i, "z"])
                if k == len(z_steps):
                    return add(*value)
                near, far = [half(value, "z", h) for h in (0, 1)]
            state[i, "near"], state[i, "z"] = near, move_z(tied(far, *keys), z_steps[k])

        if (nx, ny, nz) == (2, 2, 4):
            begin(0)
            side_start()
            side("z", 1)
            turn(0, 1, (((0, 1),), ((0, 0, 0),)))
            begin(1, (((0, 1), "side"), ((0, 0),)))
            side_sum()
            side("z", 2)
            turn_z(0, 0)
            turn(1, 1, (((1, 1), (0, "z"), "side"), ((1, 0, 0),)))
            side_sum()
            side("x", 1, (1, 1))
            turn_z(0, 1)
            begin(2, (("side",), ((1, 0),)))
            side_sum()
            side("y", 1, (2, 1))
            turn_z(1, 0)
            turn(2, 1, (((2, 1), (0, "z")), ((2, 0, 0),)))
            turn_z(2, 0, (1, "z"))
            turn_z(1, 1)
            turn_z(2, 1)
            side_sum()
        else:
            for i in range(len(WIDTHS)):
                begin(i)
                for step in range(1, len(orders[0])):
                    turn(i, step)
                for k in range(len(z_steps)):
                    turn_z(i, k)
            side_start()
            for axis, d in [("z", d) for d in z_steps] + orders[0]:
                side(axis, d)
                side_sum()
        out = [turn_z(i, len(z_steps)) for i in range(len(WIDTHS))] + [state["value"]]
        return jnp.concatenate(out, axis=1)

    return shards


def solution(mesh):
    in_specs = (
        P(("groups", "expert"), None),
        P(("groups", "expert"), None),
        P(("groups", "expert"), None),
        P("expert", None, "tensor"),
        P("expert", None, "tensor"),
        P("expert", "tensor", None),
    )
    out_specs = P(("groups", "expert"), "tensor")
    return jax.shard_map(make(mesh), mesh=mesh, in_specs=in_specs, out_specs=out_specs, check_vma=False)
```

```python
import jax
import jax.numpy as jnp
from jax import lax
from jax.sharding import PartitionSpec as P

WIDTHS = (512, 384, 128)


def after(*values):
    return lax.optimization_barrier(values)


def add(a, b):
    return (a.astype(jnp.float32) + b.astype(jnp.float32)).astype(jnp.bfloat16)


def offsets(n):
    out, d = [0], n // 2
    while d:
        out, d = out + [o ^ d for o in out], d // 2
    return out


def steps_of(n):
    return [1 << i for i in range(n.bit_length() - 1)]


def pick(value, axis, which):
    dim = 1 if axis == "x" else 0
    size = value.shape[dim] // 2
    return lax.slice_in_dim(value, which * size, (which + 1) * size, axis=dim)


def half(value, axis, which):
    return add(*[pick(v, axis, which) for v in value])


def make(mesh):
    experts, nx = mesh.shape["expert"], mesh.shape["tensor"]
    nc = 2
    ny = 2 if experts // nc == 8 else 1
    nz = experts // (nc * ny)

    def index(z, y, c):
        return (z * ny + y) * nc + c

    places = [(z, y, c) for z in range(nz) for y in range(ny) for c in range(nc)]

    def move_z(a, d):
        return lax.ppermute(a, "expert", [(index(z, y, c), index(z ^ d, y, c)) for z, y, c in places])

    def move_y(a, d):
        return lax.ppermute(a, "expert", [(index(z, y, c), index(z, y ^ d, c)) for z, y, c in places])

    def move_c(a, d):
        return lax.ppermute(a, "expert", [(index(z, y, c), index(z, y, c ^ d)) for z, y, c in places])

    def move_x(a, d):
        return lax.ppermute(a, "tensor", [(i, i ^ d) for i in range(nx)])

    moves = {"x": move_x, "y": move_y, "z": move_z}

    def shards(tokens, expert_ids, route_weights, gate_w, up_w, down_w):
        rows, width = tokens.shape
        local_experts = gate_w.shape[0]
        experts_all = local_experts * experts
        me = lax.axis_index("expert")
        x = lax.axis_index("tensor")
        z_order = offsets(nz)
        chosen = expert_ids[None, :, :] == jnp.arange(experts_all, dtype=jnp.int32)[:, None, None]
        table = jnp.sum(jnp.where(chosen, route_weights[None], 0.0), axis=2)
        table = lax.all_to_all(table, "expert", split_axis=0, concat_axis=0, tiled=True)
        down = down_w.reshape(-1, width)
        share = width // nx
        bounds = [0]
        for w in WIDTHS:
            for _ in range(2):
                bounds.append(bounds[-1] + w * share // (2 * sum(WIDTHS)))
        blocks, weights = {}, {}

        def chunk_weights(i, which):
            first, last = bounds[2 * i + which:2 * i + which + 2]
            return jnp.concatenate([
                lax.dynamic_slice_in_dim(down, (x ^ jx) * share + first, last - first, axis=1) for jx in offsets(nx)], axis=1)

        def gate_values(near, far):
            pair = jnp.concatenate(near + far, axis=0)
            return pair, [jnp.dot(pair, w, preferred_element_type=jnp.float32) for w in gate_w]

        def expert_values(pair, gates):
            return [jax.nn.silu(gate) * jnp.dot(pair, w, preferred_element_type=jnp.float32)
                    for gate, w in zip(gates, up_w)]

        def weighted(jy, jz, values):
            for e in range(local_experts):
                scale = []
                for jc in range(nc):
                    row = lax.dynamic_slice(
                        table, ((me ^ index(jz, jy, jc)) * local_experts + e, 0), (1, rows)).reshape(rows)
                    if (jy, jz) in halved:
                        row = jnp.concatenate(in_order(row[:rows // 2], row[rows // 2:]))
                    scale.append(row)
                values[e] = (values[e] * jnp.concatenate(scale)[:, None]).astype(jnp.bfloat16)
            blocks[jy, jz] = jnp.concatenate(values, axis=1) if local_experts > 1 else values[0]
            return blocks[jy, jz]

        def expert_rows(jy, jz, near, far):
            return weighted(jy, jz, expert_values(*gate_values(near, far)))

        def joined(a, b):
            return jnp.concatenate([a, b], axis=0)

        def in_order(a, b):
            return jnp.where(low, a, b), jnp.where(low, b, a)

        low = jnp.equal(x, 0)
        halved = [(0, 1), (1, 1), (0, 2), (1, 2), (0, 3), (1, 3)] if (nx, ny, nz) == (2, 2, 4) else []
        if (nx, ny, nz) == (2, 2, 4):
            m = lax.dynamic_slice_in_dim(tokens, x * (rows // 2), rows // 2, axis=0)
            y0, z1m, z2m, c00 = move_y(tokens, 1), move_z(m, 1), move_z(m, 2), move_c(tokens, 1)
            c00, down, later = after(c00, down, tokens)
            r = lax.dynamic_slice_in_dim(later, (1 - x) * (rows // 2), rows // 2, axis=0)
            weights.update({(0, which): chunk_weights(0, which) for which in (0, 1)})
            v00 = expert_values(*gate_values([tokens], [c00]))
            y0, z1m, z2m, v00, r, table, weights[0, 0], weights[0, 1] = after(
                y0, z1m, z2m, v00, r, table, weights[0, 0], weights[0, 1])
            y1m, x0r, z3m, z2r, c10 = move_y(z1m, 1), move_x(z1m, 1), move_z(z2m, 1), move_z(r, 2), move_c(y0, 1)
            h00 = weighted(0, 0, v00)
            g10 = gate_values([y0], [c10])
            y1m, x0r, h00, g10, z1m, z2m = after(y1m, x0r, h00, g10, z1m, z2m)
            b01 = joined(z1m, x0r)
            y2m, x1r, c01 = move_y(z2m, 1), move_x(y1m, 1), move_c(b01, 1)
            h10 = weighted(1, 0, expert_values(*g10))
            g01 = gate_values([b01], [c01])
            y2m, x1r, z3m, z2r, h10, g01, y1m, z2m = after(y2m, x1r, z3m, z2r, h10, g01, y1m, z2m)
            b11, b02 = joined(y1m, x1r), joined(z2m, z2r)
            y3m, x2r, z3r, c11, c02 = move_y(z3m, 1), move_x(y2m, 1), move_z(z2r, 1), move_c(b11, 1), move_c(b02, 1)
            h01 = weighted(0, 1, expert_values(*g01))
            g11 = gate_values([b11], [c11])
            y3m, x2r, z3r, c02, h01, g11, y2m, z3m = after(y3m, x2r, z3r, c02, h01, g11, y2m, z3m)
            b12, b03 = joined(y2m, x2r), joined(z3m, z3r)
            x3r, c12, c03, c13m = move_x(y3m, 1), move_c(b12, 1), move_c(b03, 1), move_c(y3m, 1)
            h11 = weighted(1, 1, expert_values(*g11))
            x3r, c12, c03, c13m, h11 = after(x3r, c12, c03, c13m, h11)
            c13r = move_c(x3r, 1)
            expert_rows(0, 2, [b02], [c02])
            expert_rows(1, 2, [b12], [c12])
            expert_rows(0, 3, [b03], [c03])
            expert_rows(1, 3, [y3m, x3r], [c13m, c13r])
            for place, h in (((0, 0), h00), ((1, 0), h10), ((0, 1), h01), ((1, 1), h11)):
                blocks[place] = h
        else:
            held = {(0, 0): tokens}
            for d in reversed(steps_of(nz)):
                for jz in sorted((key[1] for key in held), reverse=True):
                    held[0, jz ^ d] = move_z(held[0, jz], d)
            for jz in z_order:
                for jy in range(ny):
                    if jy:
                        held[1, jz] = move_y(held[0, jz], 1)
                    expert_rows(jy, jz, [held[jy, jz]], [move_c(held[jy, jz], 1)])
        hidden = []
        for jc in range(nc):
            parts = []
            for jy in range(ny):
                for jz in z_order:
                    value = blocks[jy, jz][jc * rows:(jc + 1) * rows]
                    parts += in_order(value[:rows // 2], value[rows // 2:]) if (jy, jz) in halved else [value]
            hidden.append(jnp.concatenate(parts, axis=0))

        orders = [[("x", d) for d in steps_of(nx)] + [("y", d) for d in steps_of(ny)],
                  [("y", d) for d in steps_of(ny)] + [("x", d) for d in steps_of(nx)]]
        z_steps = steps_of(nz)
        state = {}

        def product(i, which, jc, far=None):
            if (i, which) not in weights:
                weights[i, which] = chunk_weights(i, which)
            w, h = weights[i, which], hidden[jc]
            if far is not None:
                w, h = (pick(w, "x", far), h) if orders[which][0][0] == "x" else (w, pick(h, "y", far))
            return jnp.dot(h, w, preferred_element_type=jnp.float32)

        def tied(value, *keys):
            if keys:
                value, *got = after(value, *[state[key] for key in keys])
                state.update(zip(keys, got))
            return value

        def begin(i, keys=((), ())):
            if i == 0:
                got = {(which, far): move_c(product(i, which, 1, far).astype(jnp.bfloat16), 1)
                       for far in (1, 0) for which in (0, 1)}
            else:
                got = {}
                for which in (0, 1):
                    whole = move_c(product(i, which, 1).astype(jnp.bfloat16), 1)
                    for far in (1, 0):
                        got[which, far] = pick(whole, orders[which][0][0], far)
            for far in (1, 0):
                for which in (0, 1):
                    value = product(i, which, 0, far) + got[which, far].astype(jnp.float32)
                    state[i, which, far] = value.astype(jnp.bfloat16)
            if i + 1 < len(WIDTHS):
                hidden[0], hidden[1], state[i, 0, 1], state[i, 1, 1] = after(
                    hidden[0], hidden[1], state[i, 0, 1], state[i, 1, 1])
            for which in (0, 1):
                axis, d = orders[which][0]
                state[i, which] = moves[axis](tied(state[i, which, 1], *keys[which]), d)

        def turn(i, step, keys=((), ())):
            for which in (0, 1):
                if step < len(orders[which]):
                    axis, d = orders[which][step]
                    value = (state[i, which, 0], state[i, which])
                    far, state[i, which, 0] = half(value, axis, 1), half(value, axis, 0)
                    state[i, which] = moves[axis](tied(far, *keys[which]), d)

        def turn_z(i, k, *keys):
            if k == 0:
                values = [(state[i, which, 0], state[i, which]) for which in (0, 1)]
                near, far = [jnp.concatenate([half(v, "z", h) for v in values], axis=1) for h in (0, 1)]
            else:
                value = (state[i, "near"], state[i, "z"])
                if k == len(z_steps):
                    return add(*value)
                near, far = [half(value, "z", h) for h in (0, 1)]
            state[i, "near"], state[i, "z"] = near, move_z(tied(far, *keys), z_steps[k])

        if (nx, ny, nz) == (2, 2, 4):
            begin(0)
            turn(0, 1, (((0, 1),), ((0, 0, 0),)))
            begin(1, (((0, 1),), ((0, 0),)))
            turn_z(0, 0)
            turn(1, 1, (((1, 1), (0, "z")), ((1, 0, 0),)))
            turn_z(0, 1)
            begin(2, (((1, 1),), ((1, 0),)))
            turn_z(1, 0)
            turn(2, 1, (((2, 1), (0, "z")), ((2, 0, 0),)))
            turn_z(2, 0, (1, "z"))
            turn_z(1, 1)
            turn_z(2, 1)
        else:
            for i in range(len(WIDTHS)):
                begin(i)
                for step in range(1, len(orders[0])):
                    turn(i, step)
                for k in range(len(z_steps)):
                    turn_z(i, k)
        out = [turn_z(i, len(z_steps)) for i in range(len(WIDTHS))]
        return jnp.concatenate(out, axis=1)

    return shards


def solution(mesh):
    in_specs = (
        P(("groups", "expert"), None),
        P(("groups", "expert"), None),
        P(("groups", "expert"), None),
        P("expert", None, "tensor"),
        P("expert", None, "tensor"),
        P("expert", "tensor", None),
    )
    out_specs = P(("groups", "expert"), "tensor")
    return jax.shard_map(make(mesh), mesh=mesh, in_specs=in_specs, out_specs=out_specs, check_vma=False)
```

```python
import jax
import jax.numpy as jnp
from jax import lax
from jax.sharding import PartitionSpec as P

WIDTHS = (512, 384, 128)


def after(*values):
    return lax.optimization_barrier(values)


def add(a, b):
    return (a.astype(jnp.float32) + b.astype(jnp.float32)).astype(jnp.bfloat16)


def offsets(n):
    out, d = [0], n // 2
    while d:
        out, d = out + [o ^ d for o in out], d // 2
    return out


def steps_of(n):
    return [1 << i for i in range(n.bit_length() - 1)]


def pick(value, axis, which):
    dim = 1 if axis == "x" else 0
    size = value.shape[dim] // 2
    return lax.slice_in_dim(value, which * size, (which + 1) * size, axis=dim)


def half(value, axis, which):
    return add(*[pick(v, axis, which) for v in value])


def make(mesh):
    experts, nx = mesh.shape["expert"], mesh.shape["tensor"]
    nc = 2
    ny = 2 if experts // nc == 8 else 1
    nz = experts // (nc * ny)

    def index(z, y, c):
        return (z * ny + y) * nc + c

    places = [(z, y, c) for z in range(nz) for y in range(ny) for c in range(nc)]

    def move_z(a, d):
        return lax.ppermute(a, "expert", [(index(z, y, c), index(z ^ d, y, c)) for z, y, c in places])

    def move_y(a, d):
        return lax.ppermute(a, "expert", [(index(z, y, c), index(z, y ^ d, c)) for z, y, c in places])

    def move_c(a, d):
        return lax.ppermute(a, "expert", [(index(z, y, c), index(z, y, c ^ d)) for z, y, c in places])

    def move_x(a, d):
        return lax.ppermute(a, "tensor", [(i, i ^ d) for i in range(nx)])

    moves = {"x": move_x, "y": move_y, "z": move_z}

    def shards(tokens, expert_ids, route_weights, gate_w, up_w, down_w):
        rows, width = tokens.shape
        local_experts = gate_w.shape[0]
        experts_all = local_experts * experts
        me = lax.axis_index("expert")
        x = lax.axis_index("tensor")
        z_order = offsets(nz)
        chosen = expert_ids[None, :, :] == jnp.arange(experts_all, dtype=jnp.int32)[:, None, None]
        table = jnp.sum(jnp.where(chosen, route_weights[None], 0.0), axis=2)
        table = lax.all_to_all(table, "expert", split_axis=0, concat_axis=0, tiled=True)
        down = down_w.reshape(-1, width)
        share = width // nx
        bounds = [0]
        for w in WIDTHS:
            for _ in range(2):
                bounds.append(bounds[-1] + w * share // (2 * sum(WIDTHS)))
        blocks, weights = {}, {}

        def chunk_weights(i, which):
            first, last = bounds[2 * i + which:2 * i + which + 2]
            return jnp.concatenate([
                lax.dynamic_slice_in_dim(down, (x ^ jx) * share + first, last - first, axis=1) for jx in offsets(nx)], axis=1)

        def gate_values(near, far):
            return pair_gates(jnp.concatenate(near + far, axis=0))

        def pair_gates(pair):
            return pair, [jnp.dot(pair, w, preferred_element_type=jnp.float32) for w in gate_w]

        def expert_values(pair, gates):
            return [jax.nn.silu(gate) * jnp.dot(pair, w, preferred_element_type=jnp.float32)
                    for gate, w in zip(gates, up_w)]

        def weighted(jy, jz, values):
            for e in range(local_experts):
                scale = []
                for jc in range(nc):
                    row = lax.dynamic_slice(
                        table, ((me ^ index(jz, jy, jc)) * local_experts + e, 0), (1, rows)).reshape(rows)
                    if (jy, jz) in halved:
                        row = jnp.concatenate(in_order(row[:rows // 2], row[rows // 2:]))
                    scale.append(row)
                values[e] = (values[e] * jnp.concatenate(scale)[:, None]).astype(jnp.bfloat16)
            blocks[jy, jz] = jnp.concatenate(values, axis=1) if local_experts > 1 else values[0]
            return blocks[jy, jz]

        def expert_rows(jy, jz, near, far):
            return weighted(jy, jz, expert_values(*gate_values(near, far)))

        def joined(a, b):
            return jnp.concatenate([a, b], axis=0)

        def in_order(a, b):
            return jnp.where(low, a, b), jnp.where(low, b, a)

        low = jnp.equal(x, 0)
        halved = [(0, 1), (1, 1), (0, 2), (1, 2), (0, 3), (1, 3)] if (nx, ny, nz) == (2, 2, 4) else []
        if (nx, ny, nz) == (2, 2, 4):
            m = lax.dynamic_slice_in_dim(tokens, x * (rows // 2), rows // 2, axis=0)
            y0, z1m, z2m, c00 = move_y(tokens, 1), move_z(m, 1), move_z(m, 2), move_c(tokens, 1)
            c00, down, later = after(c00, down, tokens)
            r = lax.dynamic_slice_in_dim(later, (1 - x) * (rows // 2), rows // 2, axis=0)
            weights.update({(0, which): chunk_weights(0, which) for which in (0, 1)})
            v00 = expert_values(*gate_values([tokens], [c00]))
            p10 = jnp.concatenate([y0, jnp.zeros_like(y0)], axis=0)
            y0, p10, z1m, z2m, v00, r, table, weights[0, 0], weights[0, 1] = after(
                y0, p10, z1m, z2m, v00, r, table, weights[0, 0], weights[0, 1])
            y1m, x0r, z3m, z2r, c10 = move_y(z1m, 1), move_x(z1m, 1), move_z(z2m, 1), move_z(r, 2), move_c(y0, 1)
            h00 = weighted(0, 0, v00)
            g10 = pair_gates(lax.dynamic_update_slice_in_dim(p10, c10, rows, axis=0))
            y1m, x0r, h00, g10, z1m, z2m = after(y1m, x0r, h00, g10, z1m, z2m)
            b01 = joined(z1m, x0r)
            y2m, x1r, c01 = move_y(z2m, 1), move_x(y1m, 1), move_c(b01, 1)
            h10 = weighted(1, 0, expert_values(*g10))
            g01 = gate_values([b01], [c01])
            y2m, x1r, z3m, z2r, h10, g01, y1m, z2m = after(y2m, x1r, z3m, z2r, h10, g01, y1m, z2m)
            b11, b02 = joined(y1m, x1r), joined(z2m, z2r)
            y3m, x2r, z3r, c11, c02 = move_y(z3m, 1), move_x(y2m, 1), move_z(z2r, 1), move_c(b11, 1), move_c(b02, 1)
            h01 = weighted(0, 1, expert_values(*g01))
            g11 = gate_values([b11], [c11])
            y3m, x2r, z3r, c02, h01, g11, y2m, z3m = after(y3m, x2r, z3r, c02, h01, g11, y2m, z3m)
            b12, b03 = joined(y2m, x2r), joined(z3m, z3r)
            x3r, c12, c03, c13m = move_x(y3m, 1), move_c(b12, 1), move_c(b03, 1), move_c(y3m, 1)
            h11 = weighted(1, 1, expert_values(*g11))
            x3r, c12, c03, c13m, h11 = after(x3r, c12, c03, c13m, h11)
            c13r = move_c(x3r, 1)
            expert_rows(0, 2, [b02], [c02])
            expert_rows(1, 2, [b12], [c12])
            expert_rows(0, 3, [b03], [c03])
            expert_rows(1, 3, [y3m, x3r], [c13m, c13r])
            for place, h in (((0, 0), h00), ((1, 0), h10), ((0, 1), h01), ((1, 1), h11)):
                blocks[place] = h
        else:
            held = {(0, 0): tokens}
            for d in reversed(steps_of(nz)):
                for jz in sorted((key[1] for key in held), reverse=True):
                    held[0, jz ^ d] = move_z(held[0, jz], d)
            for jz in z_order:
                for jy in range(ny):
                    if jy:
                        held[1, jz] = move_y(held[0, jz], 1)
                    expert_rows(jy, jz, [held[jy, jz]], [move_c(held[jy, jz], 1)])
        hidden = []
        for jc in range(nc):
            parts = []
            for jy in range(ny):
                for jz in z_order:
                    value = blocks[jy, jz][jc * rows:(jc + 1) * rows]
                    parts += in_order(value[:rows // 2], value[rows // 2:]) if (jy, jz) in halved else [value]
            hidden.append(jnp.concatenate(parts, axis=0))

        orders = [[("x", d) for d in steps_of(nx)] + [("y", d) for d in steps_of(ny)],
                  [("y", d) for d in steps_of(ny)] + [("x", d) for d in steps_of(nx)]]
        z_steps = steps_of(nz)
        state = {}

        def product(i, which, jc, far=None):
            if (i, which) not in weights:
                weights[i, which] = chunk_weights(i, which)
            w, h = weights[i, which], hidden[jc]
            if far is not None:
                w, h = (pick(w, "x", far), h) if orders[which][0][0] == "x" else (w, pick(h, "y", far))
            return jnp.dot(h, w, preferred_element_type=jnp.float32)

        def tied(value, *keys):
            if keys:
                value, *got = after(value, *[state[key] for key in keys])
                state.update(zip(keys, got))
            return value

        def begin(i, keys=((), ())):
            if i == 0:
                got = {(which, far): move_c(product(i, which, 1, far).astype(jnp.bfloat16), 1)
                       for far in (1, 0) for which in (0, 1)}
            else:
                got = {}
                for which in (0, 1):
                    whole = move_c(product(i, which, 1).astype(jnp.bfloat16), 1)
                    for far in (1, 0):
                        got[which, far] = pick(whole, orders[which][0][0], far)
            for far in (1, 0):
                for which in (0, 1):
                    value = product(i, which, 0, far) + got[which, far].astype(jnp.float32)
                    state[i, which, far] = value.astype(jnp.bfloat16)
            if i + 1 < len(WIDTHS):
                hidden[0], hidden[1], state[i, 0, 1], state[i, 1, 1] = after(
                    hidden[0], hidden[1], state[i, 0, 1], state[i, 1, 1])
            for which in (0, 1):
                axis, d = orders[which][0]
                state[i, which] = moves[axis](tied(state[i, which, 1], *keys[which]), d)

        def turn(i, step, keys=((), ())):
            for which in (0, 1):
                if step < len(orders[which]):
                    axis, d = orders[which][step]
                    value = (state[i, which, 0], state[i, which])
                    far, state[i, which, 0] = half(value, axis, 1), half(value, axis, 0)
                    state[i, which] = moves[axis](tied(far, *keys[which]), d)

        def turn_z(i, k, *keys):
            if k == 0:
                values = [(state[i, which, 0], state[i, which]) for which in (0, 1)]
                near, far = [jnp.concatenate([half(v, "z", h) for v in values], axis=1) for h in (0, 1)]
            else:
                value = (state[i, "near"], state[i, "z"])
                if k == len(z_steps):
                    return add(*value)
                near, far = [half(value, "z", h) for h in (0, 1)]
            state[i, "near"], state[i, "z"] = near, move_z(tied(far, *keys), z_steps[k])

        if (nx, ny, nz) == (2, 2, 4):
            begin(0)
            turn(0, 1, (((0, 1),), ((0, 0, 0),)))
            begin(1, (((0, 1),), ((0, 0),)))
            turn_z(0, 0)
            turn(1, 1, (((1, 1), (0, "z")), ((1, 0, 0),)))
            turn_z(0, 1)
            begin(2, (((1, 1),), ((1, 0),)))
            turn_z(1, 0)
            turn(2, 1, (((2, 1), (0, "z")), ((2, 0, 0),)))
            turn_z(2, 0, (1, "z"))
            turn_z(1, 1)
            turn_z(2, 1)
        else:
            for i in range(len(WIDTHS)):
                begin(i)
                for step in range(1, len(orders[0])):
                    turn(i, step)
                for k in range(len(z_steps)):
                    turn_z(i, k)
        out = [turn_z(i, len(z_steps)) for i in range(len(WIDTHS))]
        return jnp.concatenate(out, axis=1)

    return shards


def solution(mesh):
    in_specs = (
        P(("groups", "expert"), None),
        P(("groups", "expert"), None),
        P(("groups", "expert"), None),
        P("expert", None, "tensor"),
        P("expert", None, "tensor"),
        P("expert", "tensor", None),
    )
    out_specs = P(("groups", "expert"), "tensor")
    return jax.shard_map(make(mesh), mesh=mesh, in_specs=in_specs, out_specs=out_specs, check_vma=False)
```
